32 devices in a mesh: ctx: 8 (over z, y), tp: 4 (over x, core).
Axes of the slice: x: 2, y: 2, z: 4, core: 2. Of those that a mesh axis runs over, the one named last changes fastest.
Arguments:
- tokens: bfloat16 [64, 5, 16, 2304], P('tp', None, 'ctx'), may hold values from -6 to 6
- doc_ids: int32 [5, 1024], replicated, may hold values from 0 to 3, as said below
- attn_in_gain: bfloat16 [2304], replicated, may hold values from 0.099609375 to 1.8984375
- query_weight: bfloat16 [2304, 2048], P(None, 'tp'), may hold values from -0.125 to 0.125
- key_weight: bfloat16 [2304, 1024], P(None, 'tp'), may hold values from -0.125 to 0.125
- value_weight: bfloat16 [2304, 1024], P(None, 'tp'), may hold values from -0.125 to 0.125
- output_weight: bfloat16 [2048, 2304], P('tp'), may hold values from -0.125 to 0.125
- attn_out_gain: bfloat16 [2304], replicated, may hold values from 0.099609375 to 1.8984375
- ffw_in_gain: bfloat16 [2304], replicated, may hold values from 0.099609375 to 1.8984375
- gate_weight: bfloat16 [2304, 9216], P(None, 'tp'), may hold values from -0.125 to 0.125
- up_weight: bfloat16 [2304, 9216], P(None, 'tp'), may hold values from -0.125 to 0.125
- down_weight: bfloat16 [9216, 2304], P('tp'), may hold values from -0.0625 to 0.0625
- ffw_out_gain: bfloat16 [2304], replicated, may hold values from 0.099609375 to 1.8984375
- cotangent: bfloat16 [64, 5, 16, 2304], P('tp', None, 'ctx'), may hold values from -6 to 6
Outputs:
- layer_out: bfloat16 [64, 5, 16, 2304], P('tp', None, 'ctx')
- tokens_grad: float32 [64, 5, 16, 2304], P('tp', None, 'ctx')
- attn_in_gain_grad: float32 [2304], P('ctx')
- query_weight_grad: float32 [2304, 2048], P('ctx', 'tp')
- key_weight_grad: float32 [2304, 1024], P('ctx', 'tp')
- value_weight_grad: float32 [2304, 1024], P('ctx', 'tp')
- output_weight_grad: float32 [2048, 2304], P('tp', 'ctx')
- attn_out_gain_grad: float32 [2304], P('ctx')
- ffw_in_gain_grad: float32 [2304], P('ctx')
- gate_weight_grad: float32 [2304, 9216], P('ctx', 'tp')
- up_weight_grad: float32 [2304, 9216], P('ctx', 'tp')
- down_weight_grad: float32 [9216, 2304], P('tp', 'ctx')
- ffw_out_gain_grad: float32 [2304], P('ctx')
The draws below stay inside these ranges and needn't reach their ends.
Inputs may be any that keep to these rules, and one draw needn't show every extreme that they name: `doc_ids`: in each sequence the document numbers start at 0 and rise by 0 or 1 from one position to the next. One sequence is a single document; every other sequence holds exactly four documents.
All inputs are finite; a program needn't handle non-finite values.
Results may differ from the reference program's by a relative error of at most 0.025.
Values may be sent and summed in bfloat16 or wider, within the bound.
A program may use at most 256 MiB of HBM per device.

```python
import math
import jax
import jax.numpy as jnp
from jax import lax

D = 2304
H = 8
KV = 4
HD = 256
FF = 9216
SEQS = 5
STRETCH = 64
LENGTH = 1024
N_CTX = 8


def draw_doc_ids(key, part):
    key = jax.random.fold_in(key, 11)
    pick_key, cut_key = jax.random.split(key)
    single = jax.random.randint(pick_key, (), 0, SEQS)
    row_keys = jax.random.split(cut_key, SEQS)
    cut_points = jax.vmap(lambda row_key: jax.random.permutation(row_key, LENGTH - 1)[:3] + 1)(row_keys)
    position = jnp.arange(LENGTH, dtype=jnp.int32)
    packed = jnp.arange(SEQS, dtype=jnp.int32)[:, None] != single
    boundary = jnp.any(position[None, :, None] == cut_points[:, None, :], axis=-1) & packed
    return jnp.cumsum(boundary.astype(jnp.int32), axis=1).astype(jnp.int32)


def block_levels(rng, shape, shards, smallest, high):
    loudness, own = 1.0, jax.random.fold_in(rng, 6)
    for axis_at, parts in shards:
        heights = jnp.exp(jax.random.uniform(jax.random.fold_in(own, axis_at), (parts,), jnp.float32, smallest / len(shards), high / len(shards)))
        loudness = loudness * jnp.repeat(heights, shape[axis_at] // parts).reshape([-1 if axis == axis_at else 1 for axis in range(len(shape))])
    return loudness


def gaussian(own_key, extent, deviation, reach, cuts=(), kind=jnp.bfloat16):
    drawn = deviation * jax.random.normal(own_key, extent, jnp.float32)
    if cuts:
        drawn = drawn * block_levels(own_key, extent, cuts, -0.22, 0.18)
    return jnp.clip(drawn, -reach, reach).astype(kind)


def setup_inputs(seed: int = 0) -> dict:
    splits = jax.random.split(jax.random.key(seed), 15)
    tokens = gaussian(splits[0], (STRETCH, SEQS, 2 * N_CTX, D), 1.0, 6.0, ((0, 4), (2, 8)))
    doc_ids = draw_doc_ids(jax.random.fold_in(splits[14], 71), 0)
    attn_in_gain = jnp.clip(1.0 + 0.18 * jax.random.normal(splits[2], (D,), jnp.float32), 0.099609375, 1.8984375).astype(jnp.bfloat16)
    query_weight = gaussian(splits[3], (D, H * HD), D ** -0.5, 0.125, ((1, 4),))
    key_weight = gaussian(splits[4], (D, KV * HD), D ** -0.5, 0.125, ((1, 4),))
    value_weight = gaussian(splits[5], (D, KV * HD), D ** -0.5, 0.125, ((1, 4),))
    output_weight = gaussian(splits[6], (H * HD, D), (H * HD) ** -0.5, 0.125, ((0, 4),))
    attn_out_gain = jnp.clip(1.0 + 0.18 * jax.random.normal(splits[7], (D,), jnp.float32), 0.099609375, 1.8984375).astype(jnp.bfloat16)
    ffw_in_gain = jnp.clip(1.0 + 0.18 * jax.random.normal(splits[8], (D,), jnp.float32), 0.099609375, 1.8984375).astype(jnp.bfloat16)
    gate_weight = gaussian(splits[9], (D, FF), D ** -0.5, 0.125, ((1, 4),))
    up_weight = gaussian(splits[10], (D, FF), D ** -0.5, 0.125, ((1, 4),))
    down_weight = gaussian(splits[11], (FF, D), FF ** -0.5, 0.0625, ((0, 4),))
    ffw_out_gain = jnp.clip(1.0 + 0.18 * jax.random.normal(splits[12], (D,), jnp.float32), 0.099609375, 1.8984375).astype(jnp.bfloat16)
    cotangent = gaussian(splits[13], (STRETCH, SEQS, 2 * N_CTX, D), 1.0, 6.0, ((0, 4), (2, 8)))
    return dict(tokens=tokens, doc_ids=doc_ids, attn_in_gain=attn_in_gain, query_weight=query_weight, key_weight=key_weight, value_weight=value_weight, output_weight=output_weight, attn_out_gain=attn_out_gain, ffw_in_gain=ffw_in_gain, gate_weight=gate_weight, up_weight=up_weight, down_weight=down_weight, ffw_out_gain=ffw_out_gain, cotangent=cotangent)


EPS = 1e-06
CAP = 50.0
BASE = 10000.0

@jax.custom_vjp
def low(v):
    return lax.optimization_barrier(v.astype(jnp.bfloat16)).astype(jnp.float32)

@jax.custom_vjp
def low_back(v):
    return v

def low_keep(v):
    return (low(v), None)

def low_pass(kept, grad):
    return (grad,)

def back_keep(v):
    return (v, None)

def back_low(kept, grad):
    return (low(grad),)
low.defvjp(low_keep, low_pass)
low_back.defvjp(back_keep, back_low)

def rms_scale(values, gain):
    return values * lax.rsqrt(lax.optimization_barrier(jnp.mean(values * values, axis=-1, keepdims=True)) + EPS) * gain

def rotate(values, positions):
    half_dim = values.shape[-1] // 2
    frequency = BASE ** (-jnp.arange(half_dim).astype(jnp.float32) / half_dim)
    angles = positions.astype(jnp.float32)[..., None, None] * frequency
    cosine = jnp.cos(angles)
    sine_part = jnp.sin(angles)
    lower_half = values[..., :half_dim]
    upper_half = values[..., half_dim:]
    return jnp.concatenate([lower_half * cosine - upper_half * sine_part, upper_half * cosine + lower_half * sine_part], -1)

def seq_starts(doc_ids):
    index = jnp.arange(doc_ids.shape[1], dtype=jnp.int32)
    change = jnp.concatenate([jnp.ones((doc_ids.shape[0], 1), bool), doc_ids[:, 1:] != doc_ids[:, :-1]], 1)
    return lax.cummax(jnp.where(change, index[None, :], jnp.zeros_like(doc_ids)), axis=1)

def undeal(arr):
    reordered = jnp.transpose(arr, (1, 2, 0, 3))
    lower_half = reordered[:, 0::2]
    upper_half = reordered[:, 1::2][:, ::-1]
    return jnp.concatenate([lower_half, upper_half], 1).reshape(SEQS, LENGTH, arr.shape[-1])

def deal_rows(arr):
    split = arr.reshape(SEQS, 2 * N_CTX, STRETCH, arr.shape[-1])
    lower_half = split[:, :N_CTX]
    upper_half = split[:, N_CTX:][:, ::-1]
    stacked = jnp.stack([lower_half, upper_half], 2).reshape(SEQS, 2 * N_CTX, STRETCH, arr.shape[-1])
    return jnp.transpose(stacked, (2, 0, 1, 3))

def product(left, right):
    return jnp.einsum('...d,df->...f', left, right, precision=lax.Precision.HIGHEST)

def attend(query_seq, key_seq, value_seq, start_seq):
    block_len = math.gcd(LENGTH, 512)
    group_size = H // KV
    score_scale = HD ** (-0.5)
    key_index = jnp.arange(LENGTH, dtype=jnp.int32)

    def query_block(args):
        query_rows, token_rows, start_rows = args
        grouped = query_rows.reshape(block_len, KV, group_size, HD)
        raw_scores = low_back(jnp.einsum('qkgd,tkd->kgqt', grouped, key_seq, precision=lax.Precision.HIGHEST))
        capped = CAP * jnp.tanh(raw_scores * (score_scale / CAP))
        allowed = (key_index[None, :] <= token_rows[:, None]) & (key_index[None, :] >= start_rows[:, None])
        weights_exp = jnp.where(allowed, jnp.exp(capped), jnp.zeros_like(capped))
        weight_total = lax.optimization_barrier(jnp.sum(weights_exp, axis=-1))
        unnormed = low_back(jnp.einsum('kgqt,tkd->kgqd', low(weights_exp), value_seq, precision=lax.Precision.HIGHEST))
        normalized = unnormed / weight_total[..., None]
        return jnp.transpose(normalized, (2, 0, 1, 3)).reshape(block_len, H * HD)
    blocks = lax.map(jax.checkpoint(query_block), (query_seq.reshape(LENGTH // block_len, block_len, H, HD), key_index.reshape(-1, block_len), start_seq.reshape(-1, block_len)))
    return blocks.reshape(LENGTH, H * HD)

def layer_forward(inputs, attn_in_gain, query_weight, key_weight, value_weight, output_weight, attn_out_gain, ffw_in_gain, gate_weight, up_weight, down_weight, ffw_out_gain, positions, starts):
    normed = low(rms_scale(inputs, attn_in_gain))
    queries = low(rotate(low_back(product(normed, query_weight)).reshape(SEQS, LENGTH, H, HD), positions))
    keys = low(rotate(low_back(product(normed, key_weight)).reshape(SEQS, LENGTH, KV, HD), positions))
    values = low(low_back(product(normed, value_weight))).reshape(SEQS, LENGTH, KV, HD)
    attended = lax.map(lambda args: attend(*args), (queries, keys, values, starts))
    attn_branch = low_back(product(low(attended), output_weight))
    resid = inputs + rms_scale(attn_branch, attn_out_gain)
    ffw_in = low(rms_scale(resid, ffw_in_gain))
    gate = low_back(product(ffw_in, gate_weight))
    up_val = low_back(product(ffw_in, up_weight))
    mixed_act = low(jax.nn.gelu(gate, approximate=True) * up_val)
    ffw_branch = low_back(product(mixed_act, down_weight))
    return resid + rms_scale(ffw_branch, ffw_out_gain)

def reference(tokens, doc_ids, attn_in_gain, query_weight, key_weight, value_weight, output_weight, attn_out_gain, ffw_in_gain, gate_weight, up_weight, down_weight, ffw_out_gain, cotangent):
    starts = seq_starts(doc_ids)
    positions = jnp.arange(LENGTH, dtype=jnp.int32)[None, :] - starts
    params = [attn_in_gain, query_weight, key_weight, value_weight, output_weight, attn_out_gain, ffw_in_gain, gate_weight, up_weight, down_weight, ffw_out_gain]
    params = [param.astype(jnp.float32) for param in params]
    inputs = undeal(tokens.astype(jnp.float32))

    def wrapped(*values):
        return layer_forward(*values, positions, starts)
    result, pullback = jax.vjp(wrapped, inputs, *params)
    grads = pullback(undeal(cotangent.astype(jnp.float32)))
    return (deal_rows(result).astype(jnp.bfloat16), deal_rows(grads[0]), grads[1], grads[2], grads[3], grads[4], grads[5], grads[6], grads[7], grads[8], grads[9], grads[10], grads[11])
```

```python
import functools

import jax
import jax.numpy as jnp
from jax import lax
from jax.experimental import pallas as pl
from jax.experimental.pallas import tpu as pltpu
from jax.sharding import PartitionSpec as P

HD = 256
EPS = 1e-06
CAP = 50.0
BASE = 10000.0
MIB = 1 << 20
F32 = jnp.float32
BF16 = jnp.bfloat16
VMEM = pltpu.VMEM
MESH = pl.DeviceIdType.MESH


def bits_of(mask):
    return [b for b in range(mask.bit_length()) if mask >> b & 1]


def flipped(index, mask):
    for b in bits_of(mask):
        index = index + (1 - 2 * ((index // (1 << b)) % 2)) * (1 << b)
    return index


def without(mask, bit):
    return (mask >> bit + 1 << bit) | (mask & (1 << bit) - 1)


def submasks(bits):
    masks = [0]
    for b in bits:
        masks = masks + [m | 1 << b for m in masks]
    return masks


def greet(axis, count):
    me = lax.axis_index(axis)
    barrier = pltpu.get_barrier_semaphore()
    steps = count.bit_length() - 1
    for b in range(steps):
        pl.semaphore_signal(
            barrier, inc=1, device_id={axis: flipped(me, 1 << b)}, device_id_type=MESH
        )
    pl.semaphore_wait(barrier, steps)


def remote(axis, src, dst, sems, at, partner):
    return pltpu.make_async_remote_copy(
        src_ref=src,
        dst_ref=dst,
        send_sem=sems[0].at[at],
        recv_sem=sems[1].at[at],
        device_id={axis: partner},
        device_id_type=MESH,
    )


def tp_kernel(fn, count, items, n_in, n_out, scatter, gather, *refs):
    refs = list(refs)
    part = refs.pop(0) if scatter else None
    ins = [refs.pop(0) for _ in range(n_in)]
    whole = refs.pop(0) if gather else None
    outs = [refs.pop(0) for _ in range(n_out)]
    if scatter:
        landed, sendbuf = refs.pop(0), refs.pop(0)
        rs_sems = (refs.pop(0), refs.pop(0))
    if gather:
        ag_sems = (refs.pop(0), refs.pop(0))
    me = lax.axis_index("tp")
    steps = count.bit_length() - 1
    order = list(range(steps))
    greet("tp", count)

    def rs_copy(item, step, sub):
        bit = 1 << order[step]
        mask = bit | sub
        src = part.at[item, :, flipped(me, mask)] if step == 0 else sendbuf.at[item, mask]
        return remote("tp", src, landed.at[item, mask], rs_sems, (item, mask), flipped(me, bit))

    def rs_sum(item, mask, upto):
        total = part[item, :, flipped(me, mask)].astype(F32)
        for step in range(upto):
            total = total + landed[item, 1 << order[step] | mask].astype(F32)
        return total

    def rs_subs(step):
        return submasks(order[step + 1 :])

    def ag_copy(item, step, mask):
        bit = 1 << order[steps - 1 - step]
        block = whole.at[item, :, flipped(me, mask)]
        return remote("tp", block, block, ag_sems, (item, mask | bit), flipped(me, bit))

    def ag_masks(step):
        return submasks([order[steps - 1 - s] for s in range(step)])

    if scatter:
        for item in range(items):
            for sub in rs_subs(0):
                rs_copy(item, 0, sub).start()
        for step in range(1, steps):
            for item in range(items):
                for sub in rs_subs(step - 1):
                    rs_copy(item, step - 1, sub).wait_recv()
                for sub in rs_subs(step):
                    mask = 1 << order[step] | sub
                    sendbuf[item, mask] = rs_sum(item, mask, step).astype(BF16)
                    rs_copy(item, step, sub).start()
    for item in range(items):
        total = None
        if scatter:
            for sub in rs_subs(steps - 1):
                rs_copy(item, steps - 1, sub).wait_recv()
            total = rs_sum(item, 0, steps)
        sent = fn(item, total, ins, outs)
        if gather:
            whole[item, :, me] = sent.astype(BF16)
            for step in range(steps):
                ag_copy(item, step, 0).start()
    if gather:
        for got in range(steps):
            for item in range(items):
                for mask in ag_masks(got):
                    ag_copy(item, got, mask).wait_recv()
                    for step in range(got + 1, steps):
                        ag_copy(item, step, mask | 1 << order[steps - 1 - got]).start()
        for step in range(steps):
            for item in range(items):
                for mask in ag_masks(step):
                    ag_copy(item, step, mask).wait_send()
    if scatter:
        for step in range(steps):
            for item in range(items):
                for sub in rs_subs(step):
                    rs_copy(item, step, sub).wait_send()


def tp_exchange(name, cid, fn, ins, outs, part=None, gather=True):
    count = lax.axis_size("tp")
    rows_shape = ins[0].shape
    items, slots, rows, width = rows_shape
    scatter = part is not None
    out_shape = list(outs)
    if gather:
        out_shape = [jax.ShapeDtypeStruct((items, slots, count, rows, width), BF16)] + out_shape
    scratch = []
    dma = pltpu.SemaphoreType.DMA((items, count))
    if scatter:
        scratch += [VMEM((items, count, slots, rows, width), BF16)] * 2 + [dma, dma]
    if gather:
        scratch += [dma, dma]
    args = ([part] if scatter else []) + list(ins)
    return pl.pallas_call(
        functools.partial(
            tp_kernel, fn, count, items, len(ins), len(outs), scatter, gather
        ),
        out_shape=out_shape,
        in_specs=[pl.BlockSpec(memory_space=VMEM)] * len(args),
        out_specs=[pl.BlockSpec(memory_space=VMEM)] * len(out_shape),
        scratch_shapes=scratch,
        compiler_params=pltpu.CompilerParams(
            collective_id=cid, has_side_effects=True, vmem_limit_bytes=40 * MIB
        ),
        name=name,
    )(*args)


def ctx_orders(items, steps):
    usual = list(range(steps))[::-1]
    if steps < 2:
        return [usual] * items
    other = usual[:-2] + [usual[-1], usual[-2]]
    return [other if i % 4 == 3 else usual for i in range(items)]


def ctx_gather_kernel(count, items, block, whole, send_sem, recv_sem, local_sem):
    me = lax.axis_index("ctx")
    steps = count.bit_length() - 1
    orders = ctx_orders(items, steps)
    own = pltpu.make_async_copy(block, whole.at[:, me], local_sem)
    own.start()
    greet("ctx", count)

    def copy(item, step, mask):
        bit = 1 << orders[item][step]
        dst = whole.at[item, flipped(me, mask)]
        src = block.at[item] if mask == 0 else dst
        return remote(
            "ctx", src, dst, (send_sem, recv_sem), (item, mask | bit), flipped(me, bit)
        )

    def masks(item, step):
        return submasks(orders[item][:step])

    for step in range(steps):
        for item in range(items):
            copy(item, step, 0).start()
    for got in range(steps):
        for item in range(items):
            for mask in masks(item, got):
                copy(item, got, mask).wait_recv()
                for step in range(got + 1, steps):
                    copy(item, step, mask | 1 << orders[item][got]).start()
    for step in range(steps):
        for item in range(items):
            for mask in masks(item, step):
                copy(item, step, mask).wait_send()
    own.wait()


def ctx_gather(block, cid):
    count = lax.axis_size("ctx")
    items, rows, cols = block.shape
    dma = pltpu.SemaphoreType.DMA((items, count))
    return pl.pallas_call(
        functools.partial(ctx_gather_kernel, count, items),
        out_shape=jax.ShapeDtypeStruct((items, count, rows, cols), block.dtype),
        in_specs=[pl.BlockSpec(memory_space=VMEM)],
        out_specs=pl.BlockSpec(memory_space=VMEM),
        scratch_shapes=[dma, dma, pltpu.SemaphoreType.DMA],
        compiler_params=pltpu.CompilerParams(
            collective_id=cid, has_side_effects=True, vmem_limit_bytes=56 * MIB
        ),
        name="ctx_gather",
    )(block)


def ctx_scatter_kernel(count, items, part, out, landed, sendbuf, send_sem, recv_sem):
    me = lax.axis_index("ctx")
    steps = count.bit_length() - 1
    orders = [order[::-1] for order in ctx_orders(items, steps)]
    greet("ctx", count)

    def copy(item, step, sub):
        bit = 1 << orders[item][step]
        mask = bit | sub
        first = orders[item][0]
        src = part.at[item, flipped(me, mask)] if step == 0 else sendbuf.at[item, without(mask, first)]
        return remote(
            "ctx", src, landed.at[item, mask], (send_sem, recv_sem), (item, mask), flipped(me, bit)
        )

    def total_of(item, mask, upto):
        total = part[item, flipped(me, mask)].astype(F32)
        for step in range(upto):
            total = total + landed[item, 1 << orders[item][step] | mask].astype(F32)
        return total

    def subs(item, step):
        return submasks(orders[item][step + 1 :])

    for item in range(items):
        for sub in subs(item, 0):
            copy(item, 0, sub).start()
    for step in range(1, steps):
        for item in range(items):
            for sub in subs(item, step - 1):
                copy(item, step - 1, sub).wait_recv()
            for sub in subs(item, step):
                mask = 1 << orders[item][step] | sub
                slot = without(mask, orders[item][0])
                sendbuf[item, slot] = total_of(item, mask, step).astype(BF16)
                copy(item, step, sub).start()
    for item in range(items):
        for sub in subs(item, steps - 1):
            copy(item, steps - 1, sub).wait_recv()
        out[item] = total_of(item, 0, steps)
    for step in range(steps):
        for item in range(items):
            for sub in subs(item, step):
                copy(item, step, sub).wait_send()


def ctx_scatter(part, cid):
    count = lax.axis_size("ctx")
    items, _, rows, cols = part.shape
    dma = pltpu.SemaphoreType.DMA((items, count))
    return pl.pallas_call(
        functools.partial(ctx_scatter_kernel, count, items),
        out_shape=jax.ShapeDtypeStruct((items, rows, cols), F32),
        in_specs=[pl.BlockSpec(memory_space=VMEM)],
        out_specs=pl.BlockSpec(memory_space=VMEM),
        scratch_shapes=[
            VMEM(part.shape, BF16),
            VMEM((items, count // 2, rows, cols), BF16),
            dma,
            dma,
        ],
        compiler_params=pltpu.CompilerParams(
            collective_id=cid, has_side_effects=True, vmem_limit_bytes=56 * MIB
        ),
        name="ctx_scatter",
    )(part)


def halve(part, order):
    count = lax.axis_size("ctx")
    steps = count.bit_length() - 1
    me = lax.axis_index("ctx")
    left = list(range(steps))[::-1]
    total = part.reshape((2,) * steps + (part.shape[0] // count, part.shape[1]))
    for at, b in enumerate(order):
        axis = left.index(b)
        left.remove(b)
        mine = (me >> b) & 1
        give = lax.dynamic_index_in_dim(total, 1 - mine, axis, keepdims=False)
        keep = lax.dynamic_index_in_dim(total, mine, axis, keepdims=False)
        got = lax.ppermute(give, "ctx", [(i, i ^ (1 << b)) for i in range(count)])
        total = keep.astype(F32) + got.astype(F32)
        if at < steps - 1:
            total = total.astype(BF16)
    return total


def inv_rms(v):
    return lax.rsqrt(jnp.mean(v * v, axis=-1, keepdims=True) + EPS)


def rms_back(dy, v, g):
    r = inv_rms(v)
    dg = jnp.sum(dy * v * r, axis=tuple(range(v.ndim - 1)), keepdims=True)
    gdy = g * dy
    dv = r * gdy - v * (r * r * r) * jnp.mean(gdy * v, axis=-1, keepdims=True)
    return dv, dg.reshape(1, -1)


def add_to(ref, item, value):
    ref[...] = value if item == 0 else ref[...] + value


def enter_rows(item, _, ins, outs):
    tokens, gain = ins
    v = tokens[item].astype(F32)
    return v * inv_rms(v) * gain[...].astype(F32)


def mid_rows(item, branch, ins, outs):
    tokens, attn_gain, ffw_gain = ins
    branch_out, resid_out = outs
    branch_out[item] = branch
    resid = tokens[item].astype(F32) + branch * inv_rms(branch) * attn_gain[...].astype(F32)
    resid_out[item] = resid
    return resid * inv_rms(resid) * ffw_gain[...].astype(F32)


def turn_rows(item, branch, ins, outs):
    resid, cotangent, gain = ins
    layer_out, gain_grad = outs
    g = gain[...].astype(F32)
    layer_out[item] = (resid[item] + branch * inv_rms(branch) * g).astype(BF16)
    dv, dg = rms_back(cotangent[item].astype(F32), branch, g)
    add_to(gain_grad, item, dg)
    return dv


def mid_back_rows(item, ffw_grad, ins, outs):
    resid, branch, cotangent, ffw_gain, attn_gain = ins
    resid_grad_out, ffw_gain_grad, attn_gain_grad = outs
    dv, dg = rms_back(ffw_grad, resid[item], ffw_gain[...].astype(F32))
    add_to(ffw_gain_grad, item, dg)
    resid_grad = cotangent[item].astype(F32) + dv
    resid_grad_out[item] = resid_grad
    dv, dg = rms_back(resid_grad, branch[item], attn_gain[...].astype(F32))
    add_to(attn_gain_grad, item, dg)
    return dv


def leave_rows(item, normed_grad, ins, outs):
    tokens, resid_grad, gain = ins
    tokens_grad, gain_grad = outs
    dv, dg = rms_back(normed_grad, tokens[item].astype(F32), gain[...].astype(F32))
    add_to(gain_grad, item, dg)
    tokens_grad[item] = resid_grad[item] + dv


def rotate(values, cosine, sine):
    half_dim = values.shape[-1] // 2
    low, high = values[..., :half_dim], values[..., half_dim:]
    return jnp.concatenate([low * cosine - high * sine, high * cosine + low * sine], -1)


def gelu_times(gate, up_val):
    return jax.nn.gelu(gate, approximate=True) * up_val


def body(
    tokens,
    doc_ids,
    attn_in_gain,
    query_weight,
    key_weight,
    value_weight,
    output_weight,
    attn_out_gain,
    ffw_in_gain,
    gate_weight,
    up_weight,
    down_weight,
    ffw_out_gain,
    cotangent,
):
    stretch_rows, seqs, slots, width = tokens.shape
    ctx_count = lax.axis_size("ctx")
    tp_count = lax.axis_size("tp")
    ctx_rank = lax.axis_index("ctx")
    stretch = stretch_rows * tp_count
    length = 2 * stretch * ctx_count
    rows = stretch * slots
    all_rows = seqs * rows
    local_heads = query_weight.shape[1] // HD
    local_kv = key_weight.shape[1] // HD
    group = local_heads // local_kv
    scale = HD ** (-0.5)
    own = (seqs, slots, stretch_rows, width)
    steps = ctx_count.bit_length() - 1
    usual = list(range(steps))
    other = usual if steps < 2 else [1, 0] + usual[2:]

    slot_stretch = jnp.stack([ctx_rank, 2 * ctx_count - 1 - ctx_rank])
    iota = jnp.arange(stretch, dtype=jnp.int32)
    query_tok = slot_stretch[:, None] * stretch + iota[None, :]
    row_tok = query_tok.reshape(rows)
    row_doc = jnp.concatenate(
        [lax.dynamic_slice_in_dim(doc_ids, slot_stretch[i] * stretch, stretch, 1) for i in (0, 1)],
        1,
    )
    row_start = jnp.sum(
        (doc_ids[:, None, :] < row_doc[:, :, None]).astype(jnp.int32), axis=-1
    )
    row_pos = row_tok[None] - row_start
    frequency = BASE ** (-jnp.arange(HD // 2).astype(F32) / (HD // 2))
    angles = row_pos.astype(F32)[..., None] * frequency
    cosine = jnp.cos(angles)[:, :, None, :]
    sine = jnp.sin(angles)[:, :, None, :]
    key_slot = jnp.arange(2 * ctx_count, dtype=jnp.int32)
    key_stretch = jnp.where(key_slot % 2 == 0, key_slot // 2, 2 * ctx_count - 1 - key_slot // 2)
    key_tok = (key_stretch[:, None] * stretch + iota[None, :]).reshape(length)
    allowed = (key_tok[None, None, :] <= row_tok[None, :, None]) & (
        key_tok[None, None, :] >= row_start[:, :, None]
    )

    def wide(gain):
        return gain.reshape(1, width)

    mine = jnp.transpose(tokens, (1, 2, 0, 3))
    upstream = jnp.transpose(cotangent, (1, 2, 0, 3))
    f32_rows = jax.ShapeDtypeStruct(own, F32)
    gain_shape = jax.ShapeDtypeStruct((1, width), F32)

    (normed_all,) = tp_exchange("enter", 1, enter_rows, [mine, wide(attn_in_gain)], [])
    normed_all = normed_all.reshape(all_rows, width)
    dot = functools.partial(jnp.dot, preferred_element_type=F32)
    ein = functools.partial(jnp.einsum, preferred_element_type=F32)
    keys = rotate(
        dot(normed_all, key_weight).reshape(seqs, rows, local_kv, HD), cosine, sine
    ).astype(BF16)
    values = dot(normed_all, value_weight).astype(BF16)
    queries = rotate(
        dot(normed_all, query_weight).reshape(seqs, rows, local_heads, HD), cosine, sine
    ).astype(BF16)
    kv = jnp.concatenate(
        [keys.reshape(seqs, rows, local_kv * HD), values.reshape(seqs, rows, local_kv * HD)], 0
    )
    kv_all = ctx_gather(kv, 2).reshape(2, seqs, length, local_kv, HD)
    keys_all, values_all = kv_all[0], kv_all[1]
    grouped = queries.reshape(seqs, rows, local_kv, group, HD)

    raw = ein("srkgd,sukd->skgru", grouped, keys_all)
    tanh = jnp.tanh(raw * (scale / CAP))
    exps = jnp.where(allowed[:, None, None], jnp.exp(CAP * tanh), 0.0)
    total = jnp.sum(exps, axis=-1)
    exps_low = exps.astype(BF16)
    attn = ein("skgru,sukd->srkgd", exps_low, values_all)
    total_rows = jnp.transpose(total, (0, 3, 1, 2))[..., None]
    attn = attn / total_rows
    attn_rows = attn.astype(BF16).reshape(all_rows, local_heads * HD)
    part = dot(attn_rows, output_weight).astype(BF16)

    def by_owner(value):
        return value.reshape(seqs, slots, tp_count, stretch_rows, width)

    ffw_all, branch, resid = tp_exchange(
        "middle",
        3,
        mid_rows,
        [mine, wide(attn_out_gain), wide(ffw_in_gain)],
        [f32_rows, f32_rows],
        by_owner(part),
    )
    ffw_all = ffw_all.reshape(all_rows, width)
    gate = dot(ffw_all, gate_weight)
    up = dot(ffw_all, up_weight)
    mixed, mixed_back = jax.vjp(gelu_times, gate, up)
    mixed = mixed.astype(BF16)
    part = dot(mixed, down_weight).astype(BF16)
    ffw_grad_all, layer_out, ffw_out_gain_part = tp_exchange(
        "turn",
        4,
        turn_rows,
        [resid, upstream, wide(ffw_out_gain)],
        [jax.ShapeDtypeStruct(own, BF16), gain_shape],
        by_owner(part),
    )
    ffw_grad_all = ffw_grad_all.reshape(all_rows, width)
    down_part = ein("rd,rf->df", ffw_grad_all, mixed).astype(BF16)
    down_sum = halve(down_part, usual)
    mixed_grad = ein("rd,fd->rf", ffw_grad_all, down_weight)
    gate_grad, up_grad = mixed_back(mixed_grad)
    gate_grad = gate_grad.astype(BF16)
    up_grad = up_grad.astype(BF16)
    gate_part = ein("rd,rf->df", ffw_all, gate_grad).astype(BF16)
    gate_sum = halve(gate_part, usual)
    up_part = ein("rd,rf->df", ffw_all, up_grad).astype(BF16)
    cut = up_part.shape[1] // 2
    up_sum = jnp.concatenate(
        [halve(up_part[:, :cut], other), halve(up_part[:, cut:], usual)], 1
    )
    part = (
        ein("rf,df->rd", gate_grad, gate_weight) + ein("rf,df->rd", up_grad, up_weight)
    ).astype(BF16)
    branch_grad_all, resid_grad, ffw_in_gain_part, attn_out_gain_part = tp_exchange(
        "middle_back",
        5,
        mid_back_rows,
        [resid, branch, upstream, wide(ffw_in_gain), wide(attn_out_gain)],
        [f32_rows, gain_shape, gain_shape],
        by_owner(part),
    )
    branch_grad_all = branch_grad_all.reshape(all_rows, width)
    output_part = ein("rd,rh->dh", branch_grad_all, attn_rows).astype(BF16)
    output_sum = halve(output_part, other)
    attn_grad = ein("rd,hd->rh", branch_grad_all, output_weight).reshape(attn.shape)
    row_dot = jnp.sum(attn_grad * attn, axis=-1)
    scaled = (attn_grad / total_rows).astype(BF16)
    shift = jnp.transpose(row_dot, (0, 2, 3, 1)) / total
    weight_grad = ein("srkgd,sukd->skgru", scaled, values_all)
    score_grad = (
        exps * (weight_grad - shift[..., None]) * (scale * (1.0 - tanh * tanh))
    ).astype(BF16)
    query_acc = ein("skgru,sukd->srkgd", score_grad, keys_all)
    key_acc = ein("skgru,srkgd->sukd", score_grad, grouped)
    value_acc = ein("skgru,srkgd->sukd", exps_low, scaled)
    kv_acc = jnp.concatenate([key_acc, value_acc], 0).astype(BF16)
    kv_sum = ctx_scatter(kv_acc.reshape(2 * seqs, ctx_count, rows, local_kv * HD), 6)
    key_grad = rotate(kv_sum[:seqs].reshape(seqs, rows, local_kv, HD), cosine, -sine)
    key_grad = key_grad.astype(BF16).reshape(all_rows, local_kv * HD)
    value_grad = kv_sum[seqs:].astype(BF16).reshape(all_rows, local_kv * HD)
    query_grad = rotate(query_acc.reshape(seqs, rows, local_heads, HD), cosine, -sine)
    query_grad = query_grad.astype(BF16).reshape(all_rows, local_heads * HD)
    qkv_grad = jnp.concatenate([query_grad, key_grad, value_grad], 1)
    qkv_weight = jnp.concatenate([query_weight, key_weight, value_weight], 1)
    part = ein("rh,dh->rd", qkv_grad, qkv_weight).astype(BF16)
    qkv_part = ein("rd,rh->dh", normed_all, qkv_grad).astype(BF16)
    qkv_sum = halve(qkv_part, usual)
    tokens_grad, attn_in_gain_part = tp_exchange(
        "leave",
        7,
        leave_rows,
        [mine, resid_grad, wide(attn_in_gain)],
        [f32_rows, gain_shape],
        by_owner(part),
        gather=False,
    )
    gains = jnp.concatenate(
        [attn_in_gain_part, attn_out_gain_part, ffw_in_gain_part, ffw_out_gain_part], 0
    )
    gains = lax.psum(gains, ("ctx", "tp"))
    share = width // ctx_count
    gains = lax.dynamic_slice_in_dim(gains, ctx_rank * share, share, 1)
    heads_end = local_heads * HD
    keys_end = heads_end + local_kv * HD
    return (
        jnp.transpose(layer_out, (2, 0, 1, 3)),
        jnp.transpose(tokens_grad, (2, 0, 1, 3)),
        gains[0],
        qkv_sum[:, :heads_end],
        qkv_sum[:, heads_end:keys_end],
        qkv_sum[:, keys_end:],
        output_sum.T,
        gains[1],
        gains[2],
        gate_sum,
        up_sum,
        down_sum.T,
        gains[3],
    )


def solution(mesh):
    placed = (
        P("tp", None, "ctx", None),
        P(),
        P(),
        P(None, "tp"),
        P(None, "tp"),
        P(None, "tp"),
        P("tp", None),
        P(),
        P(),
        P(None, "tp"),
        P(None, "tp"),
        P("tp", None),
        P(),
        P("tp", None, "ctx", None),
    )
    return jax.shard_map(
        body,
        mesh=mesh,
        in_specs=placed,
        out_specs=(
            P("tp", None, "ctx", None),
            P("tp", None, "ctx", None),
            P("ctx"),
            P("ctx", "tp"),
            P("ctx", "tp"),
            P("ctx", "tp"),
            P("tp", "ctx"),
            P("ctx"),
            P("ctx"),
            P("ctx", "tp"),
            P("ctx", "tp"),
            P("tp", "ctx"),
            P("ctx"),
        ),
        check_vma=False,
    )
```

```python
import functools

import jax
import jax.numpy as jnp
from jax import lax
from jax.experimental import pallas as pl
from jax.experimental.pallas import tpu as pltpu
from jax.sharding import PartitionSpec as P

HD = 256
EPS = 1e-06
CAP = 50.0
BASE = 10000.0
MIB = 1 << 20
F32 = jnp.float32
BF16 = jnp.bfloat16
VMEM = pltpu.VMEM
MESH = pl.DeviceIdType.MESH


def bits_of(mask):
    return [b for b in range(mask.bit_length()) if mask >> b & 1]


def flipped(index, mask):
    for b in bits_of(mask):
        index = index + (1 - 2 * ((index // (1 << b)) % 2)) * (1 << b)
    return index


def without(mask, bit):
    return (mask >> bit + 1 << bit) | (mask & (1 << bit) - 1)


def submasks(bits):
    masks = [0]
    for b in bits:
        masks = masks + [m | 1 << b for m in masks]
    return masks


def greet(axis, count):
    me = lax.axis_index(axis)
    barrier = pltpu.get_barrier_semaphore()
    steps = count.bit_length() - 1
    for b in range(steps):
        pl.semaphore_signal(
            barrier, inc=1, device_id={axis: flipped(me, 1 << b)}, device_id_type=MESH
        )
    pl.semaphore_wait(barrier, steps)


def remote(axis, src, dst, sems, at, partner):
    return pltpu.make_async_remote_copy(
        src_ref=src,
        dst_ref=dst,
        send_sem=sems[0].at[at],
        recv_sem=sems[1].at[at],
        device_id={axis: partner},
        device_id_type=MESH,
    )


def tp_kernel(fn, count, items, n_in, n_out, scatter, gather, *refs):
    refs = list(refs)
    part = refs.pop(0) if scatter else None
    ins = [refs.pop(0) for _ in range(n_in)]
    whole = refs.pop(0) if gather else None
    outs = [refs.pop(0) for _ in range(n_out)]
    if scatter:
        landed, sendbuf = refs.pop(0), refs.pop(0)
        rs_sems = (refs.pop(0), refs.pop(0))
    if gather:
        ag_sems = (refs.pop(0), refs.pop(0))
    me = lax.axis_index("tp")
    steps = count.bit_length() - 1
    order = list(range(steps))
    greet("tp", count)

    def rs_copy(item, step, sub):
        bit = 1 << order[step]
        mask = bit | sub
        src = part.at[item, :, flipped(me, mask)] if step == 0 else sendbuf.at[item, mask]
        return remote("tp", src, landed.at[item, mask], rs_sems, (item, mask), flipped(me, bit))

    def rs_sum(item, mask, upto):
        total = part[item, :, flipped(me, mask)].astype(F32)
        for step in range(upto):
            total = total + landed[item, 1 << order[step] | mask].astype(F32)
        return total

    def rs_subs(step):
        return submasks(order[step + 1 :])

    def ag_copy(item, step, mask):
        bit = 1 << order[steps - 1 - step]
        block = whole.at[item, :, flipped(me, mask)]
        return remote("tp", block, block, ag_sems, (item, mask | bit), flipped(me, bit))

    def ag_masks(step):
        return submasks([order[steps - 1 - s] for s in range(step)])

    if scatter:
        for item in range(items):
            for sub in rs_subs(0):
                rs_copy(item, 0, sub).start()
        for step in range(1, steps):
            for item in range(items):
                for sub in rs_subs(step - 1):
                    rs_copy(item, step - 1, sub).wait_recv()
                for sub in rs_subs(step):
                    mask = 1 << order[step] | sub
                    sendbuf[item, mask] = rs_sum(item, mask, step).astype(BF16)
                    rs_copy(item, step, sub).start()
    for item in range(items):
        total = None
        if scatter:
            for sub in rs_subs(steps - 1):
                rs_copy(item, steps - 1, sub).wait_recv()
            total = rs_sum(item, 0, steps)
        sent = fn(item, total, ins, outs)
        if gather:
            whole[item, :, me] = sent.astype(BF16)
            for step in range(steps):
                ag_copy(item, step, 0).start()
    if gather:
        for got in range(steps):
            for item in range(items):
                for mask in ag_masks(got):
                    ag_copy(item, got, mask).wait_recv()
                    for step in range(got + 1, steps):
                        ag_copy(item, step, mask | 1 << order[steps - 1 - got]).start()
        for step in range(steps):
            for item in range(items):
                for mask in ag_masks(step):
                    ag_copy(item, step, mask).wait_send()
    if scatter:
        for step in range(steps):
            for item in range(items):
                for sub in rs_subs(step):
                    rs_copy(item, step, sub).wait_send()


def takes(us):
    return pl.CostEstimate(flops=int(us * 1.1e9), bytes_accessed=0, transcendentals=0)


def tp_exchange(name, cid, fn, ins, outs, part=None, gather=True):
    count = lax.axis_size("tp")
    rows_shape = ins[0].shape
    items, slots, rows, width = rows_shape
    scatter = part is not None
    out_shape = list(outs)
    if gather:
        out_shape = [jax.ShapeDtypeStruct((items, slots, count, rows, width), BF16)] + out_shape
    scratch = []
    dma = pltpu.SemaphoreType.DMA((items, count))
    if scatter:
        scratch += [VMEM((items, count, slots, rows, width), BF16)] * 2 + [dma, dma]
    if gather:
        scratch += [dma, dma]
    args = ([part] if scatter else []) + list(ins)
    return pl.pallas_call(
        functools.partial(
            tp_kernel, fn, count, items, len(ins), len(outs), scatter, gather
        ),
        out_shape=out_shape,
        in_specs=[pl.BlockSpec(memory_space=VMEM)] * len(args),
        out_specs=[pl.BlockSpec(memory_space=VMEM)] * len(out_shape),
        scratch_shapes=scratch,
        compiler_params=pltpu.CompilerParams(
            collective_id=cid, has_side_effects=True, vmem_limit_bytes=40 * MIB
        ),
        cost_estimate=takes(18 * (scatter + gather)),
        name=name,
    )(*args)


def ctx_orders(items, steps):
    usual = list(range(steps))[::-1]
    if steps < 2:
        return [usual] * items
    other = usual[:-2] + [usual[-1], usual[-2]]
    return [other if i % 4 == 3 else usual for i in range(items)]


def ctx_gather_kernel(count, items, block, whole, send_sem, recv_sem, local_sem):
    me = lax.axis_index("ctx")
    steps = count.bit_length() - 1
    orders = ctx_orders(items, steps)
    own = pltpu.make_async_copy(block, whole.at[:, me], local_sem)
    own.start()
    greet("ctx", count)

    def copy(item, step, mask):
        bit = 1 << orders[item][step]
        dst = whole.at[item, flipped(me, mask)]
        src = block.at[item] if mask == 0 else dst
        return remote(
            "ctx", src, dst, (send_sem, recv_sem), (item, mask | bit), flipped(me, bit)
        )

    def masks(item, step):
        return submasks(orders[item][:step])

    for step in range(steps):
        for item in range(items):
            copy(item, step, 0).start()
    for got in range(steps):
        for item in range(items):
            for mask in masks(item, got):
                copy(item, got, mask).wait_recv()
                for step in range(got + 1, steps):
                    copy(item, step, mask | 1 << orders[item][got]).start()
    for step in range(steps):
        for item in range(items):
            for mask in masks(item, step):
                copy(item, step, mask).wait_send()
    own.wait()


def ctx_gather(block, cid):
    count = lax.axis_size("ctx")
    items, rows, cols = block.shape
    dma = pltpu.SemaphoreType.DMA((items, count))
    return pl.pallas_call(
        functools.partial(ctx_gather_kernel, count, items),
        out_shape=jax.ShapeDtypeStruct((items, count, rows, cols), block.dtype),
        in_specs=[pl.BlockSpec(memory_space=VMEM)],
        out_specs=pl.BlockSpec(memory_space=VMEM),
        scratch_shapes=[dma, dma, pltpu.SemaphoreType.DMA],
        compiler_params=pltpu.CompilerParams(
            collective_id=cid, has_side_effects=True, vmem_limit_bytes=56 * MIB
        ),
        cost_estimate=takes(55),
        name="ctx_gather",
    )(block)


def ctx_scatter_kernel(count, items, part, out, landed, sendbuf, send_sem, recv_sem):
    me = lax.axis_index("ctx")
    steps = count.bit_length() - 1
    orders = [order[::-1] for order in ctx_orders(items, steps)]
    greet("ctx", count)

    def copy(item, step, sub):
        bit = 1 << orders[item][step]
        mask = bit | sub
        first = orders[item][0]
        src = part.at[item, flipped(me, mask)] if step == 0 else sendbuf.at[item, without(mask, first)]
        return remote(
            "ctx", src, landed.at[item, mask], (send_sem, recv_sem), (item, mask), flipped(me, bit)
        )

    def total_of(item, mask, upto):
        total = part[item, flipped(me, mask)].astype(F32)
        for step in range(upto):
            total = total + landed[item, 1 << orders[item][step] | mask].astype(F32)
        return total

    def subs(item, step):
        return submasks(orders[item][step + 1 :])

    for item in range(items):
        for sub in subs(item, 0):
            copy(item, 0, sub).start()
    for step in range(1, steps):
        for item in range(items):
            for sub in subs(item, step - 1):
                copy(item, step - 1, sub).wait_recv()
            for sub in subs(item, step):
                mask = 1 << orders[item][step] | sub
                slot = without(mask, orders[item][0])
                sendbuf[item, slot] = total_of(item, mask, step).astype(BF16)
                copy(item, step, sub).start()
    for item in range(items):
        for sub in subs(item, steps - 1):
            copy(item, steps - 1, sub).wait_recv()
        out[item] = total_of(item, 0, steps)
    for step in range(steps):
        for item in range(items):
            for sub in subs(item, step):
                copy(item, step, sub).wait_send()


def ctx_scatter(part, cid):
    count = lax.axis_size("ctx")
    items, _, rows, cols = part.shape
    dma = pltpu.SemaphoreType.DMA((items, count))
    return pl.pallas_call(
        functools.partial(ctx_scatter_kernel, count, items),
        out_shape=jax.ShapeDtypeStruct((items, rows, cols), F32),
        in_specs=[pl.BlockSpec(memory_space=VMEM)],
        out_specs=pl.BlockSpec(memory_space=VMEM),
        scratch_shapes=[
            VMEM(part.shape, BF16),
            VMEM((items, count // 2, rows, cols), BF16),
            dma,
            dma,
        ],
        compiler_params=pltpu.CompilerParams(
            collective_id=cid, has_side_effects=True, vmem_limit_bytes=56 * MIB
        ),
        cost_estimate=takes(60),
        name="ctx_scatter",
    )(part)


class Halving:
    def __init__(self, part, order):
        count = lax.axis_size("ctx")
        steps = count.bit_length() - 1
        self.order = list(order)
        self.left = list(range(steps))[::-1]
        self.total = part.reshape((2,) * steps + (part.shape[0] // count, part.shape[1]))

    def send(self):
        b = self.order.pop(0)
        axis = self.left.index(b)
        self.left.remove(b)
        mine = (lax.axis_index("ctx") >> b) & 1
        pick = functools.partial(lax.dynamic_index_in_dim, axis=axis, keepdims=False)
        pairs = [(i, i ^ (1 << b)) for i in range(lax.axis_size("ctx"))]
        self.got = lax.ppermute(pick(self.total, 1 - mine), "ctx", pairs)
        self.keep = pick(self.total, mine)

    def add(self):
        self.total = self.keep.astype(F32) + self.got.astype(F32)
        if self.order:
            self.total = self.total.astype(BF16)

    def finish(self):
        self.add()
        while self.order:
            self.send()
            self.add()
        return self.total


def pin(value, *halvings):
    value, gots = lax.optimization_barrier((value, [h.got for h in halvings]))
    for h, got in zip(halvings, gots):
        h.got = got
    return value


def cube_order(steps, turn):
    usual = list(range(steps))
    return usual if turn == 0 or steps < 2 else [1, 0] + usual[2:]


def weights_scatter_kernel(count, tp_count, plan, n_parts, *refs):
    refs = list(refs)
    parts = [refs.pop(0) for _ in range(n_parts)]
    gains = refs.pop(0)
    outs = [refs.pop(0) for _ in range(n_parts)]
    gains_out = refs.pop(0)
    landed = [refs.pop(0) for _ in range(n_parts)]
    sendbuf = [refs.pop(0) for _ in range(n_parts)]
    gains_landed, gains_send = refs.pop(0), refs.pop(0)
    sems = (refs.pop(0), refs.pop(0))
    gain_sems = (refs.pop(0), refs.pop(0))
    me = lax.axis_index("ctx")
    me_tp = lax.axis_index("tp")
    steps = count.bit_length() - 1
    tp_steps = tp_count.bit_length() - 1
    barrier = pltpu.get_barrier_semaphore()
    for b in range(steps):
        pl.semaphore_signal(
            barrier, inc=1, device_id={"ctx": flipped(me, 1 << b)}, device_id_type=MESH
        )
    for b in range(tp_steps):
        pl.semaphore_signal(
            barrier, inc=1, device_id={"tp": flipped(me_tp, 1 << b)}, device_id_type=MESH
        )
    pl.semaphore_wait(barrier, steps + tp_steps)

    def subs(order, step):
        return submasks(order[step + 1 :])

    def copy(n, step, sub):
        p, item, order = plan[n]
        bit = 1 << order[step]
        mask = bit | sub
        if step == 0:
            src = parts[p].at[flipped(me, mask), item]
        else:
            src = sendbuf[p].at[without(mask, order[0]), item]
        return remote(
            "ctx", src, landed[p].at[mask, item], sems, (n, mask), flipped(me, bit)
        )

    def total_of(n, mask, upto):
        p, item, order = plan[n]
        total = parts[p][flipped(me, mask), item].astype(F32)
        for step in range(upto):
            total = total + landed[p][1 << order[step] | mask, item].astype(F32)
        return total

    for n, (_, _, order) in enumerate(plan):
        for sub in subs(order, 0):
            copy(n, 0, sub).start()

    gains_send[0] = gains[...]
    for step in range(tp_steps + steps):
        axis, bit, at = ("tp", step, me_tp) if step < tp_steps else ("ctx", step - tp_steps, me)
        go = remote(
            axis,
            gains_send.at[step],
            gains_landed.at[step],
            gain_sems,
            step,
            flipped(at, 1 << bit),
        )
        go.start()
        go.wait_recv()
        both = gains_send[step] + gains_landed[step]
        if step + 1 < tp_steps + steps:
            gains_send[step + 1] = both
        else:
            gains_out[...] = both
        go.wait_send()

    for step in range(1, steps):
        for n, (p, item, order) in enumerate(plan):
            for sub in subs(order, step - 1):
                copy(n, step - 1, sub).wait_recv()
            for sub in subs(order, step):
                mask = 1 << order[step] | sub
                sendbuf[p][without(mask, order[0]), item] = total_of(n, mask, step).astype(BF16)
                copy(n, step, sub).start()
    for n, (p, item, order) in enumerate(plan):
        for sub in subs(order, steps - 1):
            copy(n, steps - 1, sub).wait_recv()
        outs[p][item] = total_of(n, 0, steps)
    for step in range(steps):
        for n, (_, _, order) in enumerate(plan):
            for sub in subs(order, step):
                copy(n, step, sub).wait_send()


def weights_scatter(parts, gains, cid):
    count, tp_count = lax.axis_size("ctx"), lax.axis_size("tp")
    steps = count.bit_length() - 1
    rows = parts[0].shape[0] // count
    cut = max(c for c in range(1, 7) if rows % (16 * c) == 0) if rows % 16 == 0 else 1
    blocks = [p.reshape(count, cut, rows // cut, p.shape[1]) for p in parts]
    pairs = [(p, item) for item in range(cut) for p in range(len(parts))]
    plan = [(p, item, cube_order(steps, int(n % 4 == 3))) for n, (p, item) in enumerate(pairs)]
    hops = steps + tp_count.bit_length() - 1
    dma = pltpu.SemaphoreType.DMA((len(plan), count))
    out = pl.pallas_call(
        functools.partial(weights_scatter_kernel, count, tp_count, plan, len(parts)),
        out_shape=[jax.ShapeDtypeStruct(b.shape[1:], F32) for b in blocks]
        + [jax.ShapeDtypeStruct(gains.shape, F32)],
        in_specs=[pl.BlockSpec(memory_space=VMEM)] * (len(parts) + 1),
        out_specs=[pl.BlockSpec(memory_space=VMEM)] * (len(parts) + 1),
        scratch_shapes=[VMEM(b.shape, BF16) for b in blocks]
        + [VMEM((max(count // 2, 1),) + b.shape[1:], BF16) for b in blocks]
        + [VMEM((hops,) + gains.shape, F32)] * 2
        + [dma, dma, pltpu.SemaphoreType.DMA((hops,)), pltpu.SemaphoreType.DMA((hops,))],
        compiler_params=pltpu.CompilerParams(
            collective_id=cid, has_side_effects=True, vmem_limit_bytes=56 * MIB
        ),
        cost_estimate=takes(180),
        name="weights_scatter",
    )(*blocks, gains)
    return [o.reshape(rows, o.shape[-1]) for o in out[:-1]], out[-1]


def inv_rms(v):
    return lax.rsqrt(jnp.mean(v * v, axis=-1, keepdims=True) + EPS)


def rms_back(dy, v, g):
    r = inv_rms(v)
    dg = jnp.sum(dy * v * r, axis=tuple(range(v.ndim - 1)), keepdims=True)
    gdy = g * dy
    dv = r * gdy - v * (r * r * r) * jnp.mean(gdy * v, axis=-1, keepdims=True)
    return dv, dg.reshape(1, -1)


def add_to(ref, item, value):
    ref[...] = value if item == 0 else ref[...] + value


def enter_rows(item, _, ins, outs):
    tokens, gain = ins
    v = tokens[item].astype(F32)
    return v * inv_rms(v) * gain[...].astype(F32)


def mid_rows(item, branch, ins, outs):
    tokens, attn_gain, ffw_gain = ins
    branch_out, resid_out = outs
    branch_out[item] = branch
    resid = tokens[item].astype(F32) + branch * inv_rms(branch) * attn_gain[...].astype(F32)
    resid_out[item] = resid
    return resid * inv_rms(resid) * ffw_gain[...].astype(F32)


def turn_rows(item, branch, ins, outs):
    resid, cotangent, gain = ins
    layer_out, gain_grad = outs
    g = gain[...].astype(F32)
    layer_out[item] = (resid[item] + branch * inv_rms(branch) * g).astype(BF16)
    dv, dg = rms_back(cotangent[item].astype(F32), branch, g)
    add_to(gain_grad, item, dg)
    return dv


def mid_back_rows(item, ffw_grad, ins, outs):
    resid, branch, cotangent, ffw_gain, attn_gain = ins
    resid_grad_out, ffw_gain_grad, attn_gain_grad = outs
    dv, dg = rms_back(ffw_grad, resid[item], ffw_gain[...].astype(F32))
    add_to(ffw_gain_grad, item, dg)
    resid_grad = cotangent[item].astype(F32) + dv
    resid_grad_out[item] = resid_grad
    dv, dg = rms_back(resid_grad, branch[item], attn_gain[...].astype(F32))
    add_to(attn_gain_grad, item, dg)
    return dv


def leave_rows(item, normed_grad, ins, outs):
    tokens, resid_grad, gain = ins
    tokens_grad, gain_grad = outs
    dv, dg = rms_back(normed_grad, tokens[item].astype(F32), gain[...].astype(F32))
    add_to(gain_grad, item, dg)
    tokens_grad[item] = resid_grad[item] + dv


def rotate(values, cosine, sine):
    half_dim = values.shape[-1] // 2
    low, high = values[..., :half_dim], values[..., half_dim:]
    return jnp.concatenate([low * cosine - high * sine, high * cosine + low * sine], -1)


def gelu_times(gate, up_val):
    return jax.nn.gelu(gate, approximate=True) * up_val


def body(
    tokens,
    doc_ids,
    attn_in_gain,
    query_weight,
    key_weight,
    value_weight,
    output_weight,
    attn_out_gain,
    ffw_in_gain,
    gate_weight,
    up_weight,
    down_weight,
    ffw_out_gain,
    cotangent,
):
    stretch_rows, seqs, slots, width = tokens.shape
    ctx_count = lax.axis_size("ctx")
    tp_count = lax.axis_size("tp")
    ctx_rank = lax.axis_index("ctx")
    stretch = stretch_rows * tp_count
    length = 2 * stretch * ctx_count
    rows = stretch * slots
    all_rows = seqs * rows
    local_heads = query_weight.shape[1] // HD
    local_kv = key_weight.shape[1] // HD
    group = local_heads // local_kv
    scale = HD ** (-0.5)
    own = (seqs, slots, stretch_rows, width)
    steps = ctx_count.bit_length() - 1
    usual, other = cube_order(steps, 0), cube_order(steps, 1)

    slot_stretch = jnp.stack([ctx_rank, 2 * ctx_count - 1 - ctx_rank])
    iota = jnp.arange(stretch, dtype=jnp.int32)
    query_tok = slot_stretch[:, None] * stretch + iota[None, :]
    row_tok = query_tok.reshape(rows)
    row_doc = jnp.concatenate(
        [lax.dynamic_slice_in_dim(doc_ids, slot_stretch[i] * stretch, stretch, 1) for i in (0, 1)],
        1,
    )
    row_start = jnp.sum(
        (doc_ids[:, None, :] < row_doc[:, :, None]).astype(jnp.int32), axis=-1
    )
    row_pos = row_tok[None] - row_start
    frequency = BASE ** (-jnp.arange(HD // 2).astype(F32) / (HD // 2))
    angles = row_pos.astype(F32)[..., None] * frequency
    cosine = jnp.cos(angles)[:, :, None, :]
    sine = jnp.sin(angles)[:, :, None, :]
    key_slot = jnp.arange(2 * ctx_count, dtype=jnp.int32)
    key_stretch = jnp.where(key_slot % 2 == 0, key_slot // 2, 2 * ctx_count - 1 - key_slot // 2)
    key_tok = (key_stretch[:, None] * stretch + iota[None, :]).reshape(length)
    allowed = (key_tok[None, None, :] <= row_tok[None, :, None]) & (
        key_tok[None, None, :] >= row_start[:, :, None]
    )

    def wide(gain):
        return gain.reshape(1, width)

    mine = jnp.transpose(tokens, (1, 2, 0, 3))
    upstream = jnp.transpose(cotangent, (1, 2, 0, 3))
    f32_rows = jax.ShapeDtypeStruct(own, F32)
    gain_shape = jax.ShapeDtypeStruct((1, width), F32)

    (normed_all,) = tp_exchange("enter", 1, enter_rows, [mine, wide(attn_in_gain)], [])
    normed_all = normed_all.reshape(all_rows, width)
    dot = functools.partial(jnp.dot, preferred_element_type=F32)
    ein = functools.partial(jnp.einsum, preferred_element_type=F32)
    keys = rotate(
        dot(normed_all, key_weight).reshape(seqs, rows, local_kv, HD), cosine, sine
    ).astype(BF16)
    values = dot(normed_all, value_weight).astype(BF16)
    queries = rotate(
        dot(normed_all, query_weight).reshape(seqs, rows, local_heads, HD), cosine, sine
    ).astype(BF16)
    kv = jnp.concatenate(
        [keys.reshape(seqs, rows, local_kv * HD), values.reshape(seqs, rows, local_kv * HD)], 0
    )
    kv_all = ctx_gather(kv, 2).reshape(2, seqs, length, local_kv, HD)
    keys_all, values_all = kv_all[0], kv_all[1]
    grouped = queries.reshape(seqs, rows, local_kv, group, HD)

    raw = ein("srkgd,sukd->skgru", grouped, keys_all)
    tanh = jnp.tanh(raw * (scale / CAP))
    exps = jnp.where(allowed[:, None, None], jnp.exp(CAP * tanh), 0.0)
    total = jnp.sum(exps, axis=-1)
    exps_low = exps.astype(BF16)
    attn = ein("skgru,sukd->srkgd", exps_low, values_all)
    total_rows = jnp.transpose(total, (0, 3, 1, 2))[..., None]
    attn = attn / total_rows
    attn_rows = attn.astype(BF16).reshape(all_rows, local_heads * HD)
    part = dot(attn_rows, output_weight).astype(BF16)

    def by_owner(value):
        return value.reshape(seqs, slots, tp_count, stretch_rows, width)

    ffw_all, branch, resid = tp_exchange(
        "middle",
        3,
        mid_rows,
        [mine, wide(attn_out_gain), wide(ffw_in_gain)],
        [f32_rows, f32_rows],
        by_owner(part),
    )
    ffw_all = ffw_all.reshape(all_rows, width)
    gate = dot(ffw_all, gate_weight)
    up = dot(ffw_all, up_weight)
    mixed, mixed_back = jax.vjp(gelu_times, gate, up)
    mixed = mixed.astype(BF16)
    part = dot(mixed, down_weight).astype(BF16)
    ffw_grad_all, layer_out, ffw_out_gain_part = tp_exchange(
        "turn",
        4,
        turn_rows,
        [resid, upstream, wide(ffw_out_gain)],
        [jax.ShapeDtypeStruct(own, BF16), gain_shape],
        by_owner(part),
    )
    ffw_grad_all = ffw_grad_all.reshape(all_rows, width)
    down_part = ein("rd,rf->df", ffw_grad_all, mixed).astype(BF16)
    ff_cut = down_part.shape[1] * 2 // 3
    down = [Halving(down_part[:, :ff_cut], usual), Halving(down_part[:, ff_cut:], other)]
    for h in down:
        h.send()
    mixed_grad = ein("rd,fd->rf", ffw_grad_all, down_weight)
    gate_grad, up_grad = mixed_back(mixed_grad)
    gate_grad = gate_grad.astype(BF16)
    up_grad = up_grad.astype(BF16)
    gate_part = ein("rd,rf->df", ffw_all, gate_grad).astype(BF16)
    gates = [Halving(gate_part[:, :ff_cut], usual), Halving(gate_part[:, ff_cut:], other)]
    for h in gates:
        h.send()
    up_part = ein("rd,rf->df", ffw_all, up_grad).astype(BF16)
    part = (
        ein("rf,df->rd", gate_grad, gate_weight) + ein("rf,df->rd", up_grad, up_weight)
    ).astype(BF16)
    branch_grad_all, resid_grad, ffw_in_gain_part, attn_out_gain_part = tp_exchange(
        "middle_back",
        5,
        mid_back_rows,
        [resid, branch, upstream, wide(ffw_in_gain), wide(attn_out_gain)],
        [f32_rows, gain_shape, gain_shape],
        by_owner(part),
    )
    branch_grad_all = pin(branch_grad_all.reshape(all_rows, width), *down)
    for h in down:
        h.add()
        h.send()
    output_part = ein("rd,rh->dh", branch_grad_all, attn_rows).astype(BF16)
    attn_grad = ein("rd,hd->rh", branch_grad_all, output_weight).reshape(attn.shape)
    row_dot = jnp.sum(attn_grad * attn, axis=-1)
    scaled = (attn_grad / total_rows).astype(BF16)
    shift = jnp.transpose(row_dot, (0, 2, 3, 1)) / total
    weight_grad = ein("srkgd,sukd->skgru", scaled, values_all)
    score_grad = (
        exps * (weight_grad - shift[..., None]) * (scale * (1.0 - tanh * tanh))
    ).astype(BF16)
    query_acc = ein("skgru,sukd->srkgd", score_grad, keys_all)
    key_acc = ein("skgru,srkgd->sukd", score_grad, grouped)
    value_acc = ein("skgru,srkgd->sukd", exps_low, scaled)
    kv_acc = jnp.concatenate([key_acc, value_acc], 0).astype(BF16)
    kv_sum = ctx_scatter(kv_acc.reshape(2 * seqs, ctx_count, rows, local_kv * HD), 6)
    kv_sum = pin(kv_sum, *down, *gates)
    for h in down + gates:
        h.add()
        h.send()
    key_grad = rotate(kv_sum[:seqs].reshape(seqs, rows, local_kv, HD), cosine, -sine)
    key_grad = key_grad.astype(BF16).reshape(all_rows, local_kv * HD)
    value_grad = kv_sum[seqs:].astype(BF16).reshape(all_rows, local_kv * HD)
    query_grad = rotate(query_acc.reshape(seqs, rows, local_heads, HD), cosine, -sine)
    query_grad = query_grad.astype(BF16).reshape(all_rows, local_heads * HD)
    qkv_grad = jnp.concatenate([query_grad, key_grad, value_grad], 1)
    qkv_weight = jnp.concatenate([query_weight, key_weight, value_weight], 1)
    part = ein("rh,dh->rd", qkv_grad, qkv_weight).astype(BF16)
    qkv_part = ein("rd,rh->dh", normed_all, qkv_grad).astype(BF16)
    tokens_grad, attn_in_gain_part = tp_exchange(
        "leave",
        7,
        leave_rows,
        [mine, resid_grad, wide(attn_in_gain)],
        [f32_rows, gain_shape],
        by_owner(part),
        gather=False,
    )
    gains = jnp.concatenate(
        [attn_in_gain_part, attn_out_gain_part, ffw_in_gain_part, ffw_out_gain_part], 0
    )
    gains = pin(gains, *gates)
    for h in gates:
        h.add()
        h.send()
    (up_sum, output_sum, qkv_sum), gains = weights_scatter(
        [up_part, output_part, qkv_part], gains, 8
    )
    down_sum = jnp.concatenate([h.finish() for h in down], 1)
    gate_sum = jnp.concatenate([h.finish() for h in gates], 1)
    share = width // ctx_count
    gains = lax.dynamic_slice_in_dim(gains, ctx_rank * share, share, 1)
    heads_end = local_heads * HD
    keys_end = heads_end + local_kv * HD
    return (
        jnp.transpose(layer_out, (2, 0, 1, 3)),
        jnp.transpose(tokens_grad, (2, 0, 1, 3)),
        gains[0],
        qkv_sum[:, :heads_end],
        qkv_sum[:, heads_end:keys_end],
        qkv_sum[:, keys_end:],
        output_sum.T,
        gains[1],
        gains[2],
        gate_sum,
        up_sum,
        down_sum.T,
        gains[3],
    )


def solution(mesh):
    placed = (
        P("tp", None, "ctx", None),
        P(),
        P(),
        P(None, "tp"),
        P(None, "tp"),
        P(None, "tp"),
        P("tp", None),
        P(),
        P(),
        P(None, "tp"),
        P(None, "tp"),
        P("tp", None),
        P(),
        P("tp", None, "ctx", None),
    )
    return jax.shard_map(
        body,
        mesh=mesh,
        in_specs=placed,
        out_specs=(
            P("tp", None, "ctx", None),
            P("tp", None, "ctx", None),
            P("ctx"),
            P("ctx", "tp"),
            P("ctx", "tp"),
            P("ctx", "tp"),
            P("tp", "ctx"),
            P("ctx"),
            P("ctx"),
            P("ctx", "tp"),
            P("ctx", "tp"),
            P("tp", "ctx"),
            P("ctx"),
        ),
        check_vma=False,
    )
```

```python
import functools

import jax
import jax.numpy as jnp
from jax import lax
from jax.experimental import pallas as pl
from jax.experimental.pallas import tpu as pltpu
from jax.sharding import PartitionSpec as P

HD = 256
EPS = 1e-06
CAP = 50.0
BASE = 10000.0
MIB = 1 << 20
F32 = jnp.float32
BF16 = jnp.bfloat16
VMEM = pltpu.VMEM
MESH = pl.DeviceIdType.MESH


def bits_of(mask):
    return [b for b in range(mask.bit_length()) if mask >> b & 1]


def flipped(index, mask):
    for b in bits_of(mask):
        index = index + (1 - 2 * ((index // (1 << b)) % 2)) * (1 << b)
    return index


def without(mask, bit):
    return (mask >> bit + 1 << bit) | (mask & (1 << bit) - 1)


def submasks(bits):
    masks = [0]
    for b in bits:
        masks = masks + [m | 1 << b for m in masks]
    return masks


def wavefront(items, stages, lag=2):
    for t in range(items + (stages - 1) * lag):
        for stage in range(stages):
            if 0 <= t - stage * lag < items:
                yield t - stage * lag, stage


def greet(axis, count):
    me = lax.axis_index(axis)
    barrier = pltpu.get_barrier_semaphore()
    steps = count.bit_length() - 1
    for b in range(steps):
        pl.semaphore_signal(
            barrier, inc=1, device_id={axis: flipped(me, 1 << b)}, device_id_type=MESH
        )
    pl.semaphore_wait(barrier, steps)


def remote(axis, src, dst, sems, at, partner):
    return pltpu.make_async_remote_copy(
        src_ref=src,
        dst_ref=dst,
        send_sem=sems[0].at[at],
        recv_sem=sems[1].at[at],
        device_id={axis: partner},
        device_id_type=MESH,
    )


def tp_kernel(fn, count, items, n_in, n_out, scatter, gather, *refs):
    refs = list(refs)
    part = refs.pop(0) if scatter else None
    ins = [refs.pop(0) for _ in range(n_in)]
    whole = refs.pop(0) if gather else None
    outs = [refs.pop(0) for _ in range(n_out)]
    if scatter:
        landed, sendbuf = refs.pop(0), refs.pop(0)
        rs_sems = (refs.pop(0), refs.pop(0))
    if gather:
        ag_sems = (refs.pop(0), refs.pop(0))
    me = lax.axis_index("tp")
    steps = count.bit_length() - 1
    order = list(range(steps))
    greet("tp", count)

    def rs_copy(item, step, sub):
        bit = 1 << order[step]
        mask = bit | sub
        src = part.at[item, :, flipped(me, mask)] if step == 0 else sendbuf.at[item, mask]
        return remote("tp", src, landed.at[item, mask], rs_sems, (item, mask), flipped(me, bit))

    def rs_sum(item, mask, upto):
        total = part[item, :, flipped(me, mask)].astype(F32)
        for step in range(upto):
            total = total + landed[item, 1 << order[step] | mask].astype(F32)
        return total

    def rs_subs(step):
        return submasks(order[step + 1 :])

    def ag_copy(item, step, mask):
        bit = 1 << order[steps - 1 - step]
        block = whole.at[item, :, flipped(me, mask)]
        return remote("tp", block, block, ag_sems, (item, mask | bit), flipped(me, bit))

    def ag_masks(step):
        return submasks([order[steps - 1 - s] for s in range(step)])

    if scatter:
        for item in range(items):
            for sub in rs_subs(0):
                rs_copy(item, 0, sub).start()
        for step in range(1, steps):
            for item in range(items):
                for sub in rs_subs(step - 1):
                    rs_copy(item, step - 1, sub).wait_recv()
                for sub in rs_subs(step):
                    mask = 1 << order[step] | sub
                    sendbuf[item, mask] = rs_sum(item, mask, step).astype(BF16)
                    rs_copy(item, step, sub).start()
    for item in range(items):
        total = None
        if scatter:
            for sub in rs_subs(steps - 1):
                rs_copy(item, steps - 1, sub).wait_recv()
            total = rs_sum(item, 0, steps)
        sent = fn(item, total, ins, outs)
        if gather:
            whole[item, :, me] = sent.astype(BF16)
            for step in range(steps):
                ag_copy(item, step, 0).start()
    if gather:
        for got in range(steps):
            for item in range(items):
                for mask in ag_masks(got):
                    ag_copy(item, got, mask).wait_recv()
                    for step in range(got + 1, steps):
                        ag_copy(item, step, mask | 1 << order[steps - 1 - got]).start()
        for step in range(steps):
            for item in range(items):
                for mask in ag_masks(step):
                    ag_copy(item, step, mask).wait_send()
    if scatter:
        for step in range(steps):
            for item in range(items):
                for sub in rs_subs(step):
                    rs_copy(item, step, sub).wait_send()


def takes(us):
    return pl.CostEstimate(flops=int(us * 1e7), bytes_accessed=0, transcendentals=0)


def tp_exchange(name, cid, fn, ins, outs, part=None, gather=True):
    count = lax.axis_size("tp")
    rows_shape = ins[0].shape
    items, slots, rows, width = rows_shape
    scatter = part is not None
    out_shape = list(outs)
    if gather:
        out_shape = [jax.ShapeDtypeStruct((items, slots, count, rows, width), BF16)] + out_shape
    scratch = []
    dma = pltpu.SemaphoreType.DMA((items, count))
    if scatter:
        scratch += [VMEM((items, count, slots, rows, width), BF16)] * 2 + [dma, dma]
    if gather:
        scratch += [dma, dma]
    args = ([part] if scatter else []) + list(ins)
    return pl.pallas_call(
        functools.partial(
            tp_kernel, fn, count, items, len(ins), len(outs), scatter, gather
        ),
        out_shape=out_shape,
        in_specs=[pl.BlockSpec(memory_space=VMEM)] * len(args),
        out_specs=[pl.BlockSpec(memory_space=VMEM)] * len(out_shape),
        scratch_shapes=scratch,
        compiler_params=pltpu.CompilerParams(
            collective_id=cid, has_side_effects=True, vmem_limit_bytes=40 * MIB
        ),
        cost_estimate=takes(18 * (scatter + gather)),
        name=name,
    )(*args)


def ctx_orders(items, steps):
    usual = list(range(steps))[::-1]
    if steps < 2:
        return [usual] * items
    other = usual[:-2] + [usual[-1], usual[-2]]
    return [other if i % 4 == 3 else usual for i in range(items)]


def ctx_gather_kernel(count, items, block, whole, send_sem, recv_sem, local_sem):
    me = lax.axis_index("ctx")
    steps = count.bit_length() - 1
    orders = ctx_orders(items, steps)
    own = pltpu.make_async_copy(block, whole.at[:, me], local_sem)
    own.start()
    greet("ctx", count)

    def copy(item, step, mask):
        bit = 1 << orders[item][step]
        dst = whole.at[item, flipped(me, mask)]
        src = block.at[item] if mask == 0 else dst
        return remote(
            "ctx", src, dst, (send_sem, recv_sem), (item, mask | bit), flipped(me, bit)
        )

    def masks(item, step):
        return submasks(orders[item][:step])

    for step in range(steps):
        for item in range(items):
            copy(item, step, 0).start()
    for item, got in wavefront(items, steps):
        for mask in masks(item, got):
            copy(item, got, mask).wait_recv()
            for step in range(got + 1, steps):
                copy(item, step, mask | 1 << orders[item][got]).start()
    for step in range(steps):
        for item in range(items):
            for mask in masks(item, step):
                copy(item, step, mask).wait_send()
    own.wait()


def ctx_gather(block, cid):
    count = lax.axis_size("ctx")
    items, rows, cols = block.shape
    dma = pltpu.SemaphoreType.DMA((items, count))
    return pl.pallas_call(
        functools.partial(ctx_gather_kernel, count, items),
        out_shape=jax.ShapeDtypeStruct((items, count, rows, cols), block.dtype),
        in_specs=[pl.BlockSpec(memory_space=VMEM)],
        out_specs=pl.BlockSpec(memory_space=VMEM),
        scratch_shapes=[dma, dma, pltpu.SemaphoreType.DMA],
        compiler_params=pltpu.CompilerParams(
            collective_id=cid, has_side_effects=True, vmem_limit_bytes=56 * MIB
        ),
        cost_estimate=takes(55),
        name="ctx_gather",
    )(block)


def ctx_scatter_kernel(count, items, part, out, landed, sendbuf, send_sem, recv_sem):
    me = lax.axis_index("ctx")
    steps = count.bit_length() - 1
    orders = [order[::-1] for order in ctx_orders(items, steps)]
    greet("ctx", count)

    def copy(item, step, sub):
        bit = 1 << orders[item][step]
        mask = bit | sub
        first = orders[item][0]
        src = part.at[item, flipped(me, mask)] if step == 0 else sendbuf.at[item, without(mask, first)]
        return remote(
            "ctx", src, landed.at[item, mask], (send_sem, recv_sem), (item, mask), flipped(me, bit)
        )

    def total_of(item, mask, upto):
        total = part[item, flipped(me, mask)].astype(F32)
        for step in range(upto):
            total = total + landed[item, 1 << orders[item][step] | mask].astype(F32)
        return total

    def subs(item, step):
        return submasks(orders[item][step + 1 :])

    for item in range(items):
        for sub in subs(item, 0):
            copy(item, 0, sub).start()
    for item, got in wavefront(items, steps):
        for sub in subs(item, got):
            copy(item, got, sub).wait_recv()
        step = got + 1
        if step == steps:
            out[item] = total_of(item, 0, steps)
            continue
        for sub in subs(item, step):
            mask = 1 << orders[item][step] | sub
            slot = without(mask, orders[item][0])
            sendbuf[item, slot] = total_of(item, mask, step).astype(BF16)
            copy(item, step, sub).start()
    for step in range(steps):
        for item in range(items):
            for sub in subs(item, step):
                copy(item, step, sub).wait_send()


def ctx_scatter(part, cid):
    count = lax.axis_size("ctx")
    items, _, rows, cols = part.shape
    dma = pltpu.SemaphoreType.DMA((items, count))
    return pl.pallas_call(
        functools.partial(ctx_scatter_kernel, count, items),
        out_shape=jax.ShapeDtypeStruct((items, rows, cols), F32),
        in_specs=[pl.BlockSpec(memory_space=VMEM)],
        out_specs=pl.BlockSpec(memory_space=VMEM),
        scratch_shapes=[
            VMEM(part.shape, BF16),
            VMEM((items, count // 2, rows, cols), BF16),
            dma,
            dma,
        ],
        compiler_params=pltpu.CompilerParams(
            collective_id=cid, has_side_effects=True, vmem_limit_bytes=56 * MIB
        ),
        cost_estimate=takes(60),
        name="ctx_scatter",
    )(part)


def pairs_of(b):
    return [(i, i ^ (1 << b)) for i in range(lax.axis_size("ctx"))]


class Halving:
    def __init__(self, part, order):
        self.order = list(order)
        self.left = sorted(order, reverse=True)
        owners = 1 << len(self.order)
        self.total = part.reshape((2,) * len(self.order) + (part.shape[0] // owners, part.shape[1]))

    def send(self):
        b = self.order.pop(0)
        axis = self.left.index(b)
        self.left.remove(b)
        mine = (lax.axis_index("ctx") >> b) & 1
        pick = functools.partial(lax.dynamic_index_in_dim, axis=axis, keepdims=False)
        self.got = lax.ppermute(pick(self.total, 1 - mine), "ctx", pairs_of(b))
        self.keep = pick(self.total, mine)

    def add(self):
        self.total = self.keep.astype(F32) + self.got.astype(F32)
        if self.order:
            self.total = self.total.astype(BF16)

    def finish(self):
        self.add()
        while self.order:
            self.send()
            self.add()
        return self.total


class Swap:
    def __init__(self, value, b):
        self.got = lax.ppermute(value, "ctx", pairs_of(b))


def owner_half(rows_of_owners, b, which):
    total, cols = rows_of_owners.shape
    low = (total // lax.axis_size("ctx")) << b
    cut = rows_of_owners.reshape(total // (2 * low), 2, low, cols)
    return lax.dynamic_index_in_dim(cut, which, 1, keepdims=False).reshape(total // 2, cols)


def pin(value, *halvings):
    value, gots = lax.optimization_barrier((value, [h.got for h in halvings]))
    for h, got in zip(halvings, gots):
        h.got = got
    return value


def cube_order(steps, turn):
    usual = list(range(steps))
    return usual if turn == 0 or steps < 2 else [1, 0] + usual[2:]


def weights_scatter_kernel(count, tp_count, plan, n_parts, *refs):
    refs = list(refs)
    parts = [refs.pop(0) for _ in range(n_parts)]
    gains = refs.pop(0)
    outs = [refs.pop(0) for _ in range(n_parts)]
    gains_out = refs.pop(0)
    landed = [refs.pop(0) for _ in range(n_parts)]
    sendbuf = [refs.pop(0) for _ in range(n_parts)]
    gains_landed, gains_send = refs.pop(0), refs.pop(0)
    sems = (refs.pop(0), refs.pop(0))
    gain_sems = (refs.pop(0), refs.pop(0))
    me = lax.axis_index("ctx")
    me_tp = lax.axis_index("tp")
    steps = count.bit_length() - 1
    tp_steps = tp_count.bit_length() - 1
    barrier = pltpu.get_barrier_semaphore()
    for b in range(steps):
        pl.semaphore_signal(
            barrier, inc=1, device_id={"ctx": flipped(me, 1 << b)}, device_id_type=MESH
        )
    for b in range(tp_steps):
        pl.semaphore_signal(
            barrier, inc=1, device_id={"tp": flipped(me_tp, 1 << b)}, device_id_type=MESH
        )
    pl.semaphore_wait(barrier, steps + tp_steps)

    def subs(order, step):
        return submasks(order[step + 1 :])

    def copy(n, step, sub):
        p, item, order = plan[n]
        bit = 1 << order[step]
        mask = bit | sub
        if step == 0:
            src = parts[p].at[flipped(me, mask), item]
        else:
            src = sendbuf[p].at[without(mask, order[0]), item]
        return remote(
            "ctx", src, landed[p].at[mask, item], sems, (n, mask), flipped(me, bit)
        )

    def total_of(n, mask, upto):
        p, item, order = plan[n]
        total = parts[p][flipped(me, mask), item].astype(F32)
        for step in range(upto):
            total = total + landed[p][1 << order[step] | mask, item].astype(F32)
        return total

    for n, (_, _, order) in enumerate(plan):
        for sub in subs(order, 0):
            copy(n, 0, sub).start()

    gains_send[0] = gains[...]
    for step in range(tp_steps + steps):
        axis, bit, at = ("tp", step, me_tp) if step < tp_steps else ("ctx", step - tp_steps, me)
        go = remote(
            axis,
            gains_send.at[step],
            gains_landed.at[step],
            gain_sems,
            step,
            flipped(at, 1 << bit),
        )
        go.start()
        go.wait_recv()
        both = gains_send[step] + gains_landed[step]
        if step + 1 < tp_steps + steps:
            gains_send[step + 1] = both
        else:
            gains_out[...] = both
        go.wait_send()

    for n, got in wavefront(len(plan), steps):
        p, item, order = plan[n]
        for sub in subs(order, got):
            copy(n, got, sub).wait_recv()
        step = got + 1
        if step == steps:
            outs[p][item] = total_of(n, 0, steps)
            continue
        for sub in subs(order, step):
            mask = 1 << order[step] | sub
            sendbuf[p][without(mask, order[0]), item] = total_of(n, mask, step).astype(BF16)
            copy(n, step, sub).start()
    for step in range(steps):
        for n, (_, _, order) in enumerate(plan):
            for sub in subs(order, step):
                copy(n, step, sub).wait_send()


def weights_scatter(parts, gains, cid):
    count, tp_count = lax.axis_size("ctx"), lax.axis_size("tp")
    steps = count.bit_length() - 1
    rows = parts[0].shape[0] // count
    cut = max(c for c in range(1, 7) if rows % (16 * c) == 0) if rows % 16 == 0 else 1
    blocks = [p.reshape(count, cut, rows // cut, p.shape[1]) for p in parts]
    pairs = [(p, item) for item in range(cut) for p in range(len(parts))]
    plan = [(p, item, cube_order(steps, int(n % 4 == 3))) for n, (p, item) in enumerate(pairs)]
    hops = steps + tp_count.bit_length() - 1
    dma = pltpu.SemaphoreType.DMA((len(plan), count))
    out = pl.pallas_call(
        functools.partial(weights_scatter_kernel, count, tp_count, plan, len(parts)),
        out_shape=[jax.ShapeDtypeStruct(b.shape[1:], F32) for b in blocks]
        + [jax.ShapeDtypeStruct(gains.shape, F32)],
        in_specs=[pl.BlockSpec(memory_space=VMEM)] * (len(parts) + 1),
        out_specs=[pl.BlockSpec(memory_space=VMEM)] * (len(parts) + 1),
        scratch_shapes=[VMEM(b.shape, BF16) for b in blocks]
        + [VMEM((max(count // 2, 1),) + b.shape[1:], BF16) for b in blocks]
        + [VMEM((hops,) + gains.shape, F32)] * 2
        + [dma, dma, pltpu.SemaphoreType.DMA((hops,)), pltpu.SemaphoreType.DMA((hops,))],
        compiler_params=pltpu.CompilerParams(
            collective_id=cid, has_side_effects=True, vmem_limit_bytes=56 * MIB
        ),
        cost_estimate=takes(80),
        name="weights_scatter",
    )(*blocks, gains)
    return [o.reshape(rows, o.shape[-1]) for o in out[:-1]], out[-1]


def inv_rms(v):
    return lax.rsqrt(jnp.mean(v * v, axis=-1, keepdims=True) + EPS)


def rms_back(dy, v, g):
    r = inv_rms(v)
    dg = jnp.sum(dy * v * r, axis=tuple(range(v.ndim - 1)), keepdims=True)
    gdy = g * dy
    dv = r * gdy - v * (r * r * r) * jnp.mean(gdy * v, axis=-1, keepdims=True)
    return dv, dg.reshape(1, -1)


def add_to(ref, item, value):
    ref[...] = value if item == 0 else ref[...] + value


def enter_rows(item, _, ins, outs):
    tokens, gain = ins
    v = tokens[item].astype(F32)
    return v * inv_rms(v) * gain[...].astype(F32)


def mid_rows(item, branch, ins, outs):
    tokens, attn_gain, ffw_gain = ins
    branch_out, resid_out = outs
    branch_out[item] = branch
    resid = tokens[item].astype(F32) + branch * inv_rms(branch) * attn_gain[...].astype(F32)
    resid_out[item] = resid
    return resid * inv_rms(resid) * ffw_gain[...].astype(F32)


def turn_rows(item, branch, ins, outs):
    resid, cotangent, gain = ins
    layer_out, gain_grad = outs
    g = gain[...].astype(F32)
    layer_out[item] = (resid[item] + branch * inv_rms(branch) * g).astype(BF16)
    dv, dg = rms_back(cotangent[item].astype(F32), branch, g)
    add_to(gain_grad, item, dg)
    return dv


def mid_back_rows(item, ffw_grad, ins, outs):
    resid, branch, cotangent, ffw_gain, attn_gain = ins
    resid_grad_out, ffw_gain_grad, attn_gain_grad = outs
    dv, dg = rms_back(ffw_grad, resid[item], ffw_gain[...].astype(F32))
    add_to(ffw_gain_grad, item, dg)
    resid_grad = cotangent[item].astype(F32) + dv
    resid_grad_out[item] = resid_grad
    dv, dg = rms_back(resid_grad, branch[item], attn_gain[...].astype(F32))
    add_to(attn_gain_grad, item, dg)
    return dv


def leave_rows(item, normed_grad, ins, outs):
    tokens, resid_grad, gain = ins
    tokens_grad, gain_grad = outs
    dv, dg = rms_back(normed_grad, tokens[item].astype(F32), gain[...].astype(F32))
    add_to(gain_grad, item, dg)
    tokens_grad[item] = resid_grad[item] + dv


def rotate(values, cosine, sine):
    half_dim = values.shape[-1] // 2
    low, high = values[..., :half_dim], values[..., half_dim:]
    return jnp.concatenate([low * cosine - high * sine, high * cosine + low * sine], -1)


def gelu_times(gate, up_val):
    return jax.nn.gelu(gate, approximate=True) * up_val


def body(
    tokens,
    doc_ids,
    attn_in_gain,
    query_weight,
    key_weight,
    value_weight,
    output_weight,
    attn_out_gain,
    ffw_in_gain,
    gate_weight,
    up_weight,
    down_weight,
    ffw_out_gain,
    cotangent,
):
    stretch_rows, seqs, slots, width = tokens.shape
    ctx_count = lax.axis_size("ctx")
    tp_count = lax.axis_size("tp")
    ctx_rank = lax.axis_index("ctx")
    stretch = stretch_rows * tp_count
    length = 2 * stretch * ctx_count
    rows = stretch * slots
    all_rows = seqs * rows
    local_heads = query_weight.shape[1] // HD
    local_kv = key_weight.shape[1] // HD
    group = local_heads // local_kv
    scale = HD ** (-0.5)
    own = (seqs, slots, stretch_rows, width)
    steps = ctx_count.bit_length() - 1
    usual, other = cube_order(steps, 0), cube_order(steps, 1)

    slot_stretch = jnp.stack([ctx_rank, 2 * ctx_count - 1 - ctx_rank])
    iota = jnp.arange(stretch, dtype=jnp.int32)
    query_tok = slot_stretch[:, None] * stretch + iota[None, :]
    row_tok = query_tok.reshape(rows)
    row_doc = jnp.concatenate(
        [lax.dynamic_slice_in_dim(doc_ids, slot_stretch[i] * stretch, stretch, 1) for i in (0, 1)],
        1,
    )
    row_start = jnp.sum(
        (doc_ids[:, None, :] < row_doc[:, :, None]).astype(jnp.int32), axis=-1
    )
    row_pos = row_tok[None] - row_start
    frequency = BASE ** (-jnp.arange(HD // 2).astype(F32) / (HD // 2))
    angles = row_pos.astype(F32)[..., None] * frequency
    cosine = jnp.cos(angles)[:, :, None, :]
    sine = jnp.sin(angles)[:, :, None, :]
    key_slot = jnp.arange(2 * ctx_count, dtype=jnp.int32)
    key_stretch = jnp.where(key_slot % 2 == 0, key_slot // 2, 2 * ctx_count - 1 - key_slot // 2)
    key_tok = (key_stretch[:, None] * stretch + iota[None, :]).reshape(length)
    allowed = (key_tok[None, None, :] <= row_tok[None, :, None]) & (
        key_tok[None, None, :] >= row_start[:, :, None]
    )

    def wide(gain):
        return gain.reshape(1, width)

    mine = jnp.transpose(tokens, (1, 2, 0, 3))
    upstream = jnp.transpose(cotangent, (1, 2, 0, 3))
    f32_rows = jax.ShapeDtypeStruct(own, F32)
    gain_shape = jax.ShapeDtypeStruct((1, width), F32)

    (normed_all,) = tp_exchange("enter", 1, enter_rows, [mine, wide(attn_in_gain)], [])
    normed_all = normed_all.reshape(all_rows, width)
    dot = functools.partial(jnp.dot, preferred_element_type=F32)
    ein = functools.partial(jnp.einsum, preferred_element_type=F32)
    keys = rotate(
        dot(normed_all, key_weight).reshape(seqs, rows, local_kv, HD), cosine, sine
    ).astype(BF16)
    values = dot(normed_all, value_weight).astype(BF16)
    queries = rotate(
        dot(normed_all, query_weight).reshape(seqs, rows, local_heads, HD), cosine, sine
    ).astype(BF16)
    kv = jnp.concatenate(
        [keys.reshape(seqs, rows, local_kv * HD), values.reshape(seqs, rows, local_kv * HD)], 0
    )
    kv_all = ctx_gather(kv, 2).reshape(2, seqs, length, local_kv, HD)
    keys_all, values_all = kv_all[0], kv_all[1]
    grouped = queries.reshape(seqs, rows, local_kv, group, HD)

    raw = ein("srkgd,sukd->skgru", grouped, keys_all)
    tanh = jnp.tanh(raw * (scale / CAP))
    exps = jnp.where(allowed[:, None, None], jnp.exp(CAP * tanh), 0.0)
    total = jnp.sum(exps, axis=-1)
    exps_low = exps.astype(BF16)
    attn = ein("skgru,sukd->srkgd", exps_low, values_all)
    total_rows = jnp.transpose(total, (0, 3, 1, 2))[..., None]
    attn = attn / total_rows
    attn_rows = attn.astype(BF16).reshape(all_rows, local_heads * HD)
    part = dot(attn_rows, output_weight).astype(BF16)

    def by_owner(value):
        return value.reshape(seqs, slots, tp_count, stretch_rows, width)

    ffw_all, branch, resid = tp_exchange(
        "middle",
        3,
        mid_rows,
        [mine, wide(attn_out_gain), wide(ffw_in_gain)],
        [f32_rows, f32_rows],
        by_owner(part),
    )
    ffw_all = ffw_all.reshape(all_rows, width)
    pair = min(1, steps - 1)
    others = [b for b in usual if b != pair]
    pair_bit = (ctx_rank >> pair) & 1
    ffw_turned = ffw_all.T
    ffw_mine = owner_half(ffw_turned, pair, pair_bit)
    ffw_swap = Swap(owner_half(ffw_turned, pair, 1 - pair_bit), pair)
    gate = dot(ffw_all, gate_weight)
    up = dot(ffw_all, up_weight)
    mixed, mixed_back = jax.vjp(gelu_times, gate, up)
    mixed = mixed.astype(BF16)
    mixed_swap = Swap(mixed, pair)
    part = pin(dot(mixed, down_weight).astype(BF16), ffw_swap)
    ffw_grad_all, layer_out, ffw_out_gain_part = tp_exchange(
        "turn",
        4,
        turn_rows,
        [resid, upstream, wide(ffw_out_gain)],
        [jax.ShapeDtypeStruct(own, BF16), gain_shape],
        by_owner(part),
    )
    ffw_grad_all = ffw_grad_all.reshape(all_rows, width)
    grad_turned = ffw_grad_all.T
    grad_mine = owner_half(grad_turned, pair, pair_bit)
    grad_swap = Swap(owner_half(grad_turned, pair, 1 - pair_bit), pair)
    mixed_grad = ein("rd,fd->rf", ffw_grad_all, down_weight)
    gate_grad, up_grad = mixed_back(mixed_grad)
    gate_grad = gate_grad.astype(BF16)
    up_grad = up_grad.astype(BF16)
    gate_swap = Swap(gate_grad, pair)
    up_swap = Swap(up_grad, pair)
    part = (
        ein("rf,df->rd", gate_grad, gate_weight) + ein("rf,df->rd", up_grad, up_weight)
    ).astype(BF16)
    branch_grad_all, resid_grad, ffw_in_gain_part, attn_out_gain_part = tp_exchange(
        "middle_back",
        5,
        mid_back_rows,
        [resid, branch, upstream, wide(ffw_in_gain), wide(attn_out_gain)],
        [f32_rows, gain_shape, gain_shape],
        by_owner(part),
    )
    branch_grad_all = pin(branch_grad_all.reshape(all_rows, width), ffw_swap, mixed_swap, grad_swap)
    down = Halving((dot(grad_mine, mixed) + dot(grad_swap.got, mixed_swap.got)).astype(BF16), others)
    down.send()
    output_part = ein("rd,rh->dh", branch_grad_all, attn_rows).astype(BF16)
    attn_grad = ein("rd,hd->rh", branch_grad_all, output_weight).reshape(attn.shape)
    row_dot = jnp.sum(attn_grad * attn, axis=-1)
    scaled = (attn_grad / total_rows).astype(BF16)
    shift = jnp.transpose(row_dot, (0, 2, 3, 1)) / total
    weight_grad = ein("srkgd,sukd->skgru", scaled, values_all)
    score_grad = (
        exps * (weight_grad - shift[..., None]) * (scale * (1.0 - tanh * tanh))
    ).astype(BF16)
    query_acc = ein("skgru,sukd->srkgd", score_grad, keys_all)
    key_acc = ein("skgru,srkgd->sukd", score_grad, grouped)
    value_acc = ein("skgru,srkgd->sukd", exps_low, scaled)
    kv_acc = jnp.concatenate([key_acc, value_acc], 0).astype(BF16)
    kv_acc = pin(kv_acc, gate_swap, down)
    down.add()
    down.send()
    gates = Halving((dot(ffw_mine, gate_grad) + dot(ffw_swap.got, gate_swap.got)).astype(BF16), others)
    gates.send()
    kv_sum = ctx_scatter(kv_acc.reshape(2 * seqs, ctx_count, rows, local_kv * HD), 6)
    kv_sum = pin(kv_sum, up_swap, gates, down)
    down_sum = down.finish()
    gates.add()
    gates.send()
    ups = Halving((dot(ffw_mine, up_grad) + dot(ffw_swap.got, up_swap.got)).astype(BF16), others)
    ups.send()
    key_grad = rotate(kv_sum[:seqs].reshape(seqs, rows, local_kv, HD), cosine, -sine)
    key_grad = key_grad.astype(BF16).reshape(all_rows, local_kv * HD)
    value_grad = kv_sum[seqs:].astype(BF16).reshape(all_rows, local_kv * HD)
    query_grad = rotate(query_acc.reshape(seqs, rows, local_heads, HD), cosine, -sine)
    query_grad = query_grad.astype(BF16).reshape(all_rows, local_heads * HD)
    qkv_grad = jnp.concatenate([query_grad, key_grad, value_grad], 1)
    qkv_weight = jnp.concatenate([query_weight, key_weight, value_weight], 1)
    part = ein("rh,dh->rd", qkv_grad, qkv_weight).astype(BF16)
    qkv_part = ein("rd,rh->dh", normed_all, qkv_grad).astype(BF16)
    tokens_grad, attn_in_gain_part = tp_exchange(
        "leave",
        7,
        leave_rows,
        [mine, resid_grad, wide(attn_in_gain)],
        [f32_rows, gain_shape],
        by_owner(part),
        gather=False,
    )
    gains = jnp.concatenate(
        [attn_in_gain_part, attn_out_gain_part, ffw_in_gain_part, ffw_out_gain_part], 0
    )
    gains = pin(gains, ups)
    ups.add()
    ups.send()
    (output_sum, qkv_sum), gains = weights_scatter([output_part, qkv_part], gains, 8)
    gate_sum, up_sum = gates.finish(), ups.finish()
    share = width // ctx_count
    gains = lax.dynamic_slice_in_dim(gains, ctx_rank * share, share, 1)
    heads_end = local_heads * HD
    keys_end = heads_end + local_kv * HD
    return (
        jnp.transpose(layer_out, (2, 0, 1, 3)),
        jnp.transpose(tokens_grad, (2, 0, 1, 3)),
        gains[0],
        qkv_sum[:, :heads_end],
        qkv_sum[:, heads_end:keys_end],
        qkv_sum[:, keys_end:],
        output_sum.T,
        gains[1],
        gains[2],
        gate_sum,
        up_sum,
        down_sum.T,
        gains[3],
    )


def solution(mesh):
    placed = (
        P("tp", None, "ctx", None),
        P(),
        P(),
        P(None, "tp"),
        P(None, "tp"),
        P(None, "tp"),
        P("tp", None),
        P(),
        P(),
        P(None, "tp"),
        P(None, "tp"),
        P("tp", None),
        P(),
        P("tp", None, "ctx", None),
    )
    return jax.shard_map(
        body,
        mesh=mesh,
        in_specs=placed,
        out_specs=(
            P("tp", None, "ctx", None),
            P("tp", None, "ctx", None),
            P("ctx"),
            P("ctx", "tp"),
            P("ctx", "tp"),
            P("ctx", "tp"),
            P("tp", "ctx"),
            P("ctx"),
            P("ctx"),
            P("ctx", "tp"),
            P("ctx", "tp"),
            P("tp", "ctx"),
            P("ctx"),
        ),
        check_vma=False,
    )
```

```python
import functools

import jax
import jax.numpy as jnp
from jax import lax
from jax.experimental import pallas as pl
from jax.experimental.pallas import tpu as pltpu
from jax.sharding import PartitionSpec as P

HD = 256
EPS = 1e-06
CAP = 50.0
BASE = 10000.0
MIB = 1 << 20
F32 = jnp.float32
BF16 = jnp.bfloat16
VMEM = pltpu.VMEM
MESH = pl.DeviceIdType.MESH


def bits_of(mask):
    return [b for b in range(mask.bit_length()) if mask >> b & 1]


def flipped(index, mask):
    for b in bits_of(mask):
        index = index + (1 - 2 * ((index // (1 << b)) % 2)) * (1 << b)
    return index


def without(mask, bit):
    return (mask >> bit + 1 << bit) | (mask & (1 << bit) - 1)


def submasks(bits):
    masks = [0]
    for b in bits:
        masks = masks + [m | 1 << b for m in masks]
    return masks


def scatter_events(orders):
    steps = len(orders[0])
    usual = [i for i, order in enumerate(orders) if order[0] == 0]
    other = [i for i, order in enumerate(orders) if order[0] != 0]
    events = []
    for t in range(len(usual) + steps - 1):
        events += [(usual[t - s], s) for s in range(steps) if 0 <= t - s < len(usual)]
        if 1 <= t <= len(other):
            events.append((other[t - 1], 0))
    events += [(i, 0) for i in other[max(0, len(usual) + steps - 2) :]]
    for t in range(len(other) + steps - 2):
        events += [(other[t - s + 1], s) for s in range(1, steps) if 0 <= t - s + 1 < len(other)]
    return events


def greet(axis, count):
    me = lax.axis_index(axis)
    barrier = pltpu.get_barrier_semaphore()
    steps = count.bit_length() - 1
    for b in range(steps):
        pl.semaphore_signal(
            barrier, inc=1, device_id={axis: flipped(me, 1 << b)}, device_id_type=MESH
        )
    pl.semaphore_wait(barrier, steps)


def remote(axis, src, dst, sems, at, partner):
    return pltpu.make_async_remote_copy(
        src_ref=src,
        dst_ref=dst,
        send_sem=sems[0].at[at],
        recv_sem=sems[1].at[at],
        device_id={axis: partner},
        device_id_type=MESH,
    )


def tp_kernel(fn, count, items, n_in, n_out, scatter, gather, *refs):
    refs = list(refs)
    part = refs.pop(0) if scatter else None
    ins = [refs.pop(0) for _ in range(n_in)]
    whole = refs.pop(0) if gather else None
    outs = [refs.pop(0) for _ in range(n_out)]
    if scatter:
        landed, sendbuf = refs.pop(0), refs.pop(0)
        rs_sems = (refs.pop(0), refs.pop(0))
    if gather:
        ag_sems = (refs.pop(0), refs.pop(0))
    me = lax.axis_index("tp")
    steps = count.bit_length() - 1
    order = list(range(steps))
    greet("tp", count)

    def rs_copy(item, step, sub):
        bit = 1 << order[step]
        mask = bit | sub
        src = part.at[item, :, flipped(me, mask)] if step == 0 else sendbuf.at[item, mask]
        return remote("tp", src, landed.at[item, mask], rs_sems, (item, mask), flipped(me, bit))

    def rs_sum(item, mask, upto):
        total = part[item, :, flipped(me, mask)].astype(F32)
        for step in range(upto):
            total = total + landed[item, 1 << order[step] | mask].astype(F32)
        return total

    def rs_subs(step):
        return submasks(order[step + 1 :])

    def ag_copy(item, step, mask):
        bit = 1 << order[steps - 1 - step]
        block = whole.at[item, :, flipped(me, mask)]
        return remote("tp", block, block, ag_sems, (item, mask | bit), flipped(me, bit))

    def ag_masks(step):
        return submasks([order[steps - 1 - s] for s in range(step)])

    if scatter:
        for item in range(items):
            for sub in rs_subs(0):
                rs_copy(item, 0, sub).start()
        for step in range(1, steps):
            for item in range(items):
                for sub in rs_subs(step - 1):
                    rs_copy(item, step - 1, sub).wait_recv()
                for sub in rs_subs(step):
                    mask = 1 << order[step] | sub
                    sendbuf[item, mask] = rs_sum(item, mask, step).astype(BF16)
                    rs_copy(item, step, sub).start()
    for item in range(items):
        total = None
        if scatter:
            for sub in rs_subs(steps - 1):
                rs_copy(item, steps - 1, sub).wait_recv()
            total = rs_sum(item, 0, steps)
        sent = fn(item, total, ins, outs)
        if gather:
            whole[item, :, me] = sent.astype(BF16)
            for step in range(steps):
                ag_copy(item, step, 0).start()
    if gather:
        for got in range(steps):
            for item in range(items):
                for mask in ag_masks(got):
                    ag_copy(item, got, mask).wait_recv()
                    for step in range(got + 1, steps):
                        ag_copy(item, step, mask | 1 << order[steps - 1 - got]).start()
        for step in range(steps):
            for item in range(items):
                for mask in ag_masks(step):
                    ag_copy(item, step, mask).wait_send()
    if scatter:
        for step in range(steps):
            for item in range(items):
                for sub in rs_subs(step):
                    rs_copy(item, step, sub).wait_send()


def takes(us):
    return pl.CostEstimate(flops=int(us * 1e7), bytes_accessed=0, transcendentals=0)


def tp_exchange(name, cid, fn, ins, outs, part=None, gather=True):
    count = lax.axis_size("tp")
    rows_shape = ins[0].shape
    items, slots, rows, width = rows_shape
    scatter = part is not None
    out_shape = list(outs)
    if gather:
        out_shape = [jax.ShapeDtypeStruct((items, slots, count, rows, width), BF16)] + out_shape
    scratch = []
    dma = pltpu.SemaphoreType.DMA((items, count))
    if scatter:
        scratch += [VMEM((items, count, slots, rows, width), BF16)] * 2 + [dma, dma]
    if gather:
        scratch += [dma, dma]
    args = ([part] if scatter else []) + list(ins)
    return pl.pallas_call(
        functools.partial(
            tp_kernel, fn, count, items, len(ins), len(outs), scatter, gather
        ),
        out_shape=out_shape,
        in_specs=[pl.BlockSpec(memory_space=VMEM)] * len(args),
        out_specs=[pl.BlockSpec(memory_space=VMEM)] * len(out_shape),
        scratch_shapes=scratch,
        compiler_params=pltpu.CompilerParams(
            collective_id=cid, has_side_effects=True, vmem_limit_bytes=40 * MIB
        ),
        cost_estimate=takes(18 * (scatter + gather)),
        name=name,
    )(*args)


def cube_order(steps, turned):
    usual = list(range(steps))
    return [1, 0] + usual[2:] if turned and steps > 1 else usual


def ctx_orders(items, steps):
    return [cube_order(steps, i >= items - 3 * items // 10) for i in range(items)]


def rotated(values, cosine, sine):
    low, high = values[:, : HD // 2], values[:, HD // 2 :]
    return jnp.concatenate([low * cosine - high * sine, high * cosine + low * sine], 1)


def attend_kernel(count, seqs, heads, q, k, v, cosine, sine, start, tok, key_tok, *refs):
    whole, attn, attn_low, sums, queries, send_sem, recv_sem = refs
    me = lax.axis_index("ctx")
    steps = count.bit_length() - 1
    items = 2 * seqs
    orders = [order[::-1] for order in ctx_orders(items, steps)]
    rows = q.shape[1]
    scale = HD ** (-0.5)

    def copy(item, step, mask):
        bit = 1 << orders[item][step]
        block = whole.at[item, flipped(me, mask)]
        return remote(
            "ctx", block, block, (send_sem, recv_sem), (item, mask | bit), flipped(me, bit)
        )

    def masks(item, step):
        return submasks(orders[item][:step])

    def send_own(item):
        for step in range(steps):
            copy(item, step, 0).start()

    for s in range(seqs):
        whole[2 * s, me] = rotated(k[s], cosine[s], sine[s]).astype(BF16)
        whole[2 * s + 1, me] = v[s].astype(BF16)
        if s == 0:
            greet("ctx", count)
        send_own(2 * s)
        send_own(2 * s + 1)
    for s in range(seqs):
        for h in range(heads):
            at = slice(h * HD, (h + 1) * HD)
            queries[s, :, at] = rotated(q[s, :, at], cosine[s], sine[s]).astype(BF16)

    def attend(s):
        keys = whole[2 * s].reshape(count * rows, HD)
        values = whole[2 * s + 1].reshape(count * rows, HD)
        allowed = (key_tok[...] <= tok[...]) & (key_tok[...] >= start[s])
        for h in range(heads):
            at = slice(h * HD, (h + 1) * HD)
            raw = lax.dot_general(
                queries[s, :, at], keys, (((1,), (1,)), ((), ())), preferred_element_type=F32
            )
            exps = jnp.where(allowed, jnp.exp(CAP * jnp.tanh(raw * (scale / CAP))), 0.0)
            total = jnp.sum(exps, axis=-1, keepdims=True)
            out = jnp.dot(exps.astype(BF16), values, preferred_element_type=F32) / total
            sums[s, h] = total
            attn[s, :, at] = out
            attn_low[s, :, at] = out.astype(BF16)

    for got in range(steps):
        for item in range(items):
            for mask in masks(item, got):
                copy(item, got, mask).wait_recv()
                for step in range(got + 1, steps):
                    copy(item, step, mask | 1 << orders[item][got]).start()
            if got == steps - 1 and item % 2 == 1:
                attend(item // 2)
    for step in range(steps):
        for item in range(items):
            for mask in masks(item, step):
                copy(item, step, mask).wait_send()


def attend_all(q, k, v, cosine, sine, start, tok, key_tok, cid):
    count = lax.axis_size("ctx")
    seqs, rows, cols = q.shape
    heads = cols // HD
    dma = pltpu.SemaphoreType.DMA((2 * seqs, count))
    shape = jax.ShapeDtypeStruct
    args = (q, k, v, cosine, sine, start, tok, key_tok)
    outs = [
        shape((2 * seqs, count, rows, HD), BF16),
        shape(q.shape, F32),
        shape(q.shape, BF16),
        shape((seqs, heads, rows, 1), F32),
        shape(q.shape, BF16),
    ]
    return pl.pallas_call(
        functools.partial(attend_kernel, count, seqs, heads),
        out_shape=outs,
        in_specs=[pl.BlockSpec(memory_space=VMEM)] * len(args),
        out_specs=[pl.BlockSpec(memory_space=VMEM)] * len(outs),
        scratch_shapes=[dma, dma],
        compiler_params=pltpu.CompilerParams(
            collective_id=cid, has_side_effects=True, vmem_limit_bytes=56 * MIB
        ),
        cost_estimate=takes(60),
        name="attend",
    )(*args)


def attend_back_kernel(count, seqs, heads, *refs):
    queries, whole, out_grad, attn, sums, cosine, sine, start, tok, key_tok = refs[:10]
    grads, part, landed, sendbuf, query_grad, send_sem, recv_sem = refs[10:]
    me = lax.axis_index("ctx")
    steps = count.bit_length() - 1
    items = 2 * seqs
    orders = ctx_orders(items, steps)
    rows = queries.shape[1]
    scale = HD ** (-0.5)
    greet("ctx", count)

    def copy(item, step, sub):
        order = orders[item]
        bit = 1 << order[step]
        mask = bit | sub
        if step == 0:
            src = part.at[item, flipped(me, mask)]
        else:
            src = sendbuf.at[item, without(mask, order[0])]
        return remote(
            "ctx", src, landed.at[item, mask], (send_sem, recv_sem), (item, mask), flipped(me, bit)
        )

    def total_of(item, mask, upto):
        total = part[item, flipped(me, mask)].astype(F32)
        for step in range(upto):
            total = total + landed[item, 1 << orders[item][step] | mask].astype(F32)
        return total

    def subs(item, step):
        return submasks(orders[item][step + 1 :])

    def backward(s):
        keys = whole[2 * s].reshape(count * rows, HD)
        values = whole[2 * s + 1].reshape(count * rows, HD)
        allowed = (key_tok[...] <= tok[...]) & (key_tok[...] >= start[s])
        key_grad, value_grad = None, None
        for h in range(heads):
            at = slice(h * HD, (h + 1) * HD)
            query, total = queries[s, :, at], sums[s, h]
            raw = lax.dot_general(query, keys, (((1,), (1,)), ((), ())), preferred_element_type=F32)
            tanh = jnp.tanh(raw * (scale / CAP))
            exps = jnp.where(allowed, jnp.exp(CAP * tanh), 0.0)
            og = out_grad[s, :, at]
            low = (og / total).astype(BF16)
            shift = jnp.sum(og * attn[s, :, at], axis=-1, keepdims=True) / total
            toward = lax.dot_general(
                low, values, (((1,), (1,)), ((), ())), preferred_element_type=F32
            )
            score = (exps * (toward - shift) * (scale * (1.0 - tanh * tanh))).astype(BF16)
            grad = jnp.dot(score, keys, preferred_element_type=F32)
            query_grad[s, :, at] = grad
            across = (((0,), (0,)), ((), ()))
            k_term = lax.dot_general(score, query, across, preferred_element_type=F32)
            v_term = lax.dot_general(exps.astype(BF16), low, across, preferred_element_type=F32)
            key_grad = k_term if h == 0 else key_grad + k_term
            value_grad = v_term if h == 0 else value_grad + v_term
        part[2 * s] = key_grad.astype(BF16).reshape(count, rows, HD)
        part[2 * s + 1] = value_grad.astype(BF16).reshape(count, rows, HD)

    def advance(item, got):
        for sub in subs(item, got):
            copy(item, got, sub).wait_recv()
        step = got + 1
        if step == steps:
            s, total = item // 2, total_of(item, 0, steps)
            if item % 2 == 0:
                total = rotated(total, cosine[s], -sine[s])
            lane = heads * HD + (item % 2) * HD
            grads[s, :, lane : lane + HD] = total.astype(BF16)
            return
        for sub in subs(item, step):
            mask = 1 << orders[item][step] | sub
            sendbuf[item, without(mask, orders[item][0])] = total_of(item, mask, step).astype(BF16)
            copy(item, step, sub).start()

    for s in range(seqs):
        backward(s)
        for item in (2 * s, 2 * s + 1):
            for sub in subs(item, 0):
                copy(item, 0, sub).start()
    for s in range(seqs):
        for h in range(heads):
            at = slice(h * HD, (h + 1) * HD)
            grads[s, :, at] = rotated(query_grad[s, :, at], cosine[s], -sine[s]).astype(BF16)
    for item, got in scatter_events(orders):
        advance(item, got)
    for step in range(steps):
        for item in range(items):
            for sub in subs(item, step):
                copy(item, step, sub).wait_send()


def attend_back_some(queries, whole, out_grad, attn, sums, cosine, sine, start, tok, key_tok, cid):
    count = lax.axis_size("ctx")
    seqs, rows, cols = queries.shape
    heads = cols // HD
    dma = pltpu.SemaphoreType.DMA((2 * seqs, count))
    args = (queries, whole, out_grad, attn, sums, cosine, sine, start, tok, key_tok)
    return pl.pallas_call(
        functools.partial(attend_back_kernel, count, seqs, heads),
        out_shape=jax.ShapeDtypeStruct((seqs, rows, cols + 2 * HD), BF16),
        in_specs=[pl.BlockSpec(memory_space=VMEM)] * len(args),
        out_specs=pl.BlockSpec(memory_space=VMEM),
        scratch_shapes=[
            VMEM(whole.shape, BF16),
            VMEM(whole.shape, BF16),
            VMEM((2 * seqs, max(count // 2, 1), rows, HD), BF16),
            VMEM(queries.shape, F32),
            dma,
            dma,
        ],
        compiler_params=pltpu.CompilerParams(
            collective_id=cid, has_side_effects=True, vmem_limit_bytes=56 * MIB
        ),
        cost_estimate=takes(60),
        name="attend_back",
    )(*args)


def attend_back(queries, whole, out_grad, attn, sums, cosine, sine, start, tok, key_tok, cid):
    seqs = queries.shape[0]
    size = max(1, min(seqs, 8 * seqs // whole.shape[1]))
    grads = []
    for i, s in enumerate(range(0, seqs, size)):
        e = min(s + size, seqs)
        some = (queries[s:e], whole[2 * s : 2 * e], out_grad[s:e], attn[s:e], sums[s:e])
        near = (cosine[s:e], sine[s:e], start[s:e], tok, key_tok)
        grads.append(attend_back_some(*some, *near, cid + i))
    return grads[0] if len(grads) == 1 else jnp.concatenate(grads, 0)


def send_ctx(value, mask):
    return lax.ppermute(value, "ctx", [(i, i ^ mask) for i in range(lax.axis_size("ctx"))])


def send_core(value):
    return lax.ppermute(value, "tp", [(i, i ^ 1) for i in range(lax.axis_size("tp"))])


class Halving:
    def __init__(self, part, order, but=None):
        steps = lax.axis_size("ctx").bit_length() - 1
        self.order = list(order)
        self.left = [b for b in range(steps)[::-1] if b != but]
        owners = 1 << len(self.left)
        self.total = part.reshape((2,) * len(self.left) + (part.shape[0] // owners, part.shape[1]))

    def send(self):
        b = self.order.pop(0)
        axis = self.left.index(b)
        self.left.remove(b)
        mine = (lax.axis_index("ctx") >> b) & 1
        pick = functools.partial(lax.dynamic_index_in_dim, axis=axis, keepdims=False)
        self.gots = [send_ctx(pick(self.total, 1 - mine), 1 << b)]
        self.keep = pick(self.total, mine)

    def add(self):
        self.total = (self.keep.astype(F32) + self.gots[0].astype(F32)).astype(BF16)

    def step(self):
        self.add()
        if self.order:
            self.send()
        else:
            del self.gots

    def finish(self):
        if self.order and not hasattr(self, "gots"):
            self.send()
        while hasattr(self, "gots"):
            self.add()
            del self.gots
            if self.order:
                self.send()
        return self.total


class Sent:
    def __init__(self, value, b):
        self.gots = [send_ctx(value, 1 << b)]


class CoreSent(Sent):
    def __init__(self, value):
        self.gots = [send_core(value)]


def pin(value, *sent):
    value, gots = lax.optimization_barrier((value, [s.gots for s in sent]))
    for s, got in zip(sent, gots):
        s.gots = got
    return value


def product_kernel(own, far, near, mine, got, out):
    core = lax.axis_index("tp") % 2
    cols = mine.shape[-1]

    def times(left, right):
        return lax.dot_general(
            left, right.reshape(-1, cols), (((0,), (0,)), ((), ())), preferred_element_type=F32
        )

    total = times(own[...], mine[...])
    total = total + times(far[...], got[:, :, :, core])
    total = total + times(near[...], got[:, :, :, 1 - core])
    out[...] = total.astype(BF16)


def product(own, far, near, mine, got, name):
    rows, width = own.shape
    cols, tile = mine.shape[-1], 256 if width % 256 == 0 else 384
    whole = pl.BlockSpec(mine.shape, lambda i: (0,) * mine.ndim)
    return pl.pallas_call(
        product_kernel,
        grid=(width // tile,),
        out_shape=jax.ShapeDtypeStruct((width, cols), BF16),
        in_specs=[
            pl.BlockSpec((rows, tile), lambda i: (0, i)),
            pl.BlockSpec((rows // 2, tile), lambda i: (0, i)),
            pl.BlockSpec((rows // 2, tile), lambda i: (0, i)),
            whole,
            whole,
        ],
        out_specs=pl.BlockSpec((tile, cols), lambda i: (i, 0)),
        compiler_params=pltpu.CompilerParams(vmem_limit_bytes=40 * MIB),
        cost_estimate=pl.CostEstimate(
            flops=4 * rows * width * cols, bytes_accessed=0, transcendentals=0
        ),
        name=name,
    )(own, far, near, mine, got)


def weights_scatter_kernel(count, tp_count, plan, n_parts, *refs):
    refs = list(refs)
    parts = [refs.pop(0) for _ in range(n_parts)]
    gains = refs.pop(0)
    outs = [refs.pop(0) for _ in range(n_parts)]
    gains_out = refs.pop(0)
    landed = [refs.pop(0) for _ in range(n_parts)]
    sendbuf = [refs.pop(0) for _ in range(n_parts)]
    gains_landed, gains_send = refs.pop(0), refs.pop(0)
    sems = (refs.pop(0), refs.pop(0))
    gain_sems = (refs.pop(0), refs.pop(0))
    me = lax.axis_index("ctx")
    me_tp = lax.axis_index("tp")
    steps = count.bit_length() - 1
    tp_steps = tp_count.bit_length() - 1
    barrier = pltpu.get_barrier_semaphore()
    for b in range(steps):
        pl.semaphore_signal(
            barrier, inc=1, device_id={"ctx": flipped(me, 1 << b)}, device_id_type=MESH
        )
    for b in range(tp_steps):
        pl.semaphore_signal(
            barrier, inc=1, device_id={"tp": flipped(me_tp, 1 << b)}, device_id_type=MESH
        )
    pl.semaphore_wait(barrier, steps + tp_steps)

    def subs(order, step):
        return submasks(order[step + 1 :])

    def copy(n, step, sub):
        p, item, order = plan[n]
        bit = 1 << order[step]
        mask = bit | sub
        if step == 0:
            src = parts[p].at[flipped(me, mask), item]
        else:
            src = sendbuf[p].at[without(mask, order[0]), item]
        return remote(
            "ctx", src, landed[p].at[mask, item], sems, (n, mask), flipped(me, bit)
        )

    def total_of(n, mask, upto):
        p, item, order = plan[n]
        total = parts[p][flipped(me, mask), item].astype(F32)
        for step in range(upto):
            total = total + landed[p][1 << order[step] | mask, item].astype(F32)
        return total

    for n, (_, _, order) in enumerate(plan):
        for sub in subs(order, 0):
            copy(n, 0, sub).start()

    gains_send[0] = gains[...]
    for step in range(tp_steps + steps):
        axis, bit, at = ("tp", step, me_tp) if step < tp_steps else ("ctx", step - tp_steps, me)
        go = remote(
            axis,
            gains_send.at[step],
            gains_landed.at[step],
            gain_sems,
            step,
            flipped(at, 1 << bit),
        )
        go.start()
        go.wait_recv()
        both = gains_send[step] + gains_landed[step]
        if step + 1 < tp_steps + steps:
            gains_send[step + 1] = both
        else:
            gains_out[...] = both
        go.wait_send()

    for n, got in scatter_events([order for _, _, order in plan]):
        p, item, order = plan[n]
        for sub in subs(order, got):
            copy(n, got, sub).wait_recv()
        step = got + 1
        if step == steps:
            outs[p][item] = total_of(n, 0, steps)
            continue
        for sub in subs(order, step):
            mask = 1 << order[step] | sub
            sendbuf[p][without(mask, order[0]), item] = total_of(n, mask, step).astype(BF16)
            copy(n, step, sub).start()
    for step in range(steps):
        for n, (_, _, order) in enumerate(plan):
            for sub in subs(order, step):
                copy(n, step, sub).wait_send()


def weights_scatter(parts, gains, cid):
    count, tp_count = lax.axis_size("ctx"), lax.axis_size("tp")
    steps = count.bit_length() - 1
    rows = parts[0].shape[0] // count
    cut = max(c for c in range(1, 7) if rows % (16 * c) == 0) if rows % 16 == 0 else 1
    blocks = [p.reshape(count, cut, rows // cut, p.shape[1]) for p in parts]
    pairs = [(p, item) for item in range(cut) for p in range(len(parts))]
    orders = ctx_orders(len(pairs), steps)
    plan = [(p, item, order) for (p, item), order in zip(pairs, orders)]
    hops = steps + tp_count.bit_length() - 1
    dma = pltpu.SemaphoreType.DMA((len(plan), count))
    out = pl.pallas_call(
        functools.partial(weights_scatter_kernel, count, tp_count, plan, len(parts)),
        out_shape=[jax.ShapeDtypeStruct(b.shape[1:], F32) for b in blocks]
        + [jax.ShapeDtypeStruct(gains.shape, F32)],
        in_specs=[pl.BlockSpec(memory_space=VMEM)] * (len(parts) + 1),
        out_specs=[pl.BlockSpec(memory_space=VMEM)] * (len(parts) + 1),
        scratch_shapes=[VMEM(b.shape, BF16) for b in blocks]
        + [VMEM((max(count // 2, 1),) + b.shape[1:], BF16) for b in blocks]
        + [VMEM((hops,) + gains.shape, F32)] * 2
        + [dma, dma, pltpu.SemaphoreType.DMA((hops,)), pltpu.SemaphoreType.DMA((hops,))],
        compiler_params=pltpu.CompilerParams(
            collective_id=cid, has_side_effects=True, vmem_limit_bytes=56 * MIB
        ),
        cost_estimate=takes(80),
        name="weights_scatter",
    )(*blocks, gains)
    return [o.reshape(rows, o.shape[-1]) for o in out[:-1]], out[-1]


def inv_rms(v):
    return lax.rsqrt(jnp.mean(v * v, axis=-1, keepdims=True) + EPS)


def rms_back(dy, v, g):
    r = inv_rms(v)
    dg = jnp.sum(dy * v * r, axis=tuple(range(v.ndim - 1)), keepdims=True)
    gdy = g * dy
    dv = r * gdy - v * (r * r * r) * jnp.mean(gdy * v, axis=-1, keepdims=True)
    return dv, dg.reshape(1, -1)


def add_to(ref, item, value):
    ref[...] = value if item == 0 else ref[...] + value


def enter_rows(item, _, ins, outs):
    tokens, gain = ins
    v = tokens[item].astype(F32)
    return v * inv_rms(v) * gain[...].astype(F32)


def mid_rows(item, branch, ins, outs):
    tokens, attn_gain, ffw_gain = ins
    branch_out, resid_out = outs
    branch_out[item] = branch
    resid = tokens[item].astype(F32) + branch * inv_rms(branch) * attn_gain[...].astype(F32)
    resid_out[item] = resid
    return resid * inv_rms(resid) * ffw_gain[...].astype(F32)


def turn_rows(item, branch, ins, outs):
    resid, cotangent, gain = ins
    layer_out, gain_grad = outs
    g = gain[...].astype(F32)
    layer_out[item] = (resid[item] + branch * inv_rms(branch) * g).astype(BF16)
    dv, dg = rms_back(cotangent[item].astype(F32), branch, g)
    add_to(gain_grad, item, dg)
    return dv


def mid_back_rows(item, ffw_grad, ins, outs):
    resid, branch, cotangent, ffw_gain, attn_gain = ins
    resid_grad_out, ffw_gain_grad, attn_gain_grad = outs
    dv, dg = rms_back(ffw_grad, resid[item], ffw_gain[...].astype(F32))
    add_to(ffw_gain_grad, item, dg)
    resid_grad = cotangent[item].astype(F32) + dv
    resid_grad_out[item] = resid_grad
    dv, dg = rms_back(resid_grad, branch[item], attn_gain[...].astype(F32))
    add_to(attn_gain_grad, item, dg)
    return dv


def leave_rows(item, normed_grad, ins, outs):
    tokens, resid_grad, gain = ins
    tokens_grad, gain_grad = outs
    dv, dg = rms_back(normed_grad, tokens[item].astype(F32), gain[...].astype(F32))
    add_to(gain_grad, item, dg)
    tokens_grad[item] = resid_grad[item] + dv


def gelu_times(gate, up_val):
    return jax.nn.gelu(gate, approximate=True) * up_val


def body(
    tokens,
    doc_ids,
    attn_in_gain,
    query_weight,
    key_weight,
    value_weight,
    output_weight,
    attn_out_gain,
    ffw_in_gain,
    gate_weight,
    up_weight,
    down_weight,
    ffw_out_gain,
    cotangent,
):
    stretch_rows, seqs, slots, width = tokens.shape
    ctx_count = lax.axis_size("ctx")
    tp_count = lax.axis_size("tp")
    ctx_rank = lax.axis_index("ctx")
    stretch = stretch_rows * tp_count
    length = 2 * stretch * ctx_count
    rows = stretch * slots
    all_rows = seqs * rows
    local_heads = query_weight.shape[1] // HD
    assert key_weight.shape[1] == value_weight.shape[1] == HD
    own = (seqs, slots, stretch_rows, width)
    steps = ctx_count.bit_length() - 1

    slot_stretch = jnp.stack([ctx_rank, 2 * ctx_count - 1 - ctx_rank])
    iota = jnp.arange(stretch, dtype=jnp.int32)
    query_tok = slot_stretch[:, None] * stretch + iota[None, :]
    row_tok = query_tok.reshape(rows)
    row_doc = jnp.concatenate(
        [lax.dynamic_slice_in_dim(doc_ids, slot_stretch[i] * stretch, stretch, 1) for i in (0, 1)],
        1,
    )
    row_start = jnp.sum(
        (doc_ids[:, None, :] < row_doc[:, :, None]).astype(jnp.int32), axis=-1
    )
    row_pos = row_tok[None] - row_start
    frequency = BASE ** (-jnp.arange(HD // 2).astype(F32) / (HD // 2))
    angles = row_pos.astype(F32)[..., None] * frequency
    cosine, sine = jnp.cos(angles), jnp.sin(angles)
    key_slot = jnp.arange(2 * ctx_count, dtype=jnp.int32)
    key_stretch = jnp.where(key_slot % 2 == 0, key_slot // 2, 2 * ctx_count - 1 - key_slot // 2)
    key_tok = (key_stretch[:, None] * stretch + iota[None, :]).reshape(length)
    where = (row_start[..., None], row_tok[:, None], key_tok[None, :])

    def wide(gain):
        return gain.reshape(1, width)

    mine = jnp.transpose(tokens, (1, 2, 0, 3))
    upstream = jnp.transpose(cotangent, (1, 2, 0, 3))
    f32_rows = jax.ShapeDtypeStruct(own, F32)
    gain_shape = jax.ShapeDtypeStruct((1, width), F32)

    (normed_all,) = tp_exchange("enter", 1, enter_rows, [mine, wide(attn_in_gain)], [])
    normed_all = normed_all.reshape(all_rows, width)
    dot = functools.partial(jnp.dot, preferred_element_type=F32)
    ein = functools.partial(jnp.einsum, preferred_element_type=F32)
    queries = dot(normed_all, query_weight).reshape(seqs, rows, local_heads * HD)
    keys = dot(normed_all, key_weight).reshape(seqs, rows, HD)
    values = dot(normed_all, value_weight).reshape(seqs, rows, HD)
    kv_all, attn, attn_low, sums, queries = attend_all(
        queries, keys, values, cosine, sine, *where, 2
    )
    attn_rows = attn_low.reshape(all_rows, local_heads * HD)
    part = dot(attn_rows, output_weight).astype(BF16)

    def by_owner(value):
        return value.reshape(seqs, slots, tp_count, stretch_rows, width)

    ffw_all, branch, resid = tp_exchange(
        "middle",
        3,
        mid_rows,
        [mine, wide(attn_out_gain), wide(ffw_in_gain)],
        [f32_rows, f32_rows],
        by_owner(part),
    )
    ffw_all = ffw_all.reshape(all_rows, width)
    low_bit, next_bit, far_bit = 0, min(1, steps - 1), steps - 1
    high = list(range(2, steps))
    core = lax.axis_index("tp") % 2
    pick = functools.partial(lax.dynamic_index_in_dim, keepdims=False)

    def by_core(value):
        return value.reshape((seqs, slots, tp_count // 2, 2, stretch_rows, value.shape[-1]))

    def core_rows(value):
        return pick(by_core(value), core, 3).reshape(all_rows // 2, value.shape[-1])

    def halves(value, b):
        bit = (ctx_rank >> b) & 1
        cut = value.shape[1] // 2
        return [
            by_core(lax.dynamic_slice_in_dim(value, at * cut, cut, 1)) for at in (bit, 1 - bit)
        ]

    def owner_cols(value):
        bit = (ctx_rank >> far_bit) & 1
        cut = value.shape[1] // 2
        return [lax.dynamic_slice_in_dim(value, at * cut, cut, 1) for at in (bit, 1 - bit)]

    def owner_pieces(total, b):
        bit = (ctx_rank >> b) & 1
        cut = total.reshape(2, -1, total.shape[-1])
        return pick(cut, bit, 0), pick(cut, 1 - bit, 0)

    def whole_cols(own_half, got_half, b):
        bit = (ctx_rank >> b) & 1
        first = jnp.where(bit == 0, own_half, got_half)
        second = jnp.where(bit == 0, got_half, own_half)
        return jnp.concatenate([first, second], 1).astype(F32)

    ffw_send = core_rows(ffw_all)
    ffw_all, ffw_send = lax.optimization_barrier((ffw_all, ffw_send))
    ffw_far, ffw_far_low = Sent(ffw_send, next_bit), Sent(ffw_send, low_bit)
    gate = dot(ffw_all, gate_weight)
    up = dot(ffw_all, up_weight)
    mixed, mixed_back = jax.vjp(gelu_times, gate, up)
    mixed = mixed.astype(BF16)
    mixed_sent = Sent(by_core(mixed), far_bit)
    part = dot(mixed, down_weight).astype(BF16)
    part = pin(part, ffw_far, ffw_far_low)
    ffw_near, ffw_near_low = CoreSent(ffw_far.gots[0]), CoreSent(ffw_far_low.gots[0])
    ffw_grad_all, layer_out, ffw_out_gain_part = tp_exchange(
        "turn",
        4,
        turn_rows,
        [resid, upstream, wide(ffw_out_gain)],
        [jax.ShapeDtypeStruct(own, BF16), gain_shape],
        by_owner(part),
    )
    ffw_grad_all = ffw_grad_all.reshape(all_rows, width)
    grad_half, grad_give = owner_cols(ffw_grad_all)
    grad_send = core_rows(grad_give)
    ffw_grad_all, grad_send = lax.optimization_barrier((ffw_grad_all, grad_send))
    grad_far = Sent(grad_send, far_bit)
    mixed_grad = ein("rd,fd->rf", ffw_grad_all, down_weight)
    gate_grad, up_grad = mixed_back(mixed_grad)
    gate_grad = gate_grad.astype(BF16)
    up_grad = up_grad.astype(BF16)
    gate_half, gate_give = halves(gate_grad, low_bit)
    up_half, up_give = halves(up_grad, next_bit)
    gate_grad, up_grad, gate_give, up_give = lax.optimization_barrier(
        (gate_grad, up_grad, gate_give, up_give)
    )
    gate_sent, up_sent = Sent(gate_give, low_bit), Sent(up_give, next_bit)
    part = (
        ein("rf,df->rd", gate_grad, gate_weight) + ein("rf,df->rd", up_grad, up_weight)
    ).astype(BF16)
    part = pin(part, gate_sent, ffw_near, ffw_near_low)
    gate_part = product(
        ffw_all, ffw_far_low.gots[0], ffw_near_low.gots[0], gate_half, gate_sent.gots[0], "gate_product"
    )
    gates = Halving(gate_part, [next_bit] + high)
    gates.send()
    part, gate_part = lax.optimization_barrier((part, gate_part))
    part = pin(part, up_sent)
    up_part = product(
        ffw_all, ffw_far.gots[0], ffw_near.gots[0], up_half, up_sent.gots[0], "up_product"
    )
    ups = Halving(up_part, [low_bit] + high)
    ups.send()
    part, up_part = lax.optimization_barrier((part, up_part))
    part = pin(part, grad_far, mixed_sent)
    grad_near = CoreSent(grad_far.gots[0])
    down_part = product(
        grad_half,
        grad_far.gots[0],
        grad_near.gots[0],
        by_core(mixed),
        mixed_sent.gots[0],
        "down_product",
    )
    down = Halving(down_part, [b for b in range(steps) if b != far_bit], far_bit)
    down.send()
    part, down_part = lax.optimization_barrier((part, down_part))
    branch_grad_all, resid_grad, ffw_in_gain_part, attn_out_gain_part = tp_exchange(
        "middle_back",
        5,
        mid_back_rows,
        [resid, branch, upstream, wide(ffw_in_gain), wide(attn_out_gain)],
        [f32_rows, gain_shape, gain_shape],
        by_owner(part),
    )
    branch_grad_all = branch_grad_all.reshape(all_rows, width)
    output_part = ein("rd,rh->dh", branch_grad_all, attn_rows).astype(BF16)
    attn_grad = ein("rd,hd->rh", branch_grad_all, output_weight).reshape(attn.shape)
    attn_grad = pin(attn_grad, gates)
    gates.step()
    qkv_grad = attend_back(queries, kv_all, attn_grad, attn, sums, cosine, sine, *where, 16)
    qkv_grad = pin(qkv_grad, down, ups).reshape(all_rows, -1)
    ups.step()
    down.step()
    qkv_weight = jnp.concatenate([query_weight, key_weight, value_weight], 1)
    part = ein("rh,dh->rd", qkv_grad, qkv_weight).astype(BF16)
    qkv_part = ein("rd,rh->dh", normed_all, qkv_grad).astype(BF16)
    tokens_grad, attn_in_gain_part = tp_exchange(
        "leave",
        7,
        leave_rows,
        [mine, resid_grad, wide(attn_in_gain)],
        [f32_rows, gain_shape],
        by_owner(part),
        gather=False,
    )
    gains = jnp.concatenate(
        [attn_in_gain_part, attn_out_gain_part, ffw_in_gain_part, ffw_out_gain_part], 0
    )
    (output_sum, qkv_sum), gains = weights_scatter([output_part, qkv_part], gains, 8)
    gains = pin(gains, gates, ups, down)
    gate_own, gate_give = owner_pieces(gates.finish(), low_bit)
    gate_sent = Sent(gate_give, low_bit)
    up_own, up_give = owner_pieces(ups.finish(), next_bit)
    up_sent = Sent(up_give, next_bit)
    down_sum = down.finish().astype(F32)
    gate_sum = whole_cols(gate_own, gate_sent.gots[0], low_bit)
    up_sum = whole_cols(up_own, up_sent.gots[0], next_bit)
    share = width // ctx_count
    gains = lax.dynamic_slice_in_dim(gains, ctx_rank * share, share, 1)
    heads_end = local_heads * HD
    keys_end = heads_end + HD
    return (
        jnp.transpose(layer_out, (2, 0, 1, 3)),
        jnp.transpose(tokens_grad, (2, 0, 1, 3)),
        gains[0],
        qkv_sum[:, :heads_end],
        qkv_sum[:, heads_end:keys_end],
        qkv_sum[:, keys_end:],
        output_sum.T,
        gains[1],
        gains[2],
        gate_sum,
        up_sum,
        down_sum.T,
        gains[3],
    )


def solution(mesh):
    placed = (
        P("tp", None, "ctx", None),
        P(),
        P(),
        P(None, "tp"),
        P(None, "tp"),
        P(None, "tp"),
        P("tp", None),
        P(),
        P(),
        P(None, "tp"),
        P(None, "tp"),
        P("tp", None),
        P(),
        P("tp", None, "ctx", None),
    )
    return jax.shard_map(
        body,
        mesh=mesh,
        in_specs=placed,
        out_specs=(
            P("tp", None, "ctx", None),
            P("tp", None, "ctx", None),
            P("ctx"),
            P("ctx", "tp"),
            P("ctx", "tp"),
            P("ctx", "tp"),
            P("tp", "ctx"),
            P("ctx"),
            P("ctx"),
            P("ctx", "tp"),
            P("ctx", "tp"),
            P("tp", "ctx"),
            P("ctx"),
        ),
        check_vma=False,
    )
```

```python
import functools

import jax
import jax.numpy as jnp
from jax import lax
from jax.experimental import pallas as pl
from jax.experimental.pallas import tpu as pltpu
from jax.sharding import PartitionSpec as P

HD = 256
EPS = 1e-06
CAP = 50.0
BASE = 10000.0
MIB = 1 << 20
TILE = 768
BACK_TILE = 384
F32 = jnp.float32
BF16 = jnp.bfloat16
VMEM = pltpu.VMEM
MESH = pl.DeviceIdType.MESH


def bits_of(mask):
    return [b for b in range(mask.bit_length()) if mask >> b & 1]


def flipped(index, mask):
    for b in bits_of(mask):
        index = index + (1 - 2 * ((index // (1 << b)) % 2)) * (1 << b)
    return index


def without(mask, bit):
    return (mask >> bit + 1 << bit) | (mask & (1 << bit) - 1)


def submasks(bits):
    masks = [0]
    for b in bits:
        masks = masks + [m | 1 << b for m in masks]
    return masks


def scatter_events(orders):
    steps = len(orders[0])
    usual = [i for i, order in enumerate(orders) if order[0] == 0]
    other = [i for i, order in enumerate(orders) if order[0] != 0]
    events = []
    for t in range(len(usual) + steps - 1):
        events += [(usual[t - s], s) for s in range(steps) if 0 <= t - s < len(usual)]
        if 1 <= t <= len(other):
            events.append((other[t - 1], 0))
    events += [(i, 0) for i in other[max(0, len(usual) + steps - 2) :]]
    for t in range(len(other) + steps - 2):
        events += [(other[t - s + 1], s) for s in range(1, steps) if 0 <= t - s + 1 < len(other)]
    return events


def greet(axis, count):
    me = lax.axis_index(axis)
    barrier = pltpu.get_barrier_semaphore()
    steps = count.bit_length() - 1
    for b in range(steps):
        pl.semaphore_signal(
            barrier, inc=1, device_id={axis: flipped(me, 1 << b)}, device_id_type=MESH
        )
    pl.semaphore_wait(barrier, steps)


def remote(axis, src, dst, sems, at, partner):
    return pltpu.make_async_remote_copy(
        src_ref=src,
        dst_ref=dst,
        send_sem=sems[0].at[at],
        recv_sem=sems[1].at[at],
        device_id={axis: partner},
        device_id_type=MESH,
    )


def tp_kernel(fn, count, items, n_in, n_out, scatter, gather, *refs):
    refs = list(refs)
    part = refs.pop(0) if scatter else None
    ins = [refs.pop(0) for _ in range(n_in)]
    whole = refs.pop(0) if gather else None
    outs = [refs.pop(0) for _ in range(n_out)]
    if scatter:
        landed, sendbuf = refs.pop(0), refs.pop(0)
        rs_sems = (refs.pop(0), refs.pop(0))
    if gather:
        ag_sems = (refs.pop(0), refs.pop(0))
    me = lax.axis_index("tp")
    steps = count.bit_length() - 1
    order = list(range(steps))
    greet("tp", count)

    def rs_copy(item, step, sub):
        bit = 1 << order[step]
        mask = bit | sub
        src = part.at[item, :, flipped(me, mask)] if step == 0 else sendbuf.at[item, mask]
        return remote("tp", src, landed.at[item, mask], rs_sems, (item, mask), flipped(me, bit))

    def rs_sum(item, mask, upto):
        total = part[item, :, flipped(me, mask)].astype(F32)
        for step in range(upto):
            total = total + landed[item, 1 << order[step] | mask].astype(F32)
        return total

    def rs_subs(step):
        return submasks(order[step + 1 :])

    def ag_copy(item, step, mask):
        bit = 1 << order[steps - 1 - step]
        block = whole.at[item, :, flipped(me, mask)]
        return remote("tp", block, block, ag_sems, (item, mask | bit), flipped(me, bit))

    def ag_masks(step):
        return submasks([order[steps - 1 - s] for s in range(step)])

    if scatter:
        for item in range(items):
            for sub in rs_subs(0):
                rs_copy(item, 0, sub).start()
        for step in range(1, steps):
            for item in range(items):
                for sub in rs_subs(step - 1):
                    rs_copy(item, step - 1, sub).wait_recv()
                for sub in rs_subs(step):
                    mask = 1 << order[step] | sub
                    sendbuf[item, mask] = rs_sum(item, mask, step).astype(BF16)
                    rs_copy(item, step, sub).start()
    for item in range(items):
        total = None
        if scatter:
            for sub in rs_subs(steps - 1):
                rs_copy(item, steps - 1, sub).wait_recv()
            total = rs_sum(item, 0, steps)
        sent = fn(item, total, ins, outs)
        if gather:
            whole[item, :, me] = sent.astype(BF16)
            for step in range(steps):
                ag_copy(item, step, 0).start()
    if gather:
        for got in range(steps):
            for item in range(items):
                for mask in ag_masks(got):
                    ag_copy(item, got, mask).wait_recv()
                    for step in range(got + 1, steps):
                        ag_copy(item, step, mask | 1 << order[steps - 1 - got]).start()
        for step in range(steps):
            for item in range(items):
                for mask in ag_masks(step):
                    ag_copy(item, step, mask).wait_send()
    if scatter:
        for step in range(steps):
            for item in range(items):
                for sub in rs_subs(step):
                    rs_copy(item, step, sub).wait_send()


def takes(us):
    return pl.CostEstimate(flops=int(us * 1e7), bytes_accessed=0, transcendentals=0)


def tp_exchange(name, cid, fn, ins, outs, part=None, gather=True):
    count = lax.axis_size("tp")
    rows_shape = ins[0].shape
    items, slots, rows, width = rows_shape
    scatter = part is not None
    out_shape = list(outs)
    if gather:
        out_shape = [jax.ShapeDtypeStruct((items, slots, count, rows, width), BF16)] + out_shape
    scratch = []
    dma = pltpu.SemaphoreType.DMA((items, count))
    if scatter:
        scratch += [VMEM((items, count, slots, rows, width), BF16)] * 2 + [dma, dma]
    if gather:
        scratch += [dma, dma]
    args = ([part] if scatter else []) + list(ins)
    return pl.pallas_call(
        functools.partial(
            tp_kernel, fn, count, items, len(ins), len(outs), scatter, gather
        ),
        out_shape=out_shape,
        in_specs=[pl.BlockSpec(memory_space=VMEM)] * len(args),
        out_specs=[pl.BlockSpec(memory_space=VMEM)] * len(out_shape),
        scratch_shapes=scratch,
        compiler_params=pltpu.CompilerParams(
            collective_id=cid, has_side_effects=True, vmem_limit_bytes=40 * MIB
        ),
        cost_estimate=takes(18 * (scatter + gather)),
        name=name,
    )(*args)


def cube_order(steps, turned):
    usual = list(range(steps))
    return [1, 0] + usual[2:] if turned and steps > 1 else usual


def ctx_orders(items, steps):
    return [cube_order(steps, i >= items - 3 * items // 10) for i in range(items)]


def rotated(values, cosine, sine):
    low, high = values[:, : HD // 2], values[:, HD // 2 :]
    return jnp.concatenate([low * cosine - high * sine, high * cosine + low * sine], 1)


def attend_kernel(count, seqs, heads, q, k, v, cosine, sine, start, tok, key_tok, *refs):
    whole, attn, attn_low, sums, queries, send_sem, recv_sem = refs
    me = lax.axis_index("ctx")
    steps = count.bit_length() - 1
    items = 2 * seqs
    orders = [order[::-1] for order in ctx_orders(items, steps)]
    rows = q.shape[1]
    scale = HD ** (-0.5)

    def copy(item, step, mask):
        bit = 1 << orders[item][step]
        block = whole.at[item, flipped(me, mask)]
        return remote(
            "ctx", block, block, (send_sem, recv_sem), (item, mask | bit), flipped(me, bit)
        )

    def masks(item, step):
        return submasks(orders[item][:step])

    def send_own(item):
        for step in range(steps):
            copy(item, step, 0).start()

    for s in range(seqs):
        whole[2 * s, me] = rotated(k[s], cosine[s], sine[s]).astype(BF16)
        whole[2 * s + 1, me] = v[s].astype(BF16)
        if s == 0:
            greet("ctx", count)
        send_own(2 * s)
        send_own(2 * s + 1)
    for s in range(seqs):
        for h in range(heads):
            at = slice(h * HD, (h + 1) * HD)
            queries[s, :, at] = rotated(q[s, :, at], cosine[s], sine[s]).astype(BF16)

    def attend(s):
        keys = whole[2 * s].reshape(count * rows, HD)
        values = whole[2 * s + 1].reshape(count * rows, HD)
        allowed = (key_tok[...] <= tok[...]) & (key_tok[...] >= start[s])
        for h in range(heads):
            at = slice(h * HD, (h + 1) * HD)
            raw = lax.dot_general(
                queries[s, :, at], keys, (((1,), (1,)), ((), ())), preferred_element_type=F32
            )
            exps = jnp.where(allowed, jnp.exp(CAP * jnp.tanh(raw * (scale / CAP))), 0.0)
            total = jnp.sum(exps, axis=-1, keepdims=True)
            out = jnp.dot(exps.astype(BF16), values, preferred_element_type=F32) / total
            sums[s, h] = total
            attn[s, :, at] = out
            attn_low[s, :, at] = out.astype(BF16)

    for got in range(steps):
        for item in range(items):
            for mask in masks(item, got):
                copy(item, got, mask).wait_recv()
                for step in range(got + 1, steps):
                    copy(item, step, mask | 1 << orders[item][got]).start()
            if got == steps - 1 and item % 2 == 1:
                attend(item // 2)
    for step in range(steps):
        for item in range(items):
            for mask in masks(item, step):
                copy(item, step, mask).wait_send()


def attend_all(q, k, v, cosine, sine, start, tok, key_tok, cid):
    count = lax.axis_size("ctx")
    seqs, rows, cols = q.shape
    heads = cols // HD
    dma = pltpu.SemaphoreType.DMA((2 * seqs, count))
    shape = jax.ShapeDtypeStruct
    args = (q, k, v, cosine, sine, start, tok, key_tok)
    outs = [
        shape((2 * seqs, count, rows, HD), BF16),
        shape(q.shape, F32),
        shape(q.shape, BF16),
        shape((seqs, heads, rows, 1), F32),
        shape(q.shape, BF16),
    ]
    return pl.pallas_call(
        functools.partial(attend_kernel, count, seqs, heads),
        out_shape=outs,
        in_specs=[pl.BlockSpec(memory_space=VMEM)] * len(args),
        out_specs=[pl.BlockSpec(memory_space=VMEM)] * len(outs),
        scratch_shapes=[dma, dma],
        compiler_params=pltpu.CompilerParams(
            collective_id=cid, has_side_effects=True, vmem_limit_bytes=56 * MIB
        ),
        cost_estimate=takes(60),
        name="attend",
    )(*args)


def attend_back_kernel(count, seqs, heads, *refs):
    queries, whole, out_grad, attn, sums, cosine, sine, start, tok, key_tok = refs[:10]
    grads, part, landed, sendbuf, query_grad, send_sem, recv_sem = refs[10:]
    me = lax.axis_index("ctx")
    steps = count.bit_length() - 1
    items = 2 * seqs
    orders = ctx_orders(items, steps)
    rows = queries.shape[1]
    scale = HD ** (-0.5)
    greet("ctx", count)

    def copy(item, step, sub):
        order = orders[item]
        bit = 1 << order[step]
        mask = bit | sub
        if step == 0:
            src = part.at[item, flipped(me, mask)]
        else:
            src = sendbuf.at[item, without(mask, order[0])]
        return remote(
            "ctx", src, landed.at[item, mask], (send_sem, recv_sem), (item, mask), flipped(me, bit)
        )

    def total_of(item, mask, upto):
        total = part[item, flipped(me, mask)].astype(F32)
        for step in range(upto):
            total = total + landed[item, 1 << orders[item][step] | mask].astype(F32)
        return total

    def subs(item, step):
        return submasks(orders[item][step + 1 :])

    def backward(s):
        keys = whole[2 * s].reshape(count * rows, HD)
        values = whole[2 * s + 1].reshape(count * rows, HD)
        allowed = (key_tok[...] <= tok[...]) & (key_tok[...] >= start[s])
        key_grad, value_grad = None, None
        for h in range(heads):
            at = slice(h * HD, (h + 1) * HD)
            query, total = queries[s, :, at], sums[s, h]
            raw = lax.dot_general(query, keys, (((1,), (1,)), ((), ())), preferred_element_type=F32)
            tanh = jnp.tanh(raw * (scale / CAP))
            exps = jnp.where(allowed, jnp.exp(CAP * tanh), 0.0)
            og = out_grad[s, :, at]
            low = (og / total).astype(BF16)
            shift = jnp.sum(og * attn[s, :, at], axis=-1, keepdims=True) / total
            toward = lax.dot_general(
                low, values, (((1,), (1,)), ((), ())), preferred_element_type=F32
            )
            score = (exps * (toward - shift) * (scale * (1.0 - tanh * tanh))).astype(BF16)
            grad = jnp.dot(score, keys, preferred_element_type=F32)
            query_grad[s, :, at] = grad
            across = (((0,), (0,)), ((), ()))
            k_term = lax.dot_general(score, query, across, preferred_element_type=F32)
            v_term = lax.dot_general(exps.astype(BF16), low, across, preferred_element_type=F32)
            key_grad = k_term if h == 0 else key_grad + k_term
            value_grad = v_term if h == 0 else value_grad + v_term
        part[2 * s] = key_grad.astype(BF16).reshape(count, rows, HD)
        part[2 * s + 1] = value_grad.astype(BF16).reshape(count, rows, HD)

    def advance(item, got):
        for sub in subs(item, got):
            copy(item, got, sub).wait_recv()
        step = got + 1
        if step == steps:
            s, total = item // 2, total_of(item, 0, steps)
            if item % 2 == 0:
                total = rotated(total, cosine[s], -sine[s])
            lane = heads * HD + (item % 2) * HD
            grads[s, :, lane : lane + HD] = total.astype(BF16)
            return
        for sub in subs(item, step):
            mask = 1 << orders[item][step] | sub
            sendbuf[item, without(mask, orders[item][0])] = total_of(item, mask, step).astype(BF16)
            copy(item, step, sub).start()

    for s in range(seqs):
        backward(s)
        for item in (2 * s, 2 * s + 1):
            for sub in subs(item, 0):
                copy(item, 0, sub).start()
    for s in range(seqs):
        for h in range(heads):
            at = slice(h * HD, (h + 1) * HD)
            grads[s, :, at] = rotated(query_grad[s, :, at], cosine[s], -sine[s]).astype(BF16)
    for item, got in scatter_events(orders):
        advance(item, got)
    for step in range(steps):
        for item in range(items):
            for sub in subs(item, step):
                copy(item, step, sub).wait_send()


def attend_back_some(queries, whole, out_grad, attn, sums, cosine, sine, start, tok, key_tok, cid):
    count = lax.axis_size("ctx")
    seqs, rows, cols = queries.shape
    heads = cols // HD
    dma = pltpu.SemaphoreType.DMA((2 * seqs, count))
    args = (queries, whole, out_grad, attn, sums, cosine, sine, start, tok, key_tok)
    return pl.pallas_call(
        functools.partial(attend_back_kernel, count, seqs, heads),
        out_shape=jax.ShapeDtypeStruct((seqs, rows, cols + 2 * HD), BF16),
        in_specs=[pl.BlockSpec(memory_space=VMEM)] * len(args),
        out_specs=pl.BlockSpec(memory_space=VMEM),
        scratch_shapes=[
            VMEM(whole.shape, BF16),
            VMEM(whole.shape, BF16),
            VMEM((2 * seqs, max(count // 2, 1), rows, HD), BF16),
            VMEM(queries.shape, F32),
            dma,
            dma,
        ],
        compiler_params=pltpu.CompilerParams(
            collective_id=cid, has_side_effects=True, vmem_limit_bytes=56 * MIB
        ),
        cost_estimate=takes(60),
        name="attend_back",
    )(*args)


def attend_back(queries, whole, out_grad, attn, sums, cosine, sine, start, tok, key_tok, cid):
    seqs = queries.shape[0]
    size = max(1, min(seqs, 8 * seqs // whole.shape[1]))
    grads = []
    for i, s in enumerate(range(0, seqs, size)):
        e = min(s + size, seqs)
        some = (queries[s:e], whole[2 * s : 2 * e], out_grad[s:e], attn[s:e], sums[s:e])
        near = (cosine[s:e], sine[s:e], start[s:e], tok, key_tok)
        grads.append(attend_back_some(*some, *near, cid + i))
    return grads[0] if len(grads) == 1 else jnp.concatenate(grads, 0)


def send_ctx(value, mask):
    return lax.ppermute(value, "ctx", [(i, i ^ mask) for i in range(lax.axis_size("ctx"))])


def send_core(value):
    return lax.ppermute(value, "tp", [(i, i ^ 1) for i in range(lax.axis_size("tp"))])


class Halving:
    def __init__(self, part, order, but=None):
        steps = lax.axis_size("ctx").bit_length() - 1
        self.order = list(order)
        self.left = [b for b in range(steps)[::-1] if b != but]
        owners = 1 << len(self.left)
        self.total = part.reshape((2,) * len(self.left) + (part.shape[0] // owners, part.shape[1]))

    def send(self):
        b = self.order.pop(0)
        axis = self.left.index(b)
        self.left.remove(b)
        mine = (lax.axis_index("ctx") >> b) & 1
        pick = functools.partial(lax.dynamic_index_in_dim, axis=axis, keepdims=False)
        self.gots = [send_ctx(pick(self.total, 1 - mine), 1 << b)]
        self.keep = pick(self.total, mine)

    def add(self):
        self.total = (self.keep.astype(F32) + self.gots[0].astype(F32)).astype(BF16)

    def step(self):
        self.add()
        if self.order:
            self.send()
        else:
            del self.gots

    def finish(self):
        if self.order and not hasattr(self, "gots"):
            self.send()
        while hasattr(self, "gots"):
            self.add()
            del self.gots
            if self.order:
                self.send()
        return self.total


class Sent:
    def __init__(self, value, b):
        self.gots = [send_ctx(value, 1 << b)]


class CoreSent(Sent):
    def __init__(self, value):
        self.gots = [send_core(value)]


def pin(value, *sent):
    value, gots = lax.optimization_barrier((value, [s.gots for s in sent]))
    for s, got in zip(sent, gots):
        s.gots = got
    return value


def product_kernel(own, far, near, mine, got, out):
    core = lax.axis_index("tp") % 2
    cols = mine.shape[-1]

    def times(left, right):
        return lax.dot_general(
            left, right.reshape(-1, cols), (((0,), (0,)), ((), ())), preferred_element_type=F32
        )

    total = times(own[...], mine[...])
    total = total + times(far[...], got[:, :, :, core])
    total = total + times(near[...], got[:, :, :, 1 - core])
    out[...] = total.astype(BF16)


def product(own, far, near, mine, got, name):
    rows, width = own.shape
    cols, tile = mine.shape[-1], 256 if width % 256 == 0 else 384
    whole = pl.BlockSpec(mine.shape, lambda i: (0,) * mine.ndim)
    return pl.pallas_call(
        product_kernel,
        grid=(width // tile,),
        out_shape=jax.ShapeDtypeStruct((width, cols), BF16),
        in_specs=[
            pl.BlockSpec((rows, tile), lambda i: (0, i)),
            pl.BlockSpec((rows // 2, tile), lambda i: (0, i)),
            pl.BlockSpec((rows // 2, tile), lambda i: (0, i)),
            whole,
            whole,
        ],
        out_specs=pl.BlockSpec((tile, cols), lambda i: (i, 0)),
        compiler_params=pltpu.CompilerParams(vmem_limit_bytes=40 * MIB),
        cost_estimate=takes(1),
        name=name,
    )(own, far, near, mine, got)


def weights_scatter_kernel(count, tp_count, plan, n_parts, *refs):
    refs = list(refs)
    parts = [refs.pop(0) for _ in range(n_parts)]
    gains = refs.pop(0)
    outs = [refs.pop(0) for _ in range(n_parts)]
    gains_out = refs.pop(0)
    landed = [refs.pop(0) for _ in range(n_parts)]
    sendbuf = [refs.pop(0) for _ in range(n_parts)]
    gains_landed, gains_send = refs.pop(0), refs.pop(0)
    sems = (refs.pop(0), refs.pop(0))
    gain_sems = (refs.pop(0), refs.pop(0))
    me = lax.axis_index("ctx")
    me_tp = lax.axis_index("tp")
    steps = count.bit_length() - 1
    tp_steps = tp_count.bit_length() - 1
    barrier = pltpu.get_barrier_semaphore()
    for b in range(steps):
        pl.semaphore_signal(
            barrier, inc=1, device_id={"ctx": flipped(me, 1 << b)}, device_id_type=MESH
        )
    for b in range(tp_steps):
        pl.semaphore_signal(
            barrier, inc=1, device_id={"tp": flipped(me_tp, 1 << b)}, device_id_type=MESH
        )
    pl.semaphore_wait(barrier, steps + tp_steps)

    def subs(order, step):
        return submasks(order[step + 1 :])

    def copy(n, step, sub):
        p, item, order = plan[n]
        bit = 1 << order[step]
        mask = bit | sub
        if step == 0:
            src = parts[p].at[flipped(me, mask), item]
        else:
            src = sendbuf[p].at[without(mask, order[0]), item]
        return remote(
            "ctx", src, landed[p].at[mask, item], sems, (n, mask), flipped(me, bit)
        )

    def total_of(n, mask, upto):
        p, item, order = plan[n]
        total = parts[p][flipped(me, mask), item].astype(F32)
        for step in range(upto):
            total = total + landed[p][1 << order[step] | mask, item].astype(F32)
        return total

    for n, (_, _, order) in enumerate(plan):
        for sub in subs(order, 0):
            copy(n, 0, sub).start()

    hops = tp_steps + steps
    gains_send[0] = gains[...]

    def hop(step):
        axis, bit, at = ("tp", step, me_tp) if step < tp_steps else ("ctx", step - tp_steps, me)
        return remote(
            axis,
            gains_send.at[step],
            gains_landed.at[step],
            gain_sems,
            step,
            flipped(at, 1 << bit),
        )

    def end_hop(step):
        hop(step).wait_recv()
        both = gains_send[step] + gains_landed[step]
        if step + 1 < hops:
            gains_send[step + 1] = both
            hop(step + 1).start()
        else:
            gains_out[...] = both

    hop(0).start()
    for step in range(tp_steps):
        end_hop(step)
    orders = [order for _, _, order in plan]
    events = scatter_events(orders)
    first_done = max(k for k, (n, step) in enumerate(events) if step == 0)

    for k, (n, got) in enumerate(events):
        p, item, order = plan[n]
        for sub in subs(order, got):
            copy(n, got, sub).wait_recv()
        step = got + 1
        if step == steps:
            outs[p][item] = total_of(n, 0, steps)
        else:
            for sub in subs(order, step):
                mask = 1 << order[step] | sub
                sendbuf[p][without(mask, order[0]), item] = total_of(n, mask, step).astype(BF16)
                copy(n, step, sub).start()
        if k == first_done:
            end_hop(tp_steps)
    for step in range(tp_steps + 1, hops):
        end_hop(step)
    for step in range(hops):
        hop(step).wait_send()
    for step in range(steps):
        for n, (_, _, order) in enumerate(plan):
            for sub in subs(order, step):
                copy(n, step, sub).wait_send()


def weights_scatter(parts, gains, cid):
    count, tp_count = lax.axis_size("ctx"), lax.axis_size("tp")
    steps = count.bit_length() - 1
    rows = parts[0].shape[0] // count
    cut = max(c for c in range(1, 7) if rows % (16 * c) == 0) if rows % 16 == 0 else 1
    blocks = [p.reshape(count, cut, rows // cut, p.shape[1]) for p in parts]
    pairs = [(p, item) for item in range(cut) for p in range(len(parts))]
    orders = ctx_orders(len(pairs), steps)
    plan = [(p, item, order) for (p, item), order in zip(pairs, orders)]
    hops = steps + tp_count.bit_length() - 1
    dma = pltpu.SemaphoreType.DMA((len(plan), count))
    out = pl.pallas_call(
        functools.partial(weights_scatter_kernel, count, tp_count, plan, len(parts)),
        out_shape=[jax.ShapeDtypeStruct(b.shape[1:], F32) for b in blocks]
        + [jax.ShapeDtypeStruct(gains.shape, F32)],
        in_specs=[pl.BlockSpec(memory_space=VMEM)] * (len(parts) + 1),
        out_specs=[pl.BlockSpec(memory_space=VMEM)] * (len(parts) + 1),
        scratch_shapes=[VMEM(b.shape, BF16) for b in blocks]
        + [VMEM((max(count // 2, 1),) + b.shape[1:], BF16) for b in blocks]
        + [VMEM((hops,) + gains.shape, F32)] * 2
        + [dma, dma, pltpu.SemaphoreType.DMA((hops,)), pltpu.SemaphoreType.DMA((hops,))],
        compiler_params=pltpu.CompilerParams(
            collective_id=cid, has_side_effects=True, vmem_limit_bytes=56 * MIB
        ),
        cost_estimate=takes(80),
        name="weights_scatter",
    )(*blocks, gains)
    return [o.reshape(rows, o.shape[-1]) for o in out[:-1]], out[-1]


def inv_rms(v):
    return lax.rsqrt(jnp.mean(v * v, axis=-1, keepdims=True) + EPS)


def rms_back(dy, v, g):
    r = inv_rms(v)
    dg = jnp.sum(dy * v * r, axis=tuple(range(v.ndim - 1)), keepdims=True)
    gdy = g * dy
    dv = r * gdy - v * (r * r * r) * jnp.mean(gdy * v, axis=-1, keepdims=True)
    return dv, dg.reshape(1, -1)


def add_to(ref, item, value):
    ref[...] = value if item == 0 else ref[...] + value


def enter_rows(item, _, ins, outs):
    tokens, gain = ins
    v = tokens[item].astype(F32)
    return v * inv_rms(v) * gain[...].astype(F32)


def mid_rows(item, branch, ins, outs):
    tokens, attn_gain, ffw_gain = ins
    branch_out, resid_out = outs
    branch_out[item] = branch
    resid = tokens[item].astype(F32) + branch * inv_rms(branch) * attn_gain[...].astype(F32)
    resid_out[item] = resid
    return resid * inv_rms(resid) * ffw_gain[...].astype(F32)


def turn_rows(item, branch, ins, outs):
    resid, cotangent, gain = ins
    layer_out, gain_grad = outs
    g = gain[...].astype(F32)
    layer_out[item] = (resid[item] + branch * inv_rms(branch) * g).astype(BF16)
    dv, dg = rms_back(cotangent[item].astype(F32), branch, g)
    add_to(gain_grad, item, dg)
    return dv


def mid_back_rows(item, ffw_grad, ins, outs):
    resid, branch, cotangent, ffw_gain, attn_gain = ins
    resid_grad_out, ffw_gain_grad, attn_gain_grad = outs
    dv, dg = rms_back(ffw_grad, resid[item], ffw_gain[...].astype(F32))
    add_to(ffw_gain_grad, item, dg)
    resid_grad = cotangent[item].astype(F32) + dv
    resid_grad_out[item] = resid_grad
    dv, dg = rms_back(resid_grad, branch[item], attn_gain[...].astype(F32))
    add_to(attn_gain_grad, item, dg)
    return dv


def leave_rows(item, normed_grad, ins, outs):
    tokens, resid_grad, gain = ins
    tokens_grad, gain_grad = outs
    dv, dg = rms_back(normed_grad, tokens[item].astype(F32), gain[...].astype(F32))
    add_to(gain_grad, item, dg)
    tokens_grad[item] = resid_grad[item] + dv


GELU_A, GELU_B = 0.7978845608028654, 0.044715


def ffw_kernel(rows, gate_w, up_w, down_w, gate_out, up_out, mixed_out, part, total):
    step = pl.program_id(0)
    value = rows[...]
    gate = jnp.dot(value, gate_w[...], preferred_element_type=F32)
    up = jnp.dot(value, up_w[...], preferred_element_type=F32)
    tanh = jnp.tanh(GELU_A * (gate + GELU_B * (gate * gate * gate)))
    mixed = (0.5 * gate * (1.0 + tanh) * up).astype(BF16)
    gate_out[...], up_out[...], mixed_out[...] = gate, up, mixed
    term = jnp.dot(mixed, down_w[...], preferred_element_type=F32)

    @pl.when(step == 0)
    def _():
        total[...] = term

    @pl.when(step > 0)
    def _():
        total[...] += term

    @pl.when(step == pl.num_programs(0) - 1)
    def _():
        part[...] = total[...].astype(BF16)


def hidden_grad_kernel(bits, grad, gate, up, down_w, gate_give, up_give, gate_keep, up_keep):
    first, alike = pl.program_id(0) < pl.num_programs(0) // 2, bits[1] == 1
    mixed_grad = lax.dot_general(
        grad[...], down_w[...], (((1,), (1,)), ((), ())), preferred_element_type=F32
    )
    v = gate[...]
    square = v * v
    tanh = jnp.tanh(GELU_A * (v + GELU_B * (square * v)))
    half = 0.5 * (1.0 + tanh)
    slope = half + 0.5 * v * (1.0 - tanh * tanh) * (GELU_A * (1.0 + 3.0 * GELU_B * square))
    gate_g = (mixed_grad * up[...] * slope).astype(BF16)
    up_g = (mixed_grad * (half * v)).astype(BF16)

    @pl.when(first)
    def _():
        gate_give[...] = gate_g

    @pl.when(jnp.logical_not(first))
    def _():
        gate_keep[...] = gate_g

    @pl.when(first == alike)
    def _():
        up_give[...] = up_g

    @pl.when(first != alike)
    def _():
        up_keep[...] = up_g


def hidden_specs(rows, width, half_steps, tile):
    def at(i, bits):
        which = jnp.where(i < half_steps, 1 - bits[0], bits[0])
        return which * half_steps + jnp.where(i < half_steps, i, i - half_steps)

    def early(i):
        return jnp.minimum(i, half_steps - 1)

    def late(i):
        return jnp.maximum(i - half_steps, 0)

    def block(shape, index):
        return pl.BlockSpec(shape, index)

    return dict(
        cols=block((rows, tile), lambda i, bits: (0, at(i, bits))),
        tall=block((width, tile), lambda i, bits: (0, at(i, bits))),
        flat=block((tile, width), lambda i, bits: (at(i, bits), 0)),
        held=block((rows, width), lambda i, bits: (0, 0)),
        gate_give=block((rows, tile), lambda i, bits: (0, early(i))),
        gate_keep=block((rows, tile), lambda i, bits: (0, late(i))),
        up_give=block((rows, tile), lambda i, bits: (0, jnp.where(bits[1] == 1, early(i), late(i)))),
        up_keep=block((rows, tile), lambda i, bits: (0, jnp.where(bits[1] == 1, late(i), early(i)))),
    )


HALVES = ("gate_give", "up_give", "gate_keep", "up_keep")


def hidden_grads(bits, grad, gate, up, down_w):
    rows, width = grad.shape
    hidden = gate.shape[1]
    half_steps, tile = hidden // 2 // BACK_TILE, BACK_TILE
    spec = hidden_specs(rows, width, half_steps, tile)
    return pl.pallas_call(
        hidden_grad_kernel,
        grid_spec=pltpu.PrefetchScalarGridSpec(
            num_scalar_prefetch=1,
            grid=(2 * half_steps,),
            in_specs=[spec["held"], spec["cols"], spec["cols"], spec["flat"]],
            out_specs=[spec[name] for name in HALVES],
        ),
        out_shape=[jax.ShapeDtypeStruct((rows, hidden // 2), BF16)] * 4,
        compiler_params=pltpu.CompilerParams(vmem_limit_bytes=48 * MIB),
        cost_estimate=takes(1),
        name="hidden_grads",
    )(bits, grad, gate, up, down_w)


def input_grad_kernel(bits, gate_give, up_give, gate_keep, up_keep, gate_w, up_w, part, total):
    step = pl.program_id(0)
    first, alike = step < pl.num_programs(0) // 2, bits[1] == 1
    across = (((1,), (1,)), ((), ()))
    gate_g = jnp.where(first, gate_give[...], gate_keep[...])
    up_g = jnp.where(first == alike, up_give[...], up_keep[...])
    term = lax.dot_general(gate_g, gate_w[...], across, preferred_element_type=F32)
    term = term + lax.dot_general(up_g, up_w[...], across, preferred_element_type=F32)

    @pl.when(step == 0)
    def _():
        total[...] = term

    @pl.when(step > 0)
    def _():
        total[...] += term

    @pl.when(step == pl.num_programs(0) - 1)
    def _():
        part[...] = total[...].astype(BF16)


def input_grad(bits, halves, gate_w, up_w):
    rows = halves[0].shape[0]
    width, hidden = gate_w.shape
    half_steps, tile = hidden // 2 // BACK_TILE, BACK_TILE
    spec = hidden_specs(rows, width, half_steps, tile)
    return pl.pallas_call(
        input_grad_kernel,
        grid_spec=pltpu.PrefetchScalarGridSpec(
            num_scalar_prefetch=1,
            grid=(2 * half_steps,),
            in_specs=[spec[name] for name in HALVES] + [spec["tall"]] * 2,
            out_specs=spec["held"],
            scratch_shapes=[VMEM((rows, width), F32)],
        ),
        out_shape=jax.ShapeDtypeStruct((rows, width), BF16),
        compiler_params=pltpu.CompilerParams(vmem_limit_bytes=48 * MIB),
        cost_estimate=takes(1),
        name="input_grad",
    )(bits, *halves, gate_w, up_w)


def ffw_call(kernel, name, ins, weights, outs):
    rows, width = ins[0].shape
    hidden = weights[0].shape[1]
    tile = TILE
    cols = pl.BlockSpec((rows, tile), lambda i: (0, i))
    tall = pl.BlockSpec((width, tile), lambda i: (0, i))
    flat = pl.BlockSpec((tile, width), lambda i: (i, 0))
    held = pl.BlockSpec((rows, width), lambda i: (0, 0))
    return pl.pallas_call(
        kernel,
        grid=(hidden // tile,),
        out_shape=[jax.ShapeDtypeStruct((rows, hidden), t) for t in outs]
        + [jax.ShapeDtypeStruct((rows, width), BF16)],
        in_specs=[held] + [cols] * (len(ins) - 1) + [tall, tall, flat],
        out_specs=[cols] * len(outs) + [held],
        scratch_shapes=[VMEM((rows, width), F32)],
        compiler_params=pltpu.CompilerParams(vmem_limit_bytes=56 * MIB),
        cost_estimate=takes(1),
        name=name,
    )(*ins, *weights)


def body(
    tokens,
    doc_ids,
    attn_in_gain,
    query_weight,
    key_weight,
    value_weight,
    output_weight,
    attn_out_gain,
    ffw_in_gain,
    gate_weight,
    up_weight,
    down_weight,
    ffw_out_gain,
    cotangent,
):
    stretch_rows, seqs, slots, width = tokens.shape
    ctx_count = lax.axis_size("ctx")
    tp_count = lax.axis_size("tp")
    ctx_rank = lax.axis_index("ctx")
    stretch = stretch_rows * tp_count
    length = 2 * stretch * ctx_count
    rows = stretch * slots
    all_rows = seqs * rows
    local_heads = query_weight.shape[1] // HD
    assert key_weight.shape[1] == value_weight.shape[1] == HD
    own = (seqs, slots, stretch_rows, width)
    steps = ctx_count.bit_length() - 1

    slot_stretch = jnp.stack([ctx_rank, 2 * ctx_count - 1 - ctx_rank])
    iota = jnp.arange(stretch, dtype=jnp.int32)
    query_tok = slot_stretch[:, None] * stretch + iota[None, :]
    row_tok = query_tok.reshape(rows)
    row_doc = jnp.concatenate(
        [lax.dynamic_slice_in_dim(doc_ids, slot_stretch[i] * stretch, stretch, 1) for i in (0, 1)],
        1,
    )
    row_start = jnp.sum(
        (doc_ids[:, None, :] < row_doc[:, :, None]).astype(jnp.int32), axis=-1
    )
    row_pos = row_tok[None] - row_start
    frequency = BASE ** (-jnp.arange(HD // 2).astype(F32) / (HD // 2))
    angles = row_pos.astype(F32)[..., None] * frequency
    cosine, sine = jnp.cos(angles), jnp.sin(angles)
    key_slot = jnp.arange(2 * ctx_count, dtype=jnp.int32)
    key_stretch = jnp.where(key_slot % 2 == 0, key_slot // 2, 2 * ctx_count - 1 - key_slot // 2)
    key_tok = (key_stretch[:, None] * stretch + iota[None, :]).reshape(length)
    where = (row_start[..., None], row_tok[:, None], key_tok[None, :])

    def wide(gain):
        return gain.reshape(1, width)

    mine = jnp.transpose(tokens, (1, 2, 0, 3))
    upstream = jnp.transpose(cotangent, (1, 2, 0, 3))
    f32_rows = jax.ShapeDtypeStruct(own, F32)
    gain_shape = jax.ShapeDtypeStruct((1, width), F32)

    (normed_all,) = tp_exchange("enter", 1, enter_rows, [mine, wide(attn_in_gain)], [])
    normed_all = normed_all.reshape(all_rows, width)
    dot = functools.partial(jnp.dot, preferred_element_type=F32)
    ein = functools.partial(jnp.einsum, preferred_element_type=F32)
    queries = dot(normed_all, query_weight).reshape(seqs, rows, local_heads * HD)
    keys = dot(normed_all, key_weight).reshape(seqs, rows, HD)
    values = dot(normed_all, value_weight).reshape(seqs, rows, HD)
    kv_all, attn, attn_low, sums, queries = attend_all(
        queries, keys, values, cosine, sine, *where, 2
    )
    attn_rows = attn_low.reshape(all_rows, local_heads * HD)
    part = dot(attn_rows, output_weight).astype(BF16)

    def by_owner(value):
        return value.reshape(seqs, slots, tp_count, stretch_rows, width)

    ffw_all, branch, resid = tp_exchange(
        "middle",
        3,
        mid_rows,
        [mine, wide(attn_out_gain), wide(ffw_in_gain)],
        [f32_rows, f32_rows],
        by_owner(part),
    )
    ffw_all = ffw_all.reshape(all_rows, width)
    low_bit, next_bit, far_bit = 0, min(1, steps - 1), steps - 1
    high = list(range(2, steps))
    core = lax.axis_index("tp") % 2
    pick = functools.partial(lax.dynamic_index_in_dim, keepdims=False)

    def by_core(value):
        return value.reshape((seqs, slots, tp_count // 2, 2, stretch_rows, value.shape[-1]))

    def core_rows(value):
        return pick(by_core(value), core, 3).reshape(all_rows // 2, value.shape[-1])

    def owner_cols(value):
        bit = (ctx_rank >> far_bit) & 1
        cut = value.shape[1] // 2
        return [lax.dynamic_slice_in_dim(value, at * cut, cut, 1) for at in (bit, 1 - bit)]

    def owner_pieces(total, b):
        bit = (ctx_rank >> b) & 1
        cut = total.reshape(2, -1, total.shape[-1])
        return pick(cut, bit, 0), pick(cut, 1 - bit, 0)

    def whole_cols(own_half, got_half, b):
        bit = (ctx_rank >> b) & 1
        first = jnp.where(bit == 0, own_half, got_half)
        second = jnp.where(bit == 0, got_half, own_half)
        return jnp.concatenate([first, second], 1).astype(F32)

    ffw_send = core_rows(ffw_all)
    ffw_all, ffw_send = lax.optimization_barrier((ffw_all, ffw_send))
    ffw_far, ffw_far_low = Sent(ffw_send, next_bit), Sent(ffw_send, low_bit)
    ffw_weights = (gate_weight, up_weight, down_weight)
    gate, up, mixed, part = ffw_call(ffw_kernel, "ffw", [ffw_all], ffw_weights, [F32, F32, BF16])
    mixed_sent = Sent(by_core(mixed), far_bit)
    part = pin(part, ffw_far, ffw_far_low)
    ffw_near, ffw_near_low = CoreSent(ffw_far.gots[0]), CoreSent(ffw_far_low.gots[0])
    ffw_grad_all, layer_out, ffw_out_gain_part = tp_exchange(
        "turn",
        4,
        turn_rows,
        [resid, upstream, wide(ffw_out_gain)],
        [jax.ShapeDtypeStruct(own, BF16), gain_shape],
        by_owner(part),
    )
    ffw_grad_all = pin(ffw_grad_all.reshape(all_rows, width), ffw_near, ffw_near_low)
    grad_half, grad_give = owner_cols(ffw_grad_all)
    grad_send = core_rows(grad_give)
    ffw_grad_all, grad_send = lax.optimization_barrier((ffw_grad_all, grad_send))
    grad_far = Sent(grad_send, far_bit)
    gate_bit, up_bit = (ctx_rank >> low_bit) & 1, (ctx_rank >> next_bit) & 1
    bits = jnp.stack([gate_bit, (gate_bit == up_bit).astype(jnp.int32)])
    hidden = hidden_grads(bits, ffw_grad_all, gate, up, down_weight)
    gate_give, up_give, gate_half, up_half = [by_core(h) for h in hidden]
    gate_sent, up_sent = Sent(gate_give, low_bit), Sent(up_give, next_bit)
    part = input_grad(bits, hidden, gate_weight, up_weight)
    part = pin(part, gate_sent)
    gate_part = product(
        ffw_all, ffw_far_low.gots[0], ffw_near_low.gots[0], gate_half, gate_sent.gots[0], "gate_product"
    )
    gates = Halving(gate_part, [next_bit] + high)
    gates.send()
    part, gate_part = lax.optimization_barrier((part, gate_part))
    part = pin(part, up_sent)
    up_part = product(
        ffw_all, ffw_far.gots[0], ffw_near.gots[0], up_half, up_sent.gots[0], "up_product"
    )
    ups = Halving(up_part, [low_bit] + high)
    ups.send()
    part, up_part = lax.optimization_barrier((part, up_part))
    part = pin(part, grad_far, mixed_sent)
    grad_near = CoreSent(grad_far.gots[0])
    down_part = product(
        grad_half,
        grad_far.gots[0],
        grad_near.gots[0],
        by_core(mixed),
        mixed_sent.gots[0],
        "down_product",
    )
    down = Halving(down_part, [b for b in range(steps) if b != far_bit], far_bit)
    down.send()
    part, down_part = lax.optimization_barrier((part, down_part))
    branch_grad_all, resid_grad, ffw_in_gain_part, attn_out_gain_part = tp_exchange(
        "middle_back",
        5,
        mid_back_rows,
        [resid, branch, upstream, wide(ffw_in_gain), wide(attn_out_gain)],
        [f32_rows, gain_shape, gain_shape],
        by_owner(part),
    )
    branch_grad_all = branch_grad_all.reshape(all_rows, width)
    output_part = ein("rd,rh->dh", branch_grad_all, attn_rows).astype(BF16)
    attn_grad = ein("rd,hd->rh", branch_grad_all, output_weight).reshape(attn.shape)
    attn_grad = pin(attn_grad, gates)
    gates.step()
    qkv_grad = attend_back(queries, kv_all, attn_grad, attn, sums, cosine, sine, *where, 16)
    qkv_grad = pin(qkv_grad, down, ups).reshape(all_rows, -1)
    ups.step()
    down.step()
    qkv_weight = jnp.concatenate([query_weight, key_weight, value_weight], 1)
    part = ein("rh,dh->rd", qkv_grad, qkv_weight).astype(BF16)
    qkv_part = ein("rd,rh->dh", normed_all, qkv_grad).astype(BF16)
    tokens_grad, attn_in_gain_part = tp_exchange(
        "leave",
        7,
        leave_rows,
        [mine, resid_grad, wide(attn_in_gain)],
        [f32_rows, gain_shape],
        by_owner(part),
        gather=False,
    )
    gains = jnp.concatenate(
        [attn_in_gain_part, attn_out_gain_part, ffw_in_gain_part, ffw_out_gain_part], 0
    )
    (output_sum, qkv_sum), gains = weights_scatter([output_part, qkv_part], gains, 8)
    gains = pin(gains, gates, ups, down)
    gate_own, gate_give = owner_pieces(gates.finish(), low_bit)
    gate_sent = Sent(gate_give, low_bit)
    up_own, up_give = owner_pieces(ups.finish(), next_bit)
    up_sent = Sent(up_give, next_bit)
    down_sum = down.finish().astype(F32)
    gate_sum = whole_cols(gate_own, gate_sent.gots[0], low_bit)
    up_sum = whole_cols(up_own, up_sent.gots[0], next_bit)
    share = width // ctx_count
    gains = lax.dynamic_slice_in_dim(gains, ctx_rank * share, share, 1)
    heads_end = local_heads * HD
    keys_end = heads_end + HD
    return (
        jnp.transpose(layer_out, (2, 0, 1, 3)),
        jnp.transpose(tokens_grad, (2, 0, 1, 3)),
        gains[0],
        qkv_sum[:, :heads_end],
        qkv_sum[:, heads_end:keys_end],
        qkv_sum[:, keys_end:],
        output_sum.T,
        gains[1],
        gains[2],
        gate_sum,
        up_sum,
        down_sum.T,
        gains[3],
    )


def solution(mesh):
    placed = (
        P("tp", None, "ctx", None),
        P(),
        P(),
        P(None, "tp"),
        P(None, "tp"),
        P(None, "tp"),
        P("tp", None),
        P(),
        P(),
        P(None, "tp"),
        P(None, "tp"),
        P("tp", None),
        P(),
        P("tp", None, "ctx", None),
    )
    return jax.shard_map(
        body,
        mesh=mesh,
        in_specs=placed,
        out_specs=(
            P("tp", None, "ctx", None),
            P("tp", None, "ctx", None),
            P("ctx"),
            P("ctx", "tp"),
            P("ctx", "tp"),
            P("ctx", "tp"),
            P("tp", "ctx"),
            P("ctx"),
            P("ctx"),
            P("ctx", "tp"),
            P("ctx", "tp"),
            P("tp", "ctx"),
            P("ctx"),
        ),
        check_vma=False,
    )
```

```python
import functools

import jax
import jax.numpy as jnp
from jax import lax
from jax.experimental import pallas as pl
from jax.experimental.pallas import tpu as pltpu
from jax.sharding import PartitionSpec as P

HD = 256
EPS = 1e-06
CAP = 50.0
BASE = 10000.0
MIB = 1 << 20
TILE = 768
BACK_TILE = 384
F32 = jnp.float32
BF16 = jnp.bfloat16
VMEM = pltpu.VMEM
MESH = pl.DeviceIdType.MESH


def bits_of(mask):
    return [b for b in range(mask.bit_length()) if mask >> b & 1]


def flipped(index, mask):
    for b in bits_of(mask):
        index = index + (1 - 2 * ((index // (1 << b)) % 2)) * (1 << b)
    return index


def without(mask, bit):
    return (mask >> bit + 1 << bit) | (mask & (1 << bit) - 1)


def submasks(bits):
    masks = [0]
    for b in bits:
        masks = masks + [m | 1 << b for m in masks]
    return masks


def scatter_events(orders):
    steps = len(orders[0])
    usual = [i for i, order in enumerate(orders) if order[0] == 0]
    other = [i for i, order in enumerate(orders) if order[0] != 0]
    events = []
    for t in range(len(usual) + steps - 1):
        events += [(usual[t - s], s) for s in range(steps) if 0 <= t - s < len(usual)]
        if 1 <= t <= len(other):
            events.append((other[t - 1], 0))
    events += [(i, 0) for i in other[max(0, len(usual) + steps - 2) :]]
    for t in range(len(other) + steps - 2):
        events += [(other[t - s + 1], s) for s in range(1, steps) if 0 <= t - s + 1 < len(other)]
    return events


def greet(axis, count):
    me = lax.axis_index(axis)
    barrier = pltpu.get_barrier_semaphore()
    steps = count.bit_length() - 1
    for b in range(steps):
        pl.semaphore_signal(
            barrier, inc=1, device_id={axis: flipped(me, 1 << b)}, device_id_type=MESH
        )
    pl.semaphore_wait(barrier, steps)


def remote(axis, src, dst, sems, at, partner):
    return pltpu.make_async_remote_copy(
        src_ref=src,
        dst_ref=dst,
        send_sem=sems[0].at[at],
        recv_sem=sems[1].at[at],
        device_id={axis: partner},
        device_id_type=MESH,
    )


def tp_kernel(fn, count, items, n_in, n_out, scatter, gather, *refs):
    refs = list(refs)
    part = refs.pop(0) if scatter else None
    ins = [refs.pop(0) for _ in range(n_in)]
    whole = refs.pop(0) if gather else None
    outs = [refs.pop(0) for _ in range(n_out)]
    if scatter:
        landed, sendbuf = refs.pop(0), refs.pop(0)
        rs_sems = (refs.pop(0), refs.pop(0))
    if gather:
        ag_sems = (refs.pop(0), refs.pop(0))
    me = lax.axis_index("tp")
    steps = count.bit_length() - 1
    order = list(range(steps))
    greet("tp", count)

    def rs_copy(item, step, sub):
        bit = 1 << order[step]
        mask = bit | sub
        src = part.at[item, :, flipped(me, mask)] if step == 0 else sendbuf.at[item, mask]
        return remote("tp", src, landed.at[item, mask], rs_sems, (item, mask), flipped(me, bit))

    def rs_sum(item, mask, upto):
        total = part[item, :, flipped(me, mask)].astype(F32)
        for step in range(upto):
            total = total + landed[item, 1 << order[step] | mask].astype(F32)
        return total

    def rs_subs(step):
        return submasks(order[step + 1 :])

    def ag_copy(item, step, mask):
        bit = 1 << order[steps - 1 - step]
        block = whole.at[item, :, flipped(me, mask)]
        return remote("tp", block, block, ag_sems, (item, mask | bit), flipped(me, bit))

    def ag_masks(step):
        return submasks([order[steps - 1 - s] for s in range(step)])

    if scatter:
        for item in range(items):
            for sub in rs_subs(0):
                rs_copy(item, 0, sub).start()
        for step in range(1, steps):
            for item in range(items):
                for sub in rs_subs(step - 1):
                    rs_copy(item, step - 1, sub).wait_recv()
                for sub in rs_subs(step):
                    mask = 1 << order[step] | sub
                    sendbuf[item, mask] = rs_sum(item, mask, step).astype(BF16)
                    rs_copy(item, step, sub).start()
    for item in range(items):
        total = None
        if scatter:
            for sub in rs_subs(steps - 1):
                rs_copy(item, steps - 1, sub).wait_recv()
            total = rs_sum(item, 0, steps)
        sent = fn(item, total, ins, outs)
        if gather:
            whole[item, :, me] = sent.astype(BF16)
            for step in range(steps):
                ag_copy(item, step, 0).start()
    if gather:
        for got in range(steps):
            for item in range(items):
                for mask in ag_masks(got):
                    ag_copy(item, got, mask).wait_recv()
                    for step in range(got + 1, steps):
                        ag_copy(item, step, mask | 1 << order[steps - 1 - got]).start()
        for step in range(steps):
            for item in range(items):
                for mask in ag_masks(step):
                    ag_copy(item, step, mask).wait_send()
    if scatter:
        for step in range(steps):
            for item in range(items):
                for sub in rs_subs(step):
                    rs_copy(item, step, sub).wait_send()


def takes(us):
    return pl.CostEstimate(flops=int(us * 1e7), bytes_accessed=0, transcendentals=0)


def tp_exchange(name, cid, fn, ins, outs, part=None, gather=True):
    count = lax.axis_size("tp")
    rows_shape = ins[0].shape
    items, slots, rows, width = rows_shape
    scatter = part is not None
    out_shape = list(outs)
    if gather:
        out_shape = [jax.ShapeDtypeStruct((items, slots, count, rows, width), BF16)] + out_shape
    scratch = []
    dma = pltpu.SemaphoreType.DMA((items, count))
    if scatter:
        scratch += [VMEM((items, count, slots, rows, width), BF16)] * 2 + [dma, dma]
    if gather:
        scratch += [dma, dma]
    args = ([part] if scatter else []) + list(ins)
    return pl.pallas_call(
        functools.partial(
            tp_kernel, fn, count, items, len(ins), len(outs), scatter, gather
        ),
        out_shape=out_shape,
        in_specs=[pl.BlockSpec(memory_space=VMEM)] * len(args),
        out_specs=[pl.BlockSpec(memory_space=VMEM)] * len(out_shape),
        scratch_shapes=scratch,
        compiler_params=pltpu.CompilerParams(
            collective_id=cid, has_side_effects=True, vmem_limit_bytes=40 * MIB
        ),
        cost_estimate=takes(18 * (scatter + gather)),
        name=name,
    )(*args)


def cube_order(steps, turned):
    usual = list(range(steps))
    return [1, 0] + usual[2:] if turned and steps > 1 else usual


def ctx_orders(items, steps):
    return [cube_order(steps, i >= items - 3 * items // 10) for i in range(items)]


def rotated(values, cosine, sine):
    low, high = values[:, : HD // 2], values[:, HD // 2 :]
    return jnp.concatenate([low * cosine - high * sine, high * cosine + low * sine], 1)


def attend_kernel(count, seqs, heads, q, k, v, cosine, sine, start, tok, key_tok, *refs):
    whole, attn, attn_low, sums, queries, send_sem, recv_sem = refs
    me = lax.axis_index("ctx")
    steps = count.bit_length() - 1
    items = 2 * seqs
    orders = [order[::-1] for order in ctx_orders(items, steps)]
    rows = q.shape[1]
    scale = HD ** (-0.5)

    def copy(item, step, mask):
        bit = 1 << orders[item][step]
        block = whole.at[item, flipped(me, mask)]
        return remote(
            "ctx", block, block, (send_sem, recv_sem), (item, mask | bit), flipped(me, bit)
        )

    def masks(item, step):
        return submasks(orders[item][:step])

    def send_own(item):
        for step in range(steps):
            copy(item, step, 0).start()

    for s in range(seqs):
        whole[2 * s, me] = rotated(k[s], cosine[s], sine[s]).astype(BF16)
        whole[2 * s + 1, me] = v[s].astype(BF16)
        if s == 0:
            greet("ctx", count)
        send_own(2 * s)
        send_own(2 * s + 1)
    for s in range(seqs):
        for h in range(heads):
            at = slice(h * HD, (h + 1) * HD)
            queries[s, :, at] = rotated(q[s, :, at], cosine[s], sine[s]).astype(BF16)

    def attend(s):
        keys = whole[2 * s].reshape(count * rows, HD)
        values = whole[2 * s + 1].reshape(count * rows, HD)
        allowed = (key_tok[...] <= tok[...]) & (key_tok[...] >= start[s])
        for h in range(heads):
            at = slice(h * HD, (h + 1) * HD)
            raw = lax.dot_general(
                queries[s, :, at], keys, (((1,), (1,)), ((), ())), preferred_element_type=F32
            )
            exps = jnp.where(allowed, jnp.exp(CAP * jnp.tanh(raw * (scale / CAP))), 0.0)
            total = jnp.sum(exps, axis=-1, keepdims=True)
            out = jnp.dot(exps.astype(BF16), values, preferred_element_type=F32) / total
            sums[s, h] = total
            attn[s, :, at] = out
            attn_low[s, :, at] = out.astype(BF16)

    for got in range(steps):
        for item in range(items):
            for mask in masks(item, got):
                copy(item, got, mask).wait_recv()
                for step in range(got + 1, steps):
                    copy(item, step, mask | 1 << orders[item][got]).start()
            if got == steps - 1 and item % 2 == 1:
                attend(item // 2)
    for step in range(steps):
        for item in range(items):
            for mask in masks(item, step):
                copy(item, step, mask).wait_send()


def attend_all(q, k, v, cosine, sine, start, tok, key_tok, cid):
    count = lax.axis_size("ctx")
    seqs, rows, cols = q.shape
    heads = cols // HD
    dma = pltpu.SemaphoreType.DMA((2 * seqs, count))
    shape = jax.ShapeDtypeStruct
    args = (q, k, v, cosine, sine, start, tok, key_tok)
    outs = [
        shape((2 * seqs, count, rows, HD), BF16),
        shape(q.shape, F32),
        shape(q.shape, BF16),
        shape((seqs, heads, rows, 1), F32),
        shape(q.shape, BF16),
    ]
    return pl.pallas_call(
        functools.partial(attend_kernel, count, seqs, heads),
        out_shape=outs,
        in_specs=[pl.BlockSpec(memory_space=VMEM)] * len(args),
        out_specs=[pl.BlockSpec(memory_space=VMEM)] * len(outs),
        scratch_shapes=[dma, dma],
        compiler_params=pltpu.CompilerParams(
            collective_id=cid, has_side_effects=True, vmem_limit_bytes=56 * MIB
        ),
        cost_estimate=takes(60),
        name="attend",
    )(*args)


def attend_back_kernel(count, seqs, heads, *refs):
    queries, whole, out_grad, attn, sums, cosine, sine, start, tok, key_tok = refs[:10]
    grads, part, landed, sendbuf, query_grad, send_sem, recv_sem = refs[10:]
    me = lax.axis_index("ctx")
    steps = count.bit_length() - 1
    items = 2 * seqs
    orders = ctx_orders(items, steps)
    rows = queries.shape[1]
    scale = HD ** (-0.5)
    greet("ctx", count)

    def copy(item, step, sub):
        order = orders[item]
        bit = 1 << order[step]
        mask = bit | sub
        if step == 0:
            src = part.at[item, flipped(me, mask)]
        else:
            src = sendbuf.at[item, without(mask, order[0])]
        return remote(
            "ctx", src, landed.at[item, mask], (send_sem, recv_sem), (item, mask), flipped(me, bit)
        )

    def total_of(item, mask, upto):
        total = part[item, flipped(me, mask)].astype(F32)
        for step in range(upto):
            total = total + landed[item, 1 << orders[item][step] | mask].astype(F32)
        return total

    def subs(item, step):
        return submasks(orders[item][step + 1 :])

    def backward(s):
        keys = whole[2 * s].reshape(count * rows, HD)
        values = whole[2 * s + 1].reshape(count * rows, HD)
        allowed = (key_tok[...] <= tok[...]) & (key_tok[...] >= start[s])
        key_grad, value_grad = None, None
        for h in range(heads):
            at = slice(h * HD, (h + 1) * HD)
            query, total = queries[s, :, at], sums[s, h]
            raw = lax.dot_general(query, keys, (((1,), (1,)), ((), ())), preferred_element_type=F32)
            tanh = jnp.tanh(raw * (scale / CAP))
            exps = jnp.where(allowed, jnp.exp(CAP * tanh), 0.0)
            og = out_grad[s, :, at]
            low = (og / total).astype(BF16)
            shift = jnp.sum(og * attn[s, :, at], axis=-1, keepdims=True) / total
            toward = lax.dot_general(
                low, values, (((1,), (1,)), ((), ())), preferred_element_type=F32
            )
            score = (exps * (toward - shift) * (scale * (1.0 - tanh * tanh))).astype(BF16)
            grad = jnp.dot(score, keys, preferred_element_type=F32)
            query_grad[s, :, at] = grad
            across = (((0,), (0,)), ((), ()))
            k_term = lax.dot_general(score, query, across, preferred_element_type=F32)
            v_term = lax.dot_general(exps.astype(BF16), low, across, preferred_element_type=F32)
            key_grad = k_term if h == 0 else key_grad + k_term
            value_grad = v_term if h == 0 else value_grad + v_term
        part[2 * s] = key_grad.astype(BF16).reshape(count, rows, HD)
        part[2 * s + 1] = value_grad.astype(BF16).reshape(count, rows, HD)

    def advance(item, got):
        for sub in subs(item, got):
            copy(item, got, sub).wait_recv()
        step = got + 1
        if step == steps:
            s, total = item // 2, total_of(item, 0, steps)
            if item % 2 == 0:
                total = rotated(total, cosine[s], -sine[s])
            lane = heads * HD + (item % 2) * HD
            grads[s, :, lane : lane + HD] = total.astype(BF16)
            return
        for sub in subs(item, step):
            mask = 1 << orders[item][step] | sub
            sendbuf[item, without(mask, orders[item][0])] = total_of(item, mask, step).astype(BF16)
            copy(item, step, sub).start()

    for s in range(seqs):
        backward(s)
        for item in (2 * s, 2 * s + 1):
            for sub in subs(item, 0):
                copy(item, 0, sub).start()
    for s in range(seqs):
        for h in range(heads):
            at = slice(h * HD, (h + 1) * HD)
            grads[s, :, at] = rotated(query_grad[s, :, at], cosine[s], -sine[s]).astype(BF16)
    for item, got in scatter_events(orders):
        advance(item, got)
    for step in range(steps):
        for item in range(items):
            for sub in subs(item, step):
                copy(item, step, sub).wait_send()


def attend_back_some(queries, whole, out_grad, attn, sums, cosine, sine, start, tok, key_tok, cid):
    count = lax.axis_size("ctx")
    seqs, rows, cols = queries.shape
    heads = cols // HD
    dma = pltpu.SemaphoreType.DMA((2 * seqs, count))
    args = (queries, whole, out_grad, attn, sums, cosine, sine, start, tok, key_tok)
    return pl.pallas_call(
        functools.partial(attend_back_kernel, count, seqs, heads),
        out_shape=jax.ShapeDtypeStruct((seqs, rows, cols + 2 * HD), BF16),
        in_specs=[pl.BlockSpec(memory_space=VMEM)] * len(args),
        out_specs=pl.BlockSpec(memory_space=VMEM),
        scratch_shapes=[
            VMEM(whole.shape, BF16),
            VMEM(whole.shape, BF16),
            VMEM((2 * seqs, max(count // 2, 1), rows, HD), BF16),
            VMEM(queries.shape, F32),
            dma,
            dma,
        ],
        compiler_params=pltpu.CompilerParams(
            collective_id=cid, has_side_effects=True, vmem_limit_bytes=56 * MIB
        ),
        cost_estimate=takes(60),
        name="attend_back",
    )(*args)


def attend_back(queries, whole, out_grad, attn, sums, cosine, sine, start, tok, key_tok, cid):
    seqs = queries.shape[0]
    size = max(1, min(seqs, 8 * seqs // whole.shape[1]))
    grads = []
    for i, s in enumerate(range(0, seqs, size)):
        e = min(s + size, seqs)
        some = (queries[s:e], whole[2 * s : 2 * e], out_grad[s:e], attn[s:e], sums[s:e])
        near = (cosine[s:e], sine[s:e], start[s:e], tok, key_tok)
        grads.append(attend_back_some(*some, *near, cid + i))
    return grads[0] if len(grads) == 1 else jnp.concatenate(grads, 0)


def send_ctx(value, mask):
    return lax.ppermute(value, "ctx", [(i, i ^ mask) for i in range(lax.axis_size("ctx"))])


def send_core(value):
    return lax.ppermute(value, "tp", [(i, i ^ 1) for i in range(lax.axis_size("tp"))])


class Halving:
    def __init__(self, part, order, but=None):
        steps = lax.axis_size("ctx").bit_length() - 1
        self.order = list(order)
        self.left = [b for b in range(steps)[::-1] if b != but]
        owners = 1 << len(self.left)
        self.total = part.reshape((2,) * len(self.left) + (part.shape[0] // owners, part.shape[1]))

    def send(self):
        b = self.order.pop(0)
        axis = self.left.index(b)
        self.left.remove(b)
        mine = (lax.axis_index("ctx") >> b) & 1
        pick = functools.partial(lax.dynamic_index_in_dim, axis=axis, keepdims=False)
        self.gots = [send_ctx(pick(self.total, 1 - mine), 1 << b)]
        self.keep = pick(self.total, mine)

    def add(self):
        self.total = (self.keep.astype(F32) + self.gots[0].astype(F32)).astype(BF16)

    def step(self):
        self.add()
        if self.order:
            self.send()
        else:
            del self.gots

    def finish(self):
        if self.order and not hasattr(self, "gots"):
            self.send()
        while hasattr(self, "gots"):
            self.add()
            del self.gots
            if self.order:
                self.send()
        return self.total


class Sent:
    def __init__(self, value, b):
        self.gots = [send_ctx(value, 1 << b)]


class CoreSent(Sent):
    def __init__(self, value):
        self.gots = [send_core(value)]


def pin(value, *sent):
    value, gots = lax.optimization_barrier((value, [s.gots for s in sent]))
    for s, got in zip(sent, gots):
        s.gots = got
    return value


def product_kernel(own, far, near, mine, got, out):
    core = lax.axis_index("tp") % 2
    cols = mine.shape[-1]

    def times(left, right):
        return lax.dot_general(
            left, right.reshape(-1, cols), (((0,), (0,)), ((), ())), preferred_element_type=F32
        )

    total = times(own[...], mine[...])
    total = total + times(far[...], got[:, :, :, core])
    total = total + times(near[...], got[:, :, :, 1 - core])
    out[...] = total.astype(BF16)


def product(own, far, near, mine, got, name):
    rows, width = own.shape
    cols, tile = mine.shape[-1], 256 if width % 256 == 0 else 384
    whole = pl.BlockSpec(mine.shape, lambda i: (0,) * mine.ndim)
    return pl.pallas_call(
        product_kernel,
        grid=(width // tile,),
        out_shape=jax.ShapeDtypeStruct((width, cols), BF16),
        in_specs=[
            pl.BlockSpec((rows, tile), lambda i: (0, i)),
            pl.BlockSpec((rows // 2, tile), lambda i: (0, i)),
            pl.BlockSpec((rows // 2, tile), lambda i: (0, i)),
            whole,
            whole,
        ],
        out_specs=pl.BlockSpec((tile, cols), lambda i: (i, 0)),
        compiler_params=pltpu.CompilerParams(vmem_limit_bytes=40 * MIB),
        cost_estimate=takes(1),
        name=name,
    )(own, far, near, mine, got)


def weights_scatter_kernel(count, tp_count, plan, n_parts, *refs):
    refs = list(refs)
    parts = [refs.pop(0) for _ in range(n_parts)]
    gains = refs.pop(0)
    outs = [refs.pop(0) for _ in range(n_parts)]
    gains_out = refs.pop(0)
    landed = [refs.pop(0) for _ in range(n_parts)]
    sendbuf = [refs.pop(0) for _ in range(n_parts)]
    gains_landed, gains_send = refs.pop(0), refs.pop(0)
    sems = (refs.pop(0), refs.pop(0))
    gain_sems = (refs.pop(0), refs.pop(0))
    me = lax.axis_index("ctx")
    me_tp = lax.axis_index("tp")
    steps = count.bit_length() - 1
    tp_steps = tp_count.bit_length() - 1
    barrier = pltpu.get_barrier_semaphore()
    for b in range(steps):
        pl.semaphore_signal(
            barrier, inc=1, device_id={"ctx": flipped(me, 1 << b)}, device_id_type=MESH
        )
    for b in range(tp_steps):
        pl.semaphore_signal(
            barrier, inc=1, device_id={"tp": flipped(me_tp, 1 << b)}, device_id_type=MESH
        )
    pl.semaphore_wait(barrier, steps + tp_steps)

    def subs(order, step):
        return submasks(order[step + 1 :])

    def copy(n, step, sub):
        p, item, order = plan[n]
        bit = 1 << order[step]
        mask = bit | sub
        if step == 0:
            src = parts[p].at[flipped(me, mask), item]
        else:
            src = sendbuf[p].at[without(mask, order[0]), item]
        return remote(
            "ctx", src, landed[p].at[mask, item], sems, (n, mask), flipped(me, bit)
        )

    def total_of(n, mask, upto):
        p, item, order = plan[n]
        total = parts[p][flipped(me, mask), item].astype(F32)
        for step in range(upto):
            total = total + landed[p][1 << order[step] | mask, item].astype(F32)
        return total

    for n, (_, _, order) in enumerate(plan):
        for sub in subs(order, 0):
            copy(n, 0, sub).start()

    hops = tp_steps + steps
    gains_send[0] = gains[...]

    def hop(step):
        axis, bit, at = ("tp", step, me_tp) if step < tp_steps else ("ctx", step - tp_steps, me)
        return remote(
            axis,
            gains_send.at[step],
            gains_landed.at[step],
            gain_sems,
            step,
            flipped(at, 1 << bit),
        )

    def end_hop(step):
        hop(step).wait_recv()
        both = gains_send[step] + gains_landed[step]
        if step + 1 < hops:
            gains_send[step + 1] = both
            hop(step + 1).start()
        else:
            gains_out[...] = both

    hop(0).start()
    for step in range(tp_steps):
        end_hop(step)
    orders = [order for _, _, order in plan]
    events = scatter_events(orders)
    first_done = max(k for k, (n, step) in enumerate(events) if step == 0)

    for k, (n, got) in enumerate(events):
        p, item, order = plan[n]
        for sub in subs(order, got):
            copy(n, got, sub).wait_recv()
        step = got + 1
        if step == steps:
            outs[p][item] = total_of(n, 0, steps)
        else:
            for sub in subs(order, step):
                mask = 1 << order[step] | sub
                sendbuf[p][without(mask, order[0]), item] = total_of(n, mask, step).astype(BF16)
                copy(n, step, sub).start()
        if k == first_done:
            end_hop(tp_steps)
    for step in range(tp_steps + 1, hops):
        end_hop(step)
    for step in range(hops):
        hop(step).wait_send()
    for step in range(steps):
        for n, (_, _, order) in enumerate(plan):
            for sub in subs(order, step):
                copy(n, step, sub).wait_send()


def weights_scatter(parts, gains, cid):
    count, tp_count = lax.axis_size("ctx"), lax.axis_size("tp")
    steps = count.bit_length() - 1
    rows = parts[0].shape[0] // count
    cut = max(c for c in range(1, 7) if rows % (16 * c) == 0) if rows % 16 == 0 else 1
    blocks = [p.reshape(count, cut, rows // cut, p.shape[1]) for p in parts]
    pairs = [(p, item) for item in range(cut) for p in range(len(parts))]
    orders = ctx_orders(len(pairs), steps)
    plan = [(p, item, order) for (p, item), order in zip(pairs, orders)]
    hops = steps + tp_count.bit_length() - 1
    dma = pltpu.SemaphoreType.DMA((len(plan), count))
    out = pl.pallas_call(
        functools.partial(weights_scatter_kernel, count, tp_count, plan, len(parts)),
        out_shape=[jax.ShapeDtypeStruct(b.shape[1:], F32) for b in blocks]
        + [jax.ShapeDtypeStruct(gains.shape, F32)],
        in_specs=[pl.BlockSpec(memory_space=VMEM)] * (len(parts) + 1),
        out_specs=[pl.BlockSpec(memory_space=VMEM)] * (len(parts) + 1),
        scratch_shapes=[VMEM(b.shape, BF16) for b in blocks]
        + [VMEM((max(count // 2, 1),) + b.shape[1:], BF16) for b in blocks]
        + [VMEM((hops,) + gains.shape, F32)] * 2
        + [dma, dma, pltpu.SemaphoreType.DMA((hops,)), pltpu.SemaphoreType.DMA((hops,))],
        compiler_params=pltpu.CompilerParams(
            collective_id=cid, has_side_effects=True, vmem_limit_bytes=56 * MIB
        ),
        cost_estimate=takes(80),
        name="weights_scatter",
    )(*blocks, gains)
    return [o.reshape(rows, o.shape[-1]) for o in out[:-1]], out[-1]


def inv_rms(v):
    return lax.rsqrt(jnp.mean(v * v, axis=-1, keepdims=True) + EPS)


def rms_back(dy, v, g):
    r = inv_rms(v)
    dg = jnp.sum(dy * v * r, axis=tuple(range(v.ndim - 1)), keepdims=True)
    gdy = g * dy
    dv = r * gdy - v * (r * r * r) * jnp.mean(gdy * v, axis=-1, keepdims=True)
    return dv, dg.reshape(1, -1)


def add_to(ref, item, value):
    ref[...] = value if item == 0 else ref[...] + value


def enter_rows(item, _, ins, outs):
    tokens, gain = ins
    v = tokens[item].astype(F32)
    return v * inv_rms(v) * gain[...].astype(F32)


def mid_rows(item, branch, ins, outs):
    tokens, attn_gain, ffw_gain = ins
    branch_out, resid_out = outs
    branch_out[item] = branch
    resid = tokens[item].astype(F32) + branch * inv_rms(branch) * attn_gain[...].astype(F32)
    resid_out[item] = resid
    return resid * inv_rms(resid) * ffw_gain[...].astype(F32)


def turn_rows(item, branch, ins, outs):
    resid, cotangent, gain = ins
    layer_out, gain_grad = outs
    g = gain[...].astype(F32)
    layer_out[item] = (resid[item] + branch * inv_rms(branch) * g).astype(BF16)
    dv, dg = rms_back(cotangent[item].astype(F32), branch, g)
    add_to(gain_grad, item, dg)
    return dv


def mid_back_rows(item, ffw_grad, ins, outs):
    resid, branch, cotangent, ffw_gain, attn_gain = ins
    resid_grad_out, ffw_gain_grad, attn_gain_grad = outs
    dv, dg = rms_back(ffw_grad, resid[item], ffw_gain[...].astype(F32))
    add_to(ffw_gain_grad, item, dg)
    resid_grad = cotangent[item].astype(F32) + dv
    resid_grad_out[item] = resid_grad
    dv, dg = rms_back(resid_grad, branch[item], attn_gain[...].astype(F32))
    add_to(attn_gain_grad, item, dg)
    return dv


def leave_rows(item, normed_grad, ins, outs):
    tokens, resid_grad, gain = ins
    tokens_grad, gain_grad = outs
    dv, dg = rms_back(normed_grad, tokens[item].astype(F32), gain[...].astype(F32))
    add_to(gain_grad, item, dg)
    tokens_grad[item] = resid_grad[item] + dv


GELU_A, GELU_B = 0.7978845608028654, 0.044715


def ffw_kernel(rows, gate_w, up_w, down_w, gate_out, up_out, mixed_out, part, total):
    step = pl.program_id(0)
    value = rows[...]
    gate = jnp.dot(value, gate_w[...], preferred_element_type=F32)
    up = jnp.dot(value, up_w[...], preferred_element_type=F32)
    tanh = jnp.tanh(GELU_A * (gate + GELU_B * (gate * gate * gate)))
    mixed = (0.5 * gate * (1.0 + tanh) * up).astype(BF16)
    gate_out[...], up_out[...], mixed_out[...] = gate, up, mixed
    term = jnp.dot(mixed, down_w[...], preferred_element_type=F32)

    @pl.when(step == 0)
    def _():
        total[...] = term

    @pl.when(step > 0)
    def _():
        total[...] += term

    @pl.when(step == pl.num_programs(0) - 1)
    def _():
        part[...] = total[...].astype(BF16)


def hidden_grad_kernel(bits, grad, gate, up, down_w, gate_give, up_give, gate_keep, up_keep):
    first, alike = pl.program_id(0) < pl.num_programs(0) // 2, bits[1] == 1
    mixed_grad = lax.dot_general(
        grad[...], down_w[...], (((1,), (1,)), ((), ())), preferred_element_type=F32
    )
    v = gate[...]
    square = v * v
    tanh = jnp.tanh(GELU_A * (v + GELU_B * (square * v)))
    half = 0.5 * (1.0 + tanh)
    slope = half + 0.5 * v * (1.0 - tanh * tanh) * (GELU_A * (1.0 + 3.0 * GELU_B * square))
    gate_g = (mixed_grad * up[...] * slope).astype(BF16)
    up_g = (mixed_grad * (half * v)).astype(BF16)

    @pl.when(first)
    def _():
        gate_give[...] = gate_g

    @pl.when(jnp.logical_not(first))
    def _():
        gate_keep[...] = gate_g

    @pl.when(first == alike)
    def _():
        up_give[...] = up_g

    @pl.when(first != alike)
    def _():
        up_keep[...] = up_g


def hidden_specs(rows, width, half_steps, tile):
    def at(i, bits):
        which = jnp.where(i < half_steps, 1 - bits[0], bits[0])
        return which * half_steps + jnp.where(i < half_steps, i, i - half_steps)

    def early(i):
        return jnp.minimum(i, half_steps - 1)

    def late(i):
        return jnp.maximum(i - half_steps, 0)

    def block(shape, index):
        return pl.BlockSpec(shape, index)

    return dict(
        cols=block((rows, tile), lambda i, bits: (0, at(i, bits))),
        tall=block((width, tile), lambda i, bits: (0, at(i, bits))),
        flat=block((tile, width), lambda i, bits: (at(i, bits), 0)),
        held=block((rows, width), lambda i, bits: (0, 0)),
        gate_give=block((rows, tile), lambda i, bits: (0, early(i))),
        gate_keep=block((rows, tile), lambda i, bits: (0, late(i))),
        up_give=block((rows, tile), lambda i, bits: (0, jnp.where(bits[1] == 1, early(i), late(i)))),
        up_keep=block((rows, tile), lambda i, bits: (0, jnp.where(bits[1] == 1, late(i), early(i)))),
    )


HALVES = ("gate_give", "up_give", "gate_keep", "up_keep")


def hidden_grads(bits, grad, gate, up, down_w):
    rows, width = grad.shape
    hidden = gate.shape[1]
    half_steps, tile = hidden // 2 // BACK_TILE, BACK_TILE
    spec = hidden_specs(rows, width, half_steps, tile)
    return pl.pallas_call(
        hidden_grad_kernel,
        grid_spec=pltpu.PrefetchScalarGridSpec(
            num_scalar_prefetch=1,
            grid=(2 * half_steps,),
            in_specs=[spec["held"], spec["cols"], spec["cols"], spec["flat"]],
            out_specs=[spec[name] for name in HALVES],
        ),
        out_shape=[jax.ShapeDtypeStruct((rows, hidden // 2), BF16)] * 4,
        compiler_params=pltpu.CompilerParams(vmem_limit_bytes=48 * MIB),
        cost_estimate=takes(1),
        name="hidden_grads",
    )(bits, grad, gate, up, down_w)


def input_grad_kernel(bits, gate_give, up_give, gate_keep, up_keep, gate_w, up_w, part, total):
    step = pl.program_id(0)
    first, alike = step < pl.num_programs(0) // 2, bits[1] == 1
    across = (((1,), (1,)), ((), ()))
    gate_g = jnp.where(first, gate_give[...], gate_keep[...])
    up_g = jnp.where(first == alike, up_give[...], up_keep[...])
    term = lax.dot_general(gate_g, gate_w[...], across, preferred_element_type=F32)
    term = term + lax.dot_general(up_g, up_w[...], across, preferred_element_type=F32)

    @pl.when(step == 0)
    def _():
        total[...] = term

    @pl.when(step > 0)
    def _():
        total[...] += term

    @pl.when(step == pl.num_programs(0) - 1)
    def _():
        part[...] = total[...].astype(BF16)


def input_grad(bits, halves, gate_w, up_w):
    rows = halves[0].shape[0]
    width, hidden = gate_w.shape
    half_steps, tile = hidden // 2 // BACK_TILE, BACK_TILE
    spec = hidden_specs(rows, width, half_steps, tile)
    return pl.pallas_call(
        input_grad_kernel,
        grid_spec=pltpu.PrefetchScalarGridSpec(
            num_scalar_prefetch=1,
            grid=(2 * half_steps,),
            in_specs=[spec[name] for name in HALVES] + [spec["tall"]] * 2,
            out_specs=spec["held"],
            scratch_shapes=[VMEM((rows, width), F32)],
        ),
        out_shape=jax.ShapeDtypeStruct((rows, width), BF16),
        compiler_params=pltpu.CompilerParams(vmem_limit_bytes=48 * MIB),
        cost_estimate=takes(1),
        name="input_grad",
    )(bits, *halves, gate_w, up_w)


def ffw_call(kernel, name, ins, weights, outs):
    rows, width = ins[0].shape
    hidden = weights[0].shape[1]
    tile = TILE
    cols = pl.BlockSpec((rows, tile), lambda i: (0, i))
    tall = pl.BlockSpec((width, tile), lambda i: (0, i))
    flat = pl.BlockSpec((tile, width), lambda i: (i, 0))
    held = pl.BlockSpec((rows, width), lambda i: (0, 0))
    return pl.pallas_call(
        kernel,
        grid=(hidden // tile,),
        out_shape=[jax.ShapeDtypeStruct((rows, hidden), t) for t in outs]
        + [jax.ShapeDtypeStruct((rows, width), BF16)],
        in_specs=[held] + [cols] * (len(ins) - 1) + [tall, tall, flat],
        out_specs=[cols] * len(outs) + [held],
        scratch_shapes=[VMEM((rows, width), F32)],
        compiler_params=pltpu.CompilerParams(vmem_limit_bytes=56 * MIB),
        cost_estimate=takes(1),
        name=name,
    )(*ins, *weights)


def body(
    tokens,
    doc_ids,
    attn_in_gain,
    query_weight,
    key_weight,
    value_weight,
    output_weight,
    attn_out_gain,
    ffw_in_gain,
    gate_weight,
    up_weight,
    down_weight,
    ffw_out_gain,
    cotangent,
):
    stretch_rows, seqs, slots, width = tokens.shape
    ctx_count = lax.axis_size("ctx")
    tp_count = lax.axis_size("tp")
    ctx_rank = lax.axis_index("ctx")
    stretch = stretch_rows * tp_count
    length = 2 * stretch * ctx_count
    rows = stretch * slots
    all_rows = seqs * rows
    local_heads = query_weight.shape[1] // HD
    assert key_weight.shape[1] == value_weight.shape[1] == HD
    own = (seqs, slots, stretch_rows, width)
    steps = ctx_count.bit_length() - 1

    slot_stretch = jnp.stack([ctx_rank, 2 * ctx_count - 1 - ctx_rank])
    iota = jnp.arange(stretch, dtype=jnp.int32)
    query_tok = slot_stretch[:, None] * stretch + iota[None, :]
    row_tok = query_tok.reshape(rows)
    row_doc = jnp.concatenate(
        [lax.dynamic_slice_in_dim(doc_ids, slot_stretch[i] * stretch, stretch, 1) for i in (0, 1)],
        1,
    )
    row_start = jnp.sum(
        (doc_ids[:, None, :] < row_doc[:, :, None]).astype(jnp.int32), axis=-1
    )
    row_pos = row_tok[None] - row_start
    frequency = BASE ** (-jnp.arange(HD // 2).astype(F32) / (HD // 2))
    angles = row_pos.astype(F32)[..., None] * frequency
    cosine, sine = jnp.cos(angles), jnp.sin(angles)
    key_slot = jnp.arange(2 * ctx_count, dtype=jnp.int32)
    key_stretch = jnp.where(key_slot % 2 == 0, key_slot // 2, 2 * ctx_count - 1 - key_slot // 2)
    key_tok = (key_stretch[:, None] * stretch + iota[None, :]).reshape(length)
    where = (row_start[..., None], row_tok[:, None], key_tok[None, :])

    def wide(gain):
        return gain.reshape(1, width)

    mine = jnp.transpose(tokens, (1, 2, 0, 3))
    upstream = jnp.transpose(cotangent, (1, 2, 0, 3))
    f32_rows = jax.ShapeDtypeStruct(own, F32)
    gain_shape = jax.ShapeDtypeStruct((1, width), F32)

    (normed_all,) = tp_exchange("enter", 1, enter_rows, [mine, wide(attn_in_gain)], [])
    normed_all = normed_all.reshape(all_rows, width)
    dot = functools.partial(jnp.dot, preferred_element_type=F32)
    ein = functools.partial(jnp.einsum, preferred_element_type=F32)
    queries = dot(normed_all, query_weight).reshape(seqs, rows, local_heads * HD)
    keys = dot(normed_all, key_weight).reshape(seqs, rows, HD)
    values = dot(normed_all, value_weight).reshape(seqs, rows, HD)
    kv_all, attn, attn_low, sums, queries = attend_all(
        queries, keys, values, cosine, sine, *where, 2
    )
    attn_rows = attn_low.reshape(all_rows, local_heads * HD)
    part = dot(attn_rows, output_weight).astype(BF16)

    def by_owner(value):
        return value.reshape(seqs, slots, tp_count, stretch_rows, width)

    ffw_all, branch, resid = tp_exchange(
        "middle",
        3,
        mid_rows,
        [mine, wide(attn_out_gain), wide(ffw_in_gain)],
        [f32_rows, f32_rows],
        by_owner(part),
    )
    ffw_all = ffw_all.reshape(all_rows, width)
    low_bit, next_bit, far_bit = 0, min(1, steps - 1), steps - 1
    high = list(range(2, steps))
    core = lax.axis_index("tp") % 2
    pick = functools.partial(lax.dynamic_index_in_dim, keepdims=False)

    def by_core(value):
        return value.reshape((seqs, slots, tp_count // 2, 2, stretch_rows, value.shape[-1]))

    def core_rows(value):
        return pick(by_core(value), core, 3).reshape(all_rows // 2, value.shape[-1])

    def owner_cols(value):
        bit = (ctx_rank >> far_bit) & 1
        cut = value.shape[1] // 2
        return [lax.dynamic_slice_in_dim(value, at * cut, cut, 1) for at in (bit, 1 - bit)]

    def owner_pieces(total, b):
        bit = (ctx_rank >> b) & 1
        cut = total.reshape(2, -1, total.shape[-1])
        return pick(cut, bit, 0), pick(cut, 1 - bit, 0)

    def whole_cols(own_half, got_half, b):
        bit = (ctx_rank >> b) & 1
        first = jnp.where(bit == 0, own_half, got_half)
        second = jnp.where(bit == 0, got_half, own_half)
        return jnp.concatenate([first, second], 1).astype(F32)

    ffw_send = core_rows(ffw_all)
    ffw_all, ffw_send = lax.optimization_barrier((ffw_all, ffw_send))
    ffw_far, ffw_far_low = Sent(ffw_send, next_bit), Sent(ffw_send, low_bit)
    ffw_weights = (gate_weight, up_weight, down_weight)
    gate, up, mixed, part = ffw_call(ffw_kernel, "ffw", [ffw_all], ffw_weights, [F32, F32, BF16])
    mixed_sent = Sent(by_core(mixed), far_bit)
    part = pin(part, ffw_far, ffw_far_low)
    ffw_near, ffw_near_low = CoreSent(ffw_far.gots[0]), CoreSent(ffw_far_low.gots[0])
    ffw_grad_all, layer_out, ffw_out_gain_part = tp_exchange(
        "turn",
        4,
        turn_rows,
        [resid, upstream, wide(ffw_out_gain)],
        [jax.ShapeDtypeStruct(own, BF16), gain_shape],
        by_owner(part),
    )
    ffw_grad_all = pin(ffw_grad_all.reshape(all_rows, width), ffw_near, ffw_near_low)
    grad_half, grad_give = owner_cols(ffw_grad_all)
    grad_send = core_rows(grad_give)
    ffw_grad_all, grad_send = lax.optimization_barrier((ffw_grad_all, grad_send))
    grad_far = Sent(grad_send, far_bit)
    gate_bit, up_bit = (ctx_rank >> low_bit) & 1, (ctx_rank >> next_bit) & 1
    bits = jnp.stack([gate_bit, (gate_bit == up_bit).astype(jnp.int32)])
    hidden = hidden_grads(bits, ffw_grad_all, gate, up, down_weight)
    gate_give, up_give, gate_half, up_half = [by_core(h) for h in hidden]
    gate_sent, up_sent = Sent(gate_give, low_bit), Sent(up_give, next_bit)
    part = input_grad(bits, hidden, gate_weight, up_weight)
    part = pin(part, gate_sent)
    gate_part = product(
        ffw_all, ffw_far_low.gots[0], ffw_near_low.gots[0], gate_half, gate_sent.gots[0], "gate_product"
    )
    gates = Halving(gate_part, [next_bit] + high)
    gates.send()
    part, gate_part = lax.optimization_barrier((part, gate_part))
    part = pin(part, up_sent)
    up_part = product(
        ffw_all, ffw_far.gots[0], ffw_near.gots[0], up_half, up_sent.gots[0], "up_product"
    )
    ups = Halving(up_part, [low_bit] + high)
    ups.send()
    part, up_part = lax.optimization_barrier((part, up_part))
    part = pin(part, grad_far, mixed_sent)
    grad_near = CoreSent(grad_far.gots[0])
    down_part = product(
        grad_half,
        grad_far.gots[0],
        grad_near.gots[0],
        by_core(mixed),
        mixed_sent.gots[0],
        "down_product",
    )
    down = Halving(down_part, [b for b in range(steps) if b != far_bit], far_bit)
    down.send()
    part, down_part = lax.optimization_barrier((part, down_part))
    branch_grad_all, resid_grad, ffw_in_gain_part, attn_out_gain_part = tp_exchange(
        "middle_back",
        5,
        mid_back_rows,
        [resid, branch, upstream, wide(ffw_in_gain), wide(attn_out_gain)],
        [f32_rows, gain_shape, gain_shape],
        by_owner(part),
    )
    branch_grad_all = branch_grad_all.reshape(all_rows, width)
    output_part = ein("rd,rh->dh", branch_grad_all, attn_rows).astype(BF16)
    attn_grad = ein("rd,hd->rh", branch_grad_all, output_weight).reshape(attn.shape)
    attn_grad = pin(attn_grad, gates)
    gates.step()
    qkv_grad = attend_back(queries, kv_all, attn_grad, attn, sums, cosine, sine, *where, 16)
    qkv_grad = pin(qkv_grad, down, ups, gates).reshape(all_rows, -1)
    ups.step()
    down.step()
    gate_own, gate_give = owner_pieces(gates.finish(), low_bit)
    gate_sent = Sent(gate_give, low_bit)
    qkv_weight = jnp.concatenate([query_weight, key_weight, value_weight], 1)
    part = ein("rh,dh->rd", qkv_grad, qkv_weight).astype(BF16)
    qkv_part = ein("rd,rh->dh", normed_all, qkv_grad).astype(BF16)
    tokens_grad, attn_in_gain_part = tp_exchange(
        "leave",
        7,
        leave_rows,
        [mine, resid_grad, wide(attn_in_gain)],
        [f32_rows, gain_shape],
        by_owner(part),
        gather=False,
    )
    gains = jnp.concatenate(
        [attn_in_gain_part, attn_out_gain_part, ffw_in_gain_part, ffw_out_gain_part], 0
    )
    (output_sum, qkv_sum), gains = weights_scatter([output_part, qkv_part], gains, 8)
    gains = pin(gains, gate_sent, ups, down)
    up_own, up_give = owner_pieces(ups.finish(), next_bit)
    up_sent = Sent(up_give, next_bit)
    down_sum = down.finish().astype(F32)
    gate_sum = whole_cols(gate_own, gate_sent.gots[0], low_bit)
    up_sum = whole_cols(up_own, up_sent.gots[0], next_bit)
    share = width // ctx_count
    gains = lax.dynamic_slice_in_dim(gains, ctx_rank * share, share, 1)
    heads_end = local_heads * HD
    keys_end = heads_end + HD
    return (
        jnp.transpose(layer_out, (2, 0, 1, 3)),
        jnp.transpose(tokens_grad, (2, 0, 1, 3)),
        gains[0],
        qkv_sum[:, :heads_end],
        qkv_sum[:, heads_end:keys_end],
        qkv_sum[:, keys_end:],
        output_sum.T,
        gains[1],
        gains[2],
        gate_sum,
        up_sum,
        down_sum.T,
        gains[3],
    )


def solution(mesh):
    placed = (
        P("tp", None, "ctx", None),
        P(),
        P(),
        P(None, "tp"),
        P(None, "tp"),
        P(None, "tp"),
        P("tp", None),
        P(),
        P(),
        P(None, "tp"),
        P(None, "tp"),
        P("tp", None),
        P(),
        P("tp", None, "ctx", None),
    )
    return jax.shard_map(
        body,
        mesh=mesh,
        in_specs=placed,
        out_specs=(
            P("tp", None, "ctx", None),
            P("tp", None, "ctx", None),
            P("ctx"),
            P("ctx", "tp"),
            P("ctx", "tp"),
            P("ctx", "tp"),
            P("tp", "ctx"),
            P("ctx"),
            P("ctx"),
            P("ctx", "tp"),
            P("ctx", "tp"),
            P("tp", "ctx"),
            P("ctx"),
        ),
        check_vma=False,
    )
```
